32 devices in a mesh: wide: 8 (over z, x), narrow: 4 (over y, core).
Axes of the slice: x: 2, y: 2, z: 4, core: 2. Of those that a mesh axis runs over, the one named last changes fastest.
Arguments:
- tokens: bfloat16 [2, 2, 1152, 8192], P(None, None, 'narrow', 'wide')
- ada_weight: bfloat16 [1152, 6, 1152], P('wide', None, 'narrow'), may hold values from -0.1875 to 0.1875
- ada_bias: bfloat16 [6, 1152], P(None, 'narrow'), may hold values from -3 to 3
- class_table: bfloat16 [101, 1152], replicated, may hold values from -6 to 6
- query_weight: bfloat16 [1152, 1152], P('wide', 'narrow'), may hold values from -0.1875 to 0.1875
- key_weight: bfloat16 [1152, 1152], P('wide', 'narrow'), may hold values from -0.1875 to 0.1875
- value_weight: bfloat16 [1152, 1152], P('wide', 'narrow'), may hold values from -0.1875 to 0.1875
- out_weight: bfloat16 [1152, 1152], P('narrow', 'wide'), may hold values from -0.375 to 0.375
- up_weight: bfloat16 [1152, 4608], P('wide', 'narrow')
- up_bias: bfloat16 [4608], P('narrow'), may hold values from -3 to 3
- down_weight: bfloat16 [4608, 1152], P('narrow', 'wide'), may hold values from -0.09375 to 0.09375
- down_bias: bfloat16 [1152], P('narrow'), may hold values from -3 to 3
- cotangent: bfloat16 [2, 2, 1152, 8192], P(None, None, 'narrow', 'wide'), may hold values from -6 to 6
- clip_frames: int32 [2, 2], replicated, may hold values from 1 to 16, as said below
- time_ids: int32 [2, 2], replicated, may hold values from 0 to 999
- class_ids: int32 [2, 2], replicated, may hold values from 0 to 100
Outputs:
- output: bfloat16 [2, 2, 1152, 8192], P(None, None, 'narrow', 'wide')
- input_grad: float32 [2, 2, 1152, 8192], P(None, None, 'narrow', 'wide')
- ada_weight_grad: float32 [1152, 6, 1152], P('wide', None, 'narrow')
- ada_bias_grad: float32 [6, 1152], P(None, 'narrow')
- class_table_grad: float32 [101, 1152], replicated
- query_weight_grad: float32 [1152, 1152], P('wide', 'narrow')
- key_weight_grad: float32 [1152, 1152], P('wide', 'narrow')
- value_weight_grad: float32 [1152, 1152], P('wide', 'narrow')
- out_weight_grad: float32 [1152, 1152], P('narrow', 'wide')
- up_weight_grad: float32 [1152, 4608], P('wide', 'narrow')
- up_bias_grad: float32 [4608], P('narrow')
- down_weight_grad: float32 [4608, 1152], P('narrow', 'wide')
- down_bias_grad: float32 [1152], P('narrow')
The draws below stay inside these ranges and needn't reach their ends.
Inputs may be any that keep to these rules, and one draw needn't show every extreme that they name: Frames of a sequence at or after its clip_frames are single images. Some sequence of the first micro-batch is a clip of all 16 frames and some sequence of the last micro-batch has clip_frames 1.
All inputs are finite; a program needn't handle non-finite values.
Results may differ from the reference program's by a relative error of at most 0.02.
Values may be sent and summed in bfloat16 or wider, within the bound.
No kernel may reach another device: no remote copies, remote signals or barrier semaphores. Data moves between devices by JAX's collectives and lax.ppermute only.
A program may use at most 256 MiB of HBM per device.

```python
import math
import jax
import jax.numpy as jnp
from jax import lax

D = 1152
HEADS = 16
HEAD_DIM = 72
FF = 4608
CLASSES = 101
FRAMES = 16
TIMESTEPS = 1000
MICRO = 2
SEQS = 2
PATCHES = 512
SEQ_TOKENS = 8192


def draw_tokens(key, part):
    key = jax.random.fold_in(key, 5)
    key_values = jax.random.fold_in(key, 1)
    key_columns = jax.random.fold_in(key, 2)
    array_shape = (MICRO, SEQS, D, SEQ_TOKENS)
    column_place = jnp.arange(D, dtype=jnp.float32) / D
    column_scale = 0.6 * jnp.exp(math.log(3.0) * column_place) * jnp.exp(jax.random.uniform(key_columns, (D,), jnp.float32, -0.35, 0.35))
    values = jax.random.normal(key_values, array_shape, jnp.float32)
    return (values * column_scale[:, None]).astype(jnp.bfloat16)


def draw_up_weight(key, part):
    key = jax.random.fold_in(key, 7)
    key_values = jax.random.fold_in(key, 1)
    key_offsets = jax.random.fold_in(key, 2)
    entry_scale = 1.0 / math.sqrt(D)
    values = jax.random.normal(key_values, (D, FF), jnp.float32) * entry_scale
    offsets = 0.6 * jax.random.normal(key_offsets, (1, FF), jnp.float32) * entry_scale
    return (values + offsets).astype(jnp.bfloat16)


def draw_clip_frames(key, part):
    key = jax.random.fold_in(key, 11)
    key_counts = jax.random.fold_in(key, 21)
    key_full = jax.random.fold_in(key, 22)
    key_image = jax.random.fold_in(key, 23)
    counts = jax.random.randint(key_counts, (MICRO, SEQS), 1, FRAMES + 1, dtype=jnp.int32)
    full_slot = jax.random.randint(key_full, (), 0, SEQS, dtype=jnp.int32)
    image_slot = jax.random.randint(key_image, (), 0, SEQS, dtype=jnp.int32)
    seq_index = jnp.arange(SEQS, dtype=jnp.int32)
    micro_index = jnp.arange(MICRO, dtype=jnp.int32)[:, None]
    counts = jnp.where((micro_index == 0) & (seq_index[None, :] == full_slot), FRAMES, counts)
    counts = jnp.where((micro_index == MICRO - 1) & (seq_index[None, :] == image_slot), 1, counts)
    return counts.astype(jnp.int32)


def plant(values, rng, least, top_value):
    shape = values.shape
    spot = [jax.random.randint(jax.random.fold_in(rng, axis), (), 0, shape[axis]) for axis in range(len(shape))]
    values = values.at[tuple(spot)].set(least)
    longest = shape.index(max(shape))
    spot[longest] = (spot[longest] + 1) % shape[longest]
    return values.at[tuple(spot)].set(top_value)


def level_of(own_key, extent, cuts, least, top_value):
    level, own = 1.0, jax.random.fold_in(own_key, 6)
    for dim, blocks in cuts:
        draws = jnp.exp(jax.random.uniform(jax.random.fold_in(own, dim), (blocks,), jnp.float32, least / len(cuts), top_value / len(cuts)))
        level = level * jnp.repeat(draws, extent[dim] // blocks).reshape([-1 if axis == dim else 1 for axis in range(len(extent))])
    return level


def scatter_about(key, extent, deviation, reach, pieces=(), held_as=jnp.bfloat16):
    drawn = jax.random.normal(key, extent, jnp.float32) * deviation
    if len(pieces) > 0:
        drawn = level_of(key, extent, pieces, -0.22, 0.18) * drawn
    return jnp.clip(drawn, min=-reach, max=reach).astype(held_as)


def setup_inputs(seed: int = 0) -> dict:
    splits = jax.random.split(jax.random.key(seed), 17)
    tokens = draw_tokens(jax.random.fold_in(splits[16], 71), 0)
    ada_weight = scatter_about(splits[1], (D, 6, D), D ** -0.5, 0.1875, ((0, 8), (2, 4)))
    ada_bias = scatter_about(splits[2], (6, D), 0.5, 3.0, ((1, 4),))
    class_table = scatter_about(splits[3], (CLASSES, D), 1.0, 6.0)
    query_weight = scatter_about(splits[4], (D, D), D ** -0.5, 0.1875, ((0, 8), (1, 4)))
    key_weight = scatter_about(splits[5], (D, D), D ** -0.5, 0.1875, ((0, 8), (1, 4)))
    value_weight = scatter_about(splits[6], (D, D), D ** -0.5, 0.1875, ((0, 8), (1, 4)))
    out_weight = scatter_about(splits[7], (D, D), (D // 4) ** -0.5, 0.375, ((0, 4), (1, 8)))
    up_weight = draw_up_weight(jax.random.fold_in(splits[16], 71), 0)
    up_bias = scatter_about(splits[9], (FF,), 0.5, 3.0, ((0, 4),))
    down_weight = scatter_about(splits[10], (FF, D), FF ** -0.5, 0.09375, ((0, 4), (1, 8)))
    down_bias = scatter_about(splits[11], (D,), 0.5, 3.0, ((0, 4),))
    cotangent = scatter_about(splits[12], (MICRO, SEQS, D, SEQ_TOKENS), 1.0, 6.0, ((2, 4), (3, 8)))
    clip_frames = draw_clip_frames(jax.random.fold_in(splits[16], 71), 0)
    time_ids = plant(jax.random.randint(splits[14], (MICRO, SEQS), 0, TIMESTEPS), jax.random.fold_in(splits[14], 1), 0, TIMESTEPS - 1).astype(jnp.int32)
    class_ids = plant(jax.random.randint(splits[15], (MICRO, SEQS), 0, CLASSES), jax.random.fold_in(splits[15], 1), 0, CLASSES - 1).astype(jnp.int32)
    return dict(tokens=tokens, ada_weight=ada_weight, ada_bias=ada_bias, class_table=class_table, query_weight=query_weight, key_weight=key_weight, value_weight=value_weight, out_weight=out_weight, up_weight=up_weight, up_bias=up_bias, down_weight=down_weight, down_bias=down_bias, cotangent=cotangent, clip_frames=clip_frames, time_ids=time_ids, class_ids=class_ids)


@jax.custom_vjp
def low(v):
    return lax.optimization_barrier(v.astype(jnp.bfloat16)).astype(jnp.float32)

@jax.custom_vjp
def low_back(v):
    return v

def low_keep(v):
    return (low(v), None)

def low_pass(kept, grad):
    return (grad,)

def back_keep(v):
    return (v, None)

def back_low(kept, grad):
    return (low(grad),)
low.defvjp(low_keep, low_pass)
low_back.defvjp(back_keep, back_low)

def time_embedding(time_ids, full_width):
    half_width = full_width // 2
    frequency = jnp.exp(-math.log(10000.0) * jnp.arange(half_width, dtype=jnp.float32) / half_width)
    angles = time_ids.astype(jnp.float32)[..., None] * frequency
    return jnp.concatenate([jnp.cos(angles), jnp.sin(angles)], axis=-1)

def norm_rows(values):
    center = lax.optimization_barrier(jnp.mean(values, axis=-1, keepdims=True))
    shifted = values - center
    variance = lax.optimization_barrier(jnp.mean(shifted * shifted, axis=-1, keepdims=True))
    return shifted * lax.rsqrt(variance + 1e-06)

def project(source, weight):
    return jnp.einsum('msfpd,de->msfpe', source, weight, precision=lax.Precision.HIGHEST)

def reference(tokens, ada_weight, ada_bias, class_table, query_weight, key_weight, value_weight, out_weight, up_weight, up_bias, down_weight, down_bias, cotangent, clip_frames, time_ids, class_ids):
    highest = lax.Precision.HIGHEST
    embedded = time_embedding(time_ids, D)
    frame_index = jnp.arange(FRAMES)
    in_clip = frame_index[None, None, :] < clip_frames[:, :, None]
    allowed = in_clip[..., :, None] & in_clip[..., None, :] | (frame_index[:, None] == frame_index[None, :])[None, None]
    allowed = allowed[:, :, None, None]
    score_scale = 1.0 / math.sqrt(HEAD_DIM)
    head_shape = (MICRO, SEQS, FRAMES, PATCHES, HEADS, HEAD_DIM)

    def forward(params):
        tokens_flat, ada32, adab32, table32, query32, key32, value32, out32, up32, upb32, down32, downb32 = params
        tokens32 = tokens_flat.reshape(MICRO, SEQS, D, PATCHES, FRAMES).transpose(0, 1, 4, 3, 2)
        condition = embedded + table32[class_ids]
        cond_act = low(jax.nn.silu(condition))
        modulation = jnp.einsum('msd,dje->msje', cond_act, ada32, precision=highest) + adab32
        shift_one, scale_one, gate_one, shift_two, scale_two, gate_two = [modulation[:, :, slot_index][:, :, None, None, :] for slot_index in range(6)]
        input_one = low(norm_rows(tokens32) * (1.0 + scale_one) + shift_one)
        queries = low(low_back(project(input_one, query32))).reshape(head_shape)
        key_rows = low(low_back(project(input_one, key32))).reshape(head_shape)
        value_rows = low(low_back(project(input_one, value32))).reshape(head_shape)
        scores = jnp.einsum('msfphc,msgphc->msphfg', queries, key_rows, precision=highest) * score_scale
        scores = low_back(jnp.where(allowed, scores, -1000000000.0))
        probs_low = low(jax.nn.softmax(scores, axis=-1))
        attended = jnp.einsum('msphfg,msgphc->msfphc', probs_low, value_rows, precision=highest)
        attended = low(low_back(attended)).reshape(MICRO, SEQS, FRAMES, PATCHES, D)
        branch = low_back(project(attended, out32))
        middle = tokens32 + gate_one * branch
        input_two = low(norm_rows(middle) * (1.0 + scale_two) + shift_two)
        up_act = low_back(project(input_two, up32) + upb32)
        hidden_low = low(jax.nn.gelu(up_act, approximate=True))
        mlp_out = low_back(project(hidden_low, down32) + downb32)
        result = middle + gate_two * mlp_out
        return result.transpose(0, 1, 4, 3, 2).reshape(MICRO, SEQS, D, SEQ_TOKENS)
    primals = tuple((operand.astype(jnp.float32) for operand in (tokens, ada_weight, ada_bias, class_table, query_weight, key_weight, value_weight, out_weight, up_weight, up_bias, down_weight, down_bias)))
    output, pullback = jax.vjp(forward, primals)
    gradients = pullback(cotangent.astype(jnp.float32))[0]
    return (output.astype(jnp.bfloat16), gradients[0], gradients[1], gradients[2], gradients[3], gradients[4], gradients[5], gradients[6], gradients[7], gradients[8], gradients[9], gradients[10], gradients[11])
```

```python
import math

import jax
import jax.numpy as jnp
from jax import lax
from jax.experimental import pallas as pl
from jax.experimental.pallas import tpu as pltpu
from jax.sharding import PartitionSpec as P

HEAD_DIM = 72
FRAMES = 16
BLOCK = 128

norm_epsilon = 1e-06
masked_score = -1e30
both = ("narrow", "wide")


def time_embedding(time_ids, full_width):
    half_width = full_width // 2
    frequency = jnp.exp(-math.log(10000.0) * jnp.arange(half_width, dtype=jnp.float32) / half_width)
    angles = time_ids.astype(jnp.float32)[..., None] * frequency
    return jnp.concatenate([jnp.cos(angles), jnp.sin(angles)], axis=-1)


def head_rows(block, head):
    return block[head * HEAD_DIM : (head + 1) * HEAD_DIM].astype(jnp.bfloat16)


def contract(left, right, left_dim, right_dim):
    return lax.dot_general(
        left, right, (((left_dim,), (right_dim,)), ((), ())), preferred_element_type=jnp.float32
    )


def attention_forward_kernel(heads, score_scale, qkv_ref, row_ref, column_ref, out_ref, probs_ref):
    width = heads * HEAD_DIM
    rows_at = lax.broadcasted_iota(jnp.int32, (BLOCK, BLOCK), 0)
    columns_at = lax.broadcasted_iota(jnp.int32, (BLOCK, BLOCK), 1)
    allowed = (rows_at // FRAMES == columns_at // FRAMES) & (
        ((column_ref[...] > 0) & (row_ref[...] > 0)) | (rows_at == columns_at)
    )
    queries = qkv_ref[0, :width].astype(jnp.float32)
    key_rows = qkv_ref[0, width : 2 * width].astype(jnp.float32)
    value_rows = qkv_ref[0, 2 * width :].astype(jnp.float32)
    parts = []
    for head in range(heads):
        scores = (
            contract(head_rows(key_rows, head), head_rows(queries, head), 0, 0) * score_scale
        )
        scores = jnp.where(allowed, scores, masked_score)
        exp_scores = jnp.exp(scores - jnp.max(scores, axis=0, keepdims=True))
        probs = exp_scores * (1.0 / jnp.sum(exp_scores, axis=0, keepdims=True))
        probs_low = probs.astype(jnp.bfloat16)
        probs_ref[0, 0, head] = probs_low
        parts.append(contract(head_rows(value_rows, head), probs_low, 1, 0))
    out_ref[0] = jnp.concatenate(parts, axis=0).astype(jnp.bfloat16)


def attention_backward_kernel(heads, score_scale, qkv_ref, probs_ref, grad_ref, out_ref):
    width = heads * HEAD_DIM
    queries = qkv_ref[0, :width].astype(jnp.float32)
    key_rows = qkv_ref[0, width : 2 * width].astype(jnp.float32)
    value_rows = qkv_ref[0, 2 * width :].astype(jnp.float32)
    grads = grad_ref[0].astype(jnp.float32)
    query_parts, key_parts, value_parts = [], [], []
    for head in range(heads):
        probs_low = probs_ref[0, 0, head]
        grad_head = head_rows(grads, head)
        value_parts.append(contract(grad_head, probs_low, 1, 1))
        grad_probs = contract(head_rows(value_rows, head), grad_head, 0, 0)
        probs = probs_low.astype(jnp.float32)
        crossed = jnp.sum(grad_probs * probs, axis=0, keepdims=True)
        grad_scores = (probs * (grad_probs - crossed)).astype(jnp.bfloat16)
        query_parts.append(contract(head_rows(key_rows, head), grad_scores, 1, 0) * score_scale)
        key_parts.append(contract(head_rows(queries, head), grad_scores, 1, 1) * score_scale)
    out_ref[0] = jnp.concatenate(query_parts + key_parts + value_parts, axis=0).astype(jnp.bfloat16)


def attention_forward(qkv, in_clip):
    panels, triple, tokens = qkv.shape
    heads = triple // (3 * HEAD_DIM)
    blocks = tokens // BLOCK
    return pl.pallas_call(
        lambda *refs: attention_forward_kernel(heads, 1.0 / math.sqrt(HEAD_DIM), *refs),
        grid=(blocks, panels),
        in_specs=[
            pl.BlockSpec((1, triple, BLOCK), lambda b, n: (n, 0, b)),
            pl.BlockSpec((1, BLOCK), lambda b, n: (0, b)),
            pl.BlockSpec((BLOCK, 1), lambda b, n: (b, 0)),
        ],
        out_specs=[
            pl.BlockSpec((1, triple // 3, BLOCK), lambda b, n: (n, 0, b)),
            pl.BlockSpec((1, 1, heads, BLOCK, BLOCK), lambda b, n: (b, n, 0, 0, 0)),
        ],
        out_shape=[
            jax.ShapeDtypeStruct((panels, triple // 3, tokens), jnp.bfloat16),
            jax.ShapeDtypeStruct((blocks, panels, heads, BLOCK, BLOCK), jnp.bfloat16),
        ],
        name="attention_forward",
    )(qkv, in_clip[None, :], in_clip[:, None])


def attention_backward(qkv, probs, grad_attended):
    panels, triple, tokens = qkv.shape
    heads = triple // (3 * HEAD_DIM)
    blocks = tokens // BLOCK
    return pl.pallas_call(
        lambda *refs: attention_backward_kernel(heads, 1.0 / math.sqrt(HEAD_DIM), *refs),
        grid=(blocks, panels),
        in_specs=[
            pl.BlockSpec((1, triple, BLOCK), lambda b, n: (n, 0, b)),
            pl.BlockSpec((1, 1, heads, BLOCK, BLOCK), lambda b, n: (b, n, 0, 0, 0)),
            pl.BlockSpec((1, triple // 3, BLOCK), lambda b, n: (n, 0, b)),
        ],
        out_specs=pl.BlockSpec((1, triple, BLOCK), lambda b, n: (n, 0, b)),
        out_shape=jax.ShapeDtypeStruct((panels, triple, tokens), jnp.bfloat16),
        name="attention_backward",
    )(qkv, probs, grad_attended)


def gather_weight(piece):
    gathered = lax.all_gather(piece, both, axis=0, tiled=False)
    panels = lax.axis_size("narrow")
    return gathered.reshape(panels, -1, piece.shape[1])


def scatter_weight_grad(grad):
    panels = grad.shape[0]
    wide = lax.axis_size("wide")
    pieces = grad.reshape(panels * wide, grad.shape[1] // wide, grad.shape[2])
    return lax.psum_scatter(pieces, both, scatter_dimension=0, tiled=False).astype(jnp.float32)


def to_tokens(local):
    micro_count, seq_count, local_width, seq_tokens = local.shape
    panels = lax.axis_size("narrow")
    cut = local.reshape(micro_count * seq_count, local_width, panels, seq_tokens // panels)
    moved = lax.all_to_all(cut.transpose(2, 1, 0, 3), "narrow", 0, 0, tiled=True)
    return moved.reshape(panels * local_width, -1)


def to_features(whole, micro_count, seq_count):
    panels = lax.axis_size("narrow")
    width, token_count = whole.shape
    seqs = micro_count * seq_count
    cut = whole.reshape(panels, width // panels, seqs, token_count // seqs)
    moved = lax.all_to_all(cut, "narrow", 0, 0, tiled=True)
    return moved.transpose(2, 1, 0, 3).reshape(micro_count, seq_count, width // panels, -1)


def norm_forward(values):
    width = values.shape[0]
    center = jnp.sum(values, axis=0, keepdims=True) / width
    shifted = values - center
    variance = jnp.sum(shifted * shifted, axis=0, keepdims=True) / width
    inverse = lax.rsqrt(variance + norm_epsilon)
    return shifted * inverse, inverse


def norm_backward(grad_hat, normed, inverse):
    width = normed.shape[0]
    totals = jnp.sum(grad_hat, axis=0, keepdims=True) / width
    crossed = jnp.sum(grad_hat * normed, axis=0, keepdims=True) / width
    return inverse * (grad_hat - totals - normed * crossed)


def on_device(
    tokens,
    ada_weight,
    ada_bias,
    class_table,
    query_weight,
    key_weight,
    value_weight,
    out_weight,
    up_weight,
    up_bias,
    down_weight,
    down_bias,
    cotangent,
    clip_frames,
    time_ids,
    class_ids,
):
    micro_count, seq_count, local_width, seq_tokens = tokens.shape
    class_count, full_width = class_table.shape
    panels, wide_count = lax.axis_size("narrow"), lax.axis_size("wide")
    narrow_at, wide_at = lax.axis_index("narrow"), lax.axis_index("wide")
    seqs = micro_count * seq_count
    part_tokens = seq_tokens // panels
    token_count = seqs * part_tokens
    own_rows = ada_weight.shape[0]
    highest = lax.Precision.HIGHEST

    first_piece = jnp.concatenate([query_weight, key_weight, value_weight, out_weight.T], axis=1)
    first_full = gather_weight(first_piece)
    up_full = gather_weight(up_weight)
    down_full = gather_weight(down_weight.T)
    triple = 3 * local_width
    qkv_full = first_full[:, :, :triple]
    out_full = first_full[:, :, triple:]

    class_hot = (class_ids.reshape(seqs)[:, None] == jnp.arange(class_count)[None, :]).astype(
        jnp.bfloat16
    )
    condition = time_embedding(time_ids.reshape(seqs), full_width) + jnp.einsum(
        "sc,cd->sd", class_hot, class_table, preferred_element_type=jnp.float32
    )
    sigmoid_cond = jax.nn.sigmoid(condition)
    cond_act = (condition * sigmoid_cond).astype(jnp.bfloat16)
    silu_slope = sigmoid_cond * (1.0 + condition * (1.0 - sigmoid_cond))
    own_cond = lax.dynamic_slice_in_dim(cond_act, wide_at * own_rows, own_rows, axis=1)
    own_slope = lax.dynamic_slice_in_dim(silu_slope, wide_at * own_rows, own_rows, axis=1)
    mod_part = jnp.einsum(
        "sd,dje->jes", own_cond, ada_weight, preferred_element_type=jnp.float32
    ) + jnp.where(wide_at == 0, ada_bias.astype(jnp.float32), 0.0)[:, :, None]
    mod_parts = lax.all_gather(mod_part, both, axis=0, tiled=False)
    mod_sum = jnp.sum(
        mod_parts.reshape(panels, wide_count, 6, local_width, seqs), axis=1
    )
    modulation = mod_sum.transpose(1, 0, 2, 3).reshape(6, full_width, seqs)

    def spread(vector):
        return jnp.broadcast_to(
            vector[:, :, None], (vector.shape[0], seqs, part_tokens)
        ).reshape(vector.shape[0], token_count)

    def gather_sum(values):
        return jnp.sum(values.reshape(values.shape[0], seqs, part_tokens), axis=2)

    shift_one, scale_one, gate_one, shift_two, scale_two, gate_two = [
        spread(modulation[slot_index]) for slot_index in range(6)
    ]
    frame_at = jnp.arange(part_tokens) % FRAMES
    in_clip = (frame_at[None, :] < clip_frames.reshape(seqs)[:, None]).astype(jnp.int32).reshape(-1)

    residual = to_tokens(tokens).astype(jnp.float32)
    upstream = to_tokens(cotangent).astype(jnp.float32)
    normed_one, inverse_one = norm_forward(residual)
    input_one = (normed_one * (1.0 + scale_one) + shift_one).astype(jnp.bfloat16)
    qkv = jnp.einsum(
        "nde,dt->net", qkv_full, input_one, preferred_element_type=jnp.float32
    ).astype(jnp.bfloat16)
    attended, probs = attention_forward(qkv, in_clip)
    branch = jnp.einsum("nde,net->dt", out_full, attended, preferred_element_type=jnp.float32)
    middle = residual + gate_one * branch
    normed_two, inverse_two = norm_forward(middle)
    input_two = (normed_two * (1.0 + scale_two) + shift_two).astype(jnp.bfloat16)
    up_bias_full = lax.all_gather(up_bias, "narrow", axis=0).astype(jnp.float32)
    down_bias_full = lax.all_gather(down_bias, "narrow", axis=0, tiled=True).astype(jnp.float32)
    up_act = (
        jnp.einsum("nde,dt->net", up_full, input_two, preferred_element_type=jnp.float32)
        + up_bias_full[:, :, None]
    )
    hidden, gelu_back = jax.vjp(lambda v: jax.nn.gelu(v, approximate=True), up_act)
    hidden_low = hidden.astype(jnp.bfloat16)
    slope_low = gelu_back(jnp.ones_like(up_act))[0].astype(jnp.bfloat16)
    mlp_out = (
        jnp.einsum("nde,net->dt", down_full, hidden_low, preferred_element_type=jnp.float32)
        + down_bias_full[:, None]
    )
    output = (middle + gate_two * mlp_out).astype(jnp.bfloat16)
    output_local = to_features(output, micro_count, seq_count)

    grad_gate_two = gather_sum(upstream * mlp_out)
    grad_mlp = (gate_two * upstream).astype(jnp.bfloat16)
    down_bias_part = jnp.sum(grad_mlp.astype(jnp.float32), axis=1)
    down_grad = jnp.einsum(
        "dt,net->nde", grad_mlp, hidden_low, preferred_element_type=jnp.float32
    ).astype(jnp.bfloat16)
    down_grad = scatter_weight_grad(down_grad)
    grad_hidden = jnp.einsum("nde,dt->net", down_full, grad_mlp, preferred_element_type=jnp.float32)
    grad_up = (grad_hidden * slope_low.astype(jnp.float32)).astype(jnp.bfloat16)
    up_bias_part = jnp.sum(grad_up.astype(jnp.float32), axis=2)
    up_grad = jnp.einsum(
        "dt,net->nde", input_two, grad_up, preferred_element_type=jnp.float32
    ).astype(jnp.bfloat16)
    up_grad = scatter_weight_grad(up_grad)
    grad_input_two = jnp.einsum("nde,net->dt", up_full, grad_up, preferred_element_type=jnp.float32)
    grad_shift_two = gather_sum(grad_input_two)
    grad_scale_two = gather_sum(grad_input_two * normed_two)
    grad_middle = upstream + norm_backward(
        grad_input_two * (1.0 + scale_two), normed_two, inverse_two
    )
    grad_gate_one = gather_sum(grad_middle * branch)
    grad_branch = (gate_one * grad_middle).astype(jnp.bfloat16)
    out_grad = jnp.einsum(
        "dt,net->nde", grad_branch, attended, preferred_element_type=jnp.float32
    ).astype(jnp.bfloat16)
    grad_attended = jnp.einsum(
        "nde,dt->net", out_full, grad_branch, preferred_element_type=jnp.float32
    ).astype(jnp.bfloat16)
    grad_qkv = attention_backward(qkv, probs, grad_attended)
    qkv_grad = jnp.einsum(
        "dt,net->nde", input_one, grad_qkv, preferred_element_type=jnp.float32
    ).astype(jnp.bfloat16)
    first_grad = scatter_weight_grad(jnp.concatenate([qkv_grad, out_grad], axis=2))
    grad_input_one = jnp.einsum(
        "nde,net->dt", qkv_full, grad_qkv, preferred_element_type=jnp.float32
    )
    grad_shift_one = gather_sum(grad_input_one)
    grad_scale_one = gather_sum(grad_input_one * normed_one)
    grad_tokens = grad_middle + norm_backward(
        grad_input_one * (1.0 + scale_one), normed_one, inverse_one
    )
    grad_local = to_features(grad_tokens.astype(jnp.bfloat16), micro_count, seq_count)

    mod_part = jnp.stack(
        [
            grad_shift_one,
            grad_scale_one,
            grad_gate_one,
            grad_shift_two,
            grad_scale_two,
            grad_gate_two,
        ]
    )
    mod_grad, up_bias_sum, down_bias_sum = lax.psum((mod_part, up_bias_part, down_bias_part), both)
    own_mod = lax.dynamic_slice_in_dim(mod_grad, narrow_at * local_width, local_width, axis=1)
    up_bias_grad = lax.dynamic_index_in_dim(up_bias_sum, narrow_at, 0, keepdims=False)
    down_bias_grad = lax.dynamic_slice_in_dim(down_bias_sum, narrow_at * local_width, local_width)
    ada_grad = jnp.einsum(
        "sd,jes->dje", own_cond.astype(jnp.float32), own_mod, precision=highest
    )
    ada_bias_grad = jnp.sum(own_mod, axis=2)
    cond_local = own_slope * jnp.einsum(
        "jes,dje->sd", own_mod, ada_weight.astype(jnp.float32), precision=highest
    )
    cond_grad = lax.psum(
        lax.dynamic_update_slice_in_dim(
            jnp.zeros((seqs, full_width), jnp.float32), cond_local, wide_at * own_rows, axis=1
        ),
        both,
    )
    table_grad = jnp.einsum(
        "sc,sd->cd", class_hot.astype(jnp.float32), cond_grad, precision=highest
    )
    return (
        output_local,
        grad_local.astype(jnp.float32),
        ada_grad,
        ada_bias_grad,
        table_grad,
        first_grad[:, :local_width],
        first_grad[:, local_width : 2 * local_width],
        first_grad[:, 2 * local_width : triple],
        first_grad[:, triple:].T,
        up_grad,
        up_bias_grad,
        down_grad.T,
        down_bias_grad,
    )


def solution(mesh):
    return jax.shard_map(
        on_device,
        mesh=mesh,
        in_specs=(
            P(None, None, "narrow", "wide"),
            P("wide", None, "narrow"),
            P(None, "narrow"),
            P(),
            P("wide", "narrow"),
            P("wide", "narrow"),
            P("wide", "narrow"),
            P("narrow", "wide"),
            P("wide", "narrow"),
            P("narrow"),
            P("narrow", "wide"),
            P("narrow"),
            P(None, None, "narrow", "wide"),
            P(),
            P(),
            P(),
        ),
        out_specs=(
            P(None, None, "narrow", "wide"),
            P(None, None, "narrow", "wide"),
            P("wide", None, "narrow"),
            P(None, "narrow"),
            P(),
            P("wide", "narrow"),
            P("wide", "narrow"),
            P("wide", "narrow"),
            P("narrow", "wide"),
            P("wide", "narrow"),
            P("narrow"),
            P("narrow", "wide"),
            P("narrow"),
        ),
        check_vma=False,
    )
```

```python
import functools
import math

import jax
import jax.numpy as jnp
from jax import lax
from jax.experimental import pallas as pl
from jax.experimental.pallas import tpu as pltpu
from jax.sharding import PartitionSpec as P

HEAD_DIM = 72
FRAMES = 16
BLOCK = 128
MIB = 1024 * 1024
COSTS = {
    "project_qkv": 15,
    "attention_forward": 24,
    "project_out": 17,
    "project_up": 28,
    "project_down": 25,
    "down_weight_grad": 10,
    "up_weight_grad": 10,
    "first_weight_grad": 12,
    "hidden_backward": 21,
    "middle_backward": 30,
    "attended_backward": 9,
    "attention_backward": 33,
    "input_backward": 25,
}
COST_SCALE = 1.15e9

norm_epsilon = 1e-06
masked_score = -1e30
both = ("wide", "narrow")
low = jnp.bfloat16
high = jnp.float32


def time_embedding(time_ids, full_width):
    half_width = full_width // 2
    frequency = jnp.exp(-math.log(10000.0) * jnp.arange(half_width, dtype=jnp.float32) / half_width)
    angles = time_ids.astype(jnp.float32)[..., None] * frequency
    return jnp.concatenate([jnp.cos(angles), jnp.sin(angles)], axis=-1)


def place():
    deep, tall = lax.axis_size("wide") // 2, lax.axis_size("narrow") // 2
    wide_at, narrow_at = lax.axis_index("wide"), lax.axis_index("narrow")
    return deep, tall, wide_at // 2, wide_at % 2, narrow_at // 2, narrow_at % 2


def send(value, deep_by=0, side_by=0, tall_by=0, core_by=0):
    deep, tall = lax.axis_size("wide") // 2, lax.axis_size("narrow") // 2
    pairs = []
    for z in range(deep):
        for x in range(2):
            for y in range(tall):
                for c in range(2):
                    source = ((z * 2 + x) * tall + y) * 2 + c
                    target = (
                        ((z + deep_by) % deep * 2 + (x + side_by) % 2) * tall + (y + tall_by) % tall
                    ) * 2 + (c + core_by) % 2
                    pairs.append((source, target))
    return lax.ppermute(value, both, pairs)


def after(value, *earlier):
    return lax.optimization_barrier((value, earlier))[0]


class Gather:
    def __init__(self, piece):
        self.deep = lax.axis_size("wide") // 2
        self.tall = lax.axis_size("narrow") // 2
        self.ring = [piece]
        self.rows = piece.shape[0]
        self.got = {}

    def step(self, *earlier):
        self.ring.append(send(after(self.ring[-1], *earlier), deep_by=1))
        return self.ring[-1]

    def front_side(self, *earlier):
        self.front = jnp.concatenate(self.ring[: self.deep // 2], axis=0)
        got = send(after(self.front, *earlier), side_by=1)
        self.front = jnp.concatenate([self.front, got], axis=0)
        return self.front

    def rear_tall(self, *earlier):
        half = self.deep // 2
        rear = jnp.concatenate(self.ring[half:], axis=0)
        gots = [send(after(rear, *earlier), tall_by=k) for k in range(1, self.tall)]
        self.rear = jnp.concatenate([rear] + gots, axis=0)
        return self.rear

    def front_tall(self, *earlier):
        self.fronts = [self.front] + [
            send(after(self.front, *earlier), tall_by=k) for k in range(1, self.tall)
        ]
        return self.fronts[-1]

    def rear_side(self, *earlier):
        self.beside = send(after(self.rear, *earlier), side_by=1)
        return self.beside

    def early_cores(self, *earlier):
        self.got = {
            0: send(after(self.front, *earlier), core_by=1),
            self.tall: send(after(self.rear, *earlier), core_by=1),
        }
        return list(self.got.values())

    def cores(self, *earlier):
        arrays = self.fronts + [self.rear, self.beside]
        count = len(arrays)
        arrays = arrays + [
            self.got[at] if at in self.got else send(after(part, *earlier), core_by=1)
            for at, part in enumerate(arrays)
        ]
        near = self.deep // 2 * self.rows
        far = self.deep * self.rows - near
        panels = []
        for c in range(2):
            for y in range(self.tall):
                panels.append(
                    [
                        (c * count + y, (), 0, 0, near),
                        (c * count + self.tall, (), y * far, near, far),
                        (c * count + y, (), near, near + far, near),
                        (c * count + self.tall + 1, (), y * far, 2 * near + far, far),
                    ]
                )
        return arrays, panels


class LateGather:
    def __init__(self, piece):
        self.deep = lax.axis_size("wide") // 2
        self.tall = lax.axis_size("narrow") // 2
        self.piece = piece
        self.got = []

    def side(self, *earlier):
        self.line = jnp.stack([self.piece, send(after(self.piece, *earlier), side_by=1)])
        return self.line

    def along_tall(self, *earlier):
        gots = [send(after(self.line, *earlier), tall_by=k) for k in range(1, self.tall)]
        self.ring = [jnp.stack([self.line] + gots)]
        return self.ring[0]

    def step(self, *earlier):
        self.ring.append(send(after(self.ring[-1], *earlier), deep_by=1))
        return self.ring[-1]

    def core(self, *earlier):
        self.got.append(send(after(self.ring[len(self.got)], *earlier), core_by=1))
        return self.got[-1]

    def cores(self):
        tall, deep, rows = self.tall, self.deep, self.piece.shape[0]
        arrays = self.ring + self.got
        if rows % 16:
            whole = [
                jnp.concatenate([arrays[c * deep + k][y, x] for x in range(2) for k in range(deep)])
                for c in range(2)
                for y in range(tall)
            ]
            return whole, [[(at, (), 0, 0, 2 * deep * rows)] for at in range(2 * tall)]
        panels = [
            [
                (c * deep + k, (y, x), 0, (x * deep + k) * rows, rows)
                for x in range(2)
                for k in range(deep)
            ]
            for c in range(2)
            for y in range(tall)
        ]
        return arrays, panels


def added(arrays, *index):
    return sum(array[index].astype(high) for array in arrays)


class GradSum:
    def __init__(self, other):
        self.deep = lax.axis_size("wide") // 2
        self.tall = lax.axis_size("narrow") // 2
        self.shape = (self.tall, self.deep, other[0].shape[1] // self.deep, other[0].shape[2])
        self.got = [send(other[1], core_by=-1), send(other[0], core_by=-1)][::-1]

    def hold(self, *earlier):
        self.parts = [[after(v, *earlier) for v in arrays] for arrays in self.parts]

    def near(self, near):
        self.parts = [[v.reshape(self.shape), g.reshape(self.shape)] for v, g in zip(near, self.got)]

    def split(self, at):
        cuts = [GradSum.__new__(GradSum), GradSum.__new__(GradSum)]
        for one, cut in zip(cuts, (slice(0, at), slice(at, self.deep))):
            one.deep, one.tall, one.shape = self.deep, self.tall, self.shape
            one.parts = [[v[:, cut] for v in arrays] for arrays in self.parts]
        return cuts

    def sums_side(self):
        return [added(self.parts[1], slice(None)).astype(low)]

    def side(self, sums, *earlier):
        got = send(after(sums[0], *earlier), side_by=-1)
        self.parts = [self.parts[0] + [got]]
        return [got]

    def sums_tall(self):
        return [
            jnp.stack([added(arrays, slice(k, k + 1)).astype(low) for arrays in self.parts])
            for k in range(1, self.tall)
        ]

    def along_tall(self, sums, *earlier):
        gots = [send(after(v, *earlier), tall_by=-k) for k, v in enumerate(sums, 1)]
        self.parts = [
            [v[:1] for v in arrays] + [got[x] for got in gots] for x, arrays in enumerate(self.parts)
        ]
        return gots

    def sums_each_deep(self):
        return [added(self.parts[0], slice(None), k).astype(low) for k in range(1, self.deep)]

    def along_each_deep(self, sums, *earlier):
        gots = [send(after(v, *earlier), deep_by=-k) for k, v in enumerate(sums, 1)]
        self.parts = [[v[:, :1] for v in self.parts[0]] + [got[:, None] for got in gots]]
        return gots

    def sums_deep(self):
        z = lax.axis_index("wide") // 2
        blocks = []
        for target in range(self.deep):
            at = (z - target) % self.deep
            blocks.append(
                sum(
                    lax.dynamic_index_in_dim(v, at, 1, keepdims=False).astype(high)
                    for v in self.parts[0]
                ).astype(low)
            )
        return [jnp.stack(blocks)]

    def along_deep(self, sums, *earlier):
        groups = [[z * 2 + x for z in range(self.deep)] for x in range(2)]
        got = lax.all_to_all(
            after(sums[0], *earlier), "wide", 0, 0, axis_index_groups=groups, tiled=True
        )
        self.parts = [[got[k][:, None] for k in range(self.deep)]]
        return [got]

    def sums_late_tall(self):
        return [added(self.parts[0], k).astype(low) for k in range(1, self.tall)]

    def late_tall(self, sums, *earlier):
        gots = [send(after(v, *earlier), tall_by=-k) for k, v in enumerate(sums, 1)]
        self.parts = [[v[:1] for v in self.parts[0]] + [got[None] for got in gots]]
        return gots

    def result(self):
        return added(self.parts[0], 0, 0)


def swap_narrow(parts):
    return lax.all_to_all(parts, "narrow", 0, 0, tiled=True)


def orders():
    deep, tall, z, x, y, c = place()
    wide_count, narrow_count = 2 * deep, 2 * tall
    ratio = wide_count // narrow_count

    def stands(n, h):
        w = n * ratio + h
        return (x - w % 2) % 2 * deep + (z - w // 2) % deep

    there = [stands(n, h) for n in range(narrow_count) for h in range(ratio)]
    came, goes = [], []
    for core_by in range(2):
        for tall_by in range(tall):
            source = (y - tall_by) % tall * 2 + (c - core_by) % 2
            target = (y + tall_by) % tall * 2 + (c + core_by) % 2
            came += [stands(source, h) for h in range(ratio)]
            goes += [stands(target, h) for h in range(ratio)]
    return [jnp.stack(v).astype(jnp.int32) for v in (there, came, goes)]


def sum_wide(value):
    deep = lax.axis_size("wide") // 2
    value = value + send(value, side_by=1)
    step = 1
    while step < deep:
        value = value + send(value, deep_by=step)
        step *= 2
    return value


def sum_narrow(value):
    tall = lax.axis_size("narrow") // 2
    value = value + send(value, core_by=1)
    step = 1
    while step < tall:
        value = value + send(value, tall_by=step)
        step *= 2
    return value


def gather_narrow(value):
    tall = lax.axis_size("narrow") // 2
    own = jnp.stack([value] + [send(value, tall_by=k) for k in range(1, tall)])
    return jnp.concatenate([own, send(own, core_by=1)])


def scatter_narrow(value):
    tall = lax.axis_size("narrow") // 2
    value = value.reshape(2, tall, *value.shape[1:])
    total = value[0] + send(value[1], core_by=1)
    return sum([total[0]] + [send(total[k], tall_by=k) for k in range(1, tall)])


def contract(left, right, left_dim, right_dim):
    return lax.dot_general(
        left, right, (((left_dim,), (right_dim,)), ((), ())), preferred_element_type=jnp.float32
    )


def call(kernel, name, grid, ins, outs, scratch=(), prefetch=(), vmem=60):
    in_specs = []
    for array, block, index in ins:
        if block == "any":
            in_specs.append(pl.BlockSpec(memory_space=pl.ANY))
        elif block is None:
            in_specs.append(pl.BlockSpec(array.shape, lambda *_, r=array.ndim: (0,) * r))
        else:
            in_specs.append(pl.BlockSpec(block, index))
    out_specs = []
    for shape, _, block, index in outs:
        if block is None:
            out_specs.append(pl.BlockSpec(shape, lambda *_, r=len(shape): (0,) * r))
        else:
            out_specs.append(pl.BlockSpec(block, index))
    return pl.pallas_call(
        kernel,
        grid_spec=pltpu.PrefetchScalarGridSpec(
            num_scalar_prefetch=len(prefetch),
            grid=grid,
            in_specs=in_specs,
            out_specs=out_specs,
            scratch_shapes=list(scratch),
        ),
        out_shape=[jax.ShapeDtypeStruct(shape, kind) for shape, kind, _, _ in outs],
        compiler_params=pltpu.CompilerParams(vmem_limit_bytes=vmem * MIB),
        cost_estimate=pl.CostEstimate(
            flops=int(COSTS.get(name, 4) * COST_SCALE), bytes_accessed=0, transcendentals=0
        ),
        name=name,
    )(*prefetch, *[array for array, _, _ in ins])


class Weights:
    def __init__(self, gathered, start=0, stop=None):
        self.arrays, self.panels = gathered
        self.columns = self.arrays[0].shape[-1]
        self.start, self.stop = start, self.columns if stop is None else stop
        self.rows = sum(size for *_, size in self.panels[0])

    def ins(self):
        return [(array, "any", None) for array in self.arrays]

    def scratch(self):
        count = len(self.panels)
        return [
            pltpu.VMEM((count, self.rows, self.stop - self.start), low),
            pltpu.SemaphoreType.DMA((count, len(self.panels[0]))),
        ]

    def panel(self, refs, held, sems, at):
        def copy(panel, piece):
            array, lead, begin, row, size = self.panels[panel][piece]
            source = refs[array].at[(*lead, pl.ds(begin, size), slice(self.start, self.stop))]
            return pltpu.make_async_copy(
                source, held.at[panel, pl.ds(row, size)], sems.at[panel, piece]
            )

        @pl.when(at == 0)
        def _():
            for panel in range(len(self.panels)):
                for piece in range(len(self.panels[0])):
                    copy(panel, piece).start()

        for panel in range(len(self.panels)):

            @pl.when(at == panel)
            def _(panel=panel):
                for piece in range(len(self.panels[0])):
                    copy(panel, piece).wait()

        return held.at[at]


class Shape:
    def __init__(self, seqs, part, width, panels):
        self.seqs, self.part, self.width, self.panels = seqs, part, width, panels
        self.tokens = seqs * part
        self.block = part if part % BLOCK == 0 else self.tokens
        self.blocks = self.tokens // self.block
        self.share = self.block // part
        local = width // panels
        self.local = local
        self.qkv_rows = min(-(-3 * local // BLOCK) * BLOCK, 4 * local)
        self.out_from = 3 * local // BLOCK * BLOCK
        self.out_rows = 4 * local - self.out_from
        self.out_skip = 3 * local - self.out_from


def pick(table, at):
    lane = lax.broadcasted_iota(jnp.int32, table.shape, 1)
    return jnp.sum(jnp.where(lane == at, table, 0.0), axis=1, keepdims=True)


def spread(shape, table, slot, block):
    picked = [pick(table, slot * shape.seqs + block * shape.share + j) for j in range(shape.share)]
    if shape.share == 1:
        return picked[0]
    return jnp.concatenate(
        [jnp.broadcast_to(one, (one.shape[0], shape.part)) for one in picked], axis=1
    )


def seq_sums(shape, values):
    return [
        jnp.sum(values[:, j * shape.part : (j + 1) * shape.part], axis=1, keepdims=True)
        for j in range(shape.share)
    ]


def normed_rows(values):
    width = values.shape[0]
    center = jnp.sum(values, axis=0, keepdims=True) * (1.0 / width)
    shifted = values - center
    variance = jnp.sum(shifted * shifted, axis=0, keepdims=True) * (1.0 / width)
    inverse = lax.rsqrt(variance + norm_epsilon)
    return shifted * inverse, inverse


def norm_backward(grad_hat, normed, inverse):
    width = normed.shape[0]
    totals = jnp.sum(grad_hat, axis=0, keepdims=True) * (1.0 / width)
    crossed = jnp.sum(grad_hat * normed, axis=0, keepdims=True) * (1.0 / width)
    return inverse * (grad_hat - totals - normed * crossed)


def put_pieces(shape, at_ref, pieces_ref, held):
    rows = held.shape[1]
    ratio = shape.local // rows
    for n in range(shape.panels):
        for h in range(ratio):
            for j in range(shape.share):
                held[at_ref[n * ratio + h], :, j * shape.part : (j + 1) * shape.part] = pieces_ref[
                    n, j, h * rows : (h + 1) * rows
                ].astype(high)


def take_pieces(shape, at_ref, held, pieces_ref, block):
    rows = held.shape[1]
    ratio = shape.local // rows
    for n in range(shape.panels):
        for h in range(ratio):
            for j in range(shape.share):
                pieces_ref[n, block * shape.share + j, h * rows : (h + 1) * rows, :] = held[
                    at_ref[n * ratio + h], :, j * shape.part : (j + 1) * shape.part
                ].astype(pieces_ref.dtype)


def pieces_in(shape, pieces):
    return (
        pieces,
        (shape.panels, shape.share, shape.local, shape.part),
        lambda b, *_: (0, b, 0, 0),
    )


def pieces_out(shape):
    return ((shape.panels, shape.seqs, shape.local, shape.part), low, None, None)


def token_out(shape, kind):
    return (
        (shape.width, shape.tokens),
        kind,
        (shape.width, shape.block),
        lambda b, *_: (0, b),
    )


def prepare_tokens(shape, there, pieces, table, wide_count):
    def kernel(at_ref, pieces_ref, table_ref, whole_ref, input_ref, held):
        block = pl.program_id(0)
        put_pieces(shape, at_ref, pieces_ref, held)
        values = held[...].reshape(shape.width, shape.block)
        normed, _ = normed_rows(values)
        table = table_ref[...]
        whole_ref[...] = values.astype(low)
        input_ref[...] = (
            normed * (1.0 + spread(shape, table, 1, block)) + spread(shape, table, 0, block)
        ).astype(low)

    return call(
        kernel,
        "prepare_tokens",
        (shape.blocks,),
        [pieces_in(shape, pieces), (table, None, None)],
        [token_out(shape, low), token_out(shape, low)],
        [pltpu.VMEM((wide_count, shape.width // wide_count, shape.block), high)],
        [there],
    )


def prepare_upstream(shape, there, pieces, table, wide_count):
    def kernel(at_ref, pieces_ref, table_ref, whole_ref, grad_ref, bias_ref, held):
        block = pl.program_id(0)
        put_pieces(shape, at_ref, pieces_ref, held)
        values = held[...].reshape(shape.width, shape.block)
        whole_ref[...] = values.astype(low)
        grad_low = (values * spread(shape, table_ref[...], 5, block)).astype(low)
        grad_ref[...] = grad_low
        total = jnp.sum(grad_low.astype(high), axis=1, keepdims=True)

        @pl.when(block == 0)
        def _():
            bias_ref[...] = total

        @pl.when(block > 0)
        def _():
            bias_ref[...] += total

    return call(
        kernel,
        "prepare_upstream",
        (shape.blocks,),
        [pieces_in(shape, pieces), (table, None, None)],
        [token_out(shape, low), token_out(shape, low), ((shape.width, 1), high, None, None)],
        [pltpu.VMEM((wide_count, shape.width // wide_count, shape.block), high)],
        [there],
    )


def lay_small(shape, came, small, wide_count):
    rows = shape.width // wide_count
    ratio = shape.local // rows
    first = 6 * shape.seqs + 1
    count = small.shape[1]
    ups = count - first

    def kernel(at_ref, small_ref, table_ref, bias_ref, held):
        for p in range(shape.panels):
            turned = small_ref[p].T
            for h in range(ratio):
                held[at_ref[p * ratio + h]] = turned[h * rows : (h + 1) * rows]
            bias_ref[p] = jnp.concatenate(
                [turned[:, first + k : first + k + 1] for k in range(ups)], axis=0
            )
        table_ref[...] = held[...].reshape(shape.width, count)

    return call(
        kernel,
        "lay_small",
        (1,),
        [(small, None, None)],
        [
            ((shape.width, count), high, None, None),
            ((shape.panels, ups * shape.local, 1), high, None, None),
        ],
        [pltpu.VMEM((wide_count, rows, count), high)],
        [came],
    )


def lay_small_grads(shape, goes, late, middle, gate_two, down_bias, up_bias, wide_count):
    rows = shape.width // wide_count
    ratio = shape.local // rows
    seqs = shape.seqs
    ups = up_bias.shape[1] // shape.local
    count = 6 * seqs + 1 + ups

    def kernel(at_ref, late_ref, middle_ref, gate_ref, down_ref, up_ref, small_ref, held):
        table = jnp.concatenate(
            [
                late_ref[...],
                middle_ref[...],
                gate_ref[...],
                down_ref[...],
            ],
            axis=1,
        )
        held[...] = table.reshape(wide_count, rows, 6 * seqs + 1)
        for p in range(shape.panels):
            parts = [held[at_ref[p * ratio + h]] for h in range(ratio)]
            column = jnp.concatenate(parts, axis=0) if ratio > 1 else parts[0]
            bias = up_ref[p]
            column = jnp.concatenate(
                [column] + [bias[k * shape.local : (k + 1) * shape.local] for k in range(ups)],
                axis=1,
            )
            small_ref[p] = column.T

    return call(
        kernel,
        "lay_small_grads",
        (1,),
        [(v, None, None) for v in (late, middle, gate_two, down_bias, up_bias)],
        [((shape.panels, count, shape.local), high, None, None)],
        [pltpu.VMEM((wide_count, rows, 6 * seqs + 1), high)],
        [goes],
    )[0]


def cut_tokens(shape, local):
    def kernel(local_ref, out_ref):
        for n in range(shape.panels):
            out_ref[n, 0] = local_ref[0, :, n * shape.part : (n + 1) * shape.part]

    return call(
        kernel,
        "cut_tokens",
        (shape.seqs,),
        [(local, (1, *local.shape[1:]), lambda s, *_: (s, 0, 0))],
        [
            (
                (shape.panels, shape.seqs, shape.local, shape.part),
                low,
                (shape.panels, 1, shape.local, shape.part),
                lambda s, *_: (0, s, 0, 0),
            )
        ],
    )[0]


def join_tokens(shape, pieces, kind):
    def kernel(pieces_ref, out_ref):
        for n in range(shape.panels):
            out_ref[0, :, n * shape.part : (n + 1) * shape.part] = pieces_ref[n, 0].astype(kind)

    return call(
        kernel,
        "join_tokens",
        (shape.seqs,),
        [
            (
                pieces,
                (shape.panels, 1, shape.local, shape.part),
                lambda s, *_: (0, s, 0, 0),
            )
        ],
        [
            (
                (shape.seqs, shape.local, shape.panels * shape.part),
                kind,
                (1, shape.local, shape.panels * shape.part),
                lambda s, *_: (s, 0, 0),
            )
        ],
    )[0]


def by_panel(shape, rows, kind):
    return (
        (shape.panels, rows, shape.tokens),
        kind,
        (1, rows, shape.tokens),
        lambda n, *_: (n, 0, 0),
    )


def panel_in(array):
    return (array, (1, *array.shape[1:]), lambda n, *_: (n, 0, 0))


def project_qkv(shape, weights, source):
    count = len(weights.arrays)

    def kernel(*refs):
        weight_refs, (source_ref, out_ref, held, sems) = refs[:count], refs[count:]
        panel = weights.panel(weight_refs, held, sems, pl.program_id(0))
        out_ref[0] = contract(panel[...], source_ref[...], 0, 0).astype(low)

    return call(
        kernel,
        "project_qkv",
        (shape.panels,),
        weights.ins() + [(source, None, None)],
        [by_panel(shape, shape.qkv_rows, low)],
        weights.scratch(),
    )[0]


def head_rows(block, head):
    return block[head * HEAD_DIM : (head + 1) * HEAD_DIM].astype(low)


def attention_forward(shape, qkv, in_clip):
    width = shape.local
    heads = width // HEAD_DIM
    blocks = shape.tokens // BLOCK
    score_scale = 1.0 / math.sqrt(HEAD_DIM)

    def kernel(qkv_ref, row_ref, column_ref, out_ref, probs_ref):
        rows_at = lax.broadcasted_iota(jnp.int32, (BLOCK, BLOCK), 0)
        columns_at = lax.broadcasted_iota(jnp.int32, (BLOCK, BLOCK), 1)
        allowed = (rows_at // FRAMES == columns_at // FRAMES) & (
            ((column_ref[...] > 0) & (row_ref[...] > 0)) | (rows_at == columns_at)
        )
        queries = qkv_ref[0, :width].astype(high)
        key_rows = qkv_ref[0, width : 2 * width].astype(high)
        value_rows = qkv_ref[0, 2 * width : 3 * width].astype(high)
        parts = [jnp.zeros((shape.out_skip, BLOCK), high)]
        for head in range(heads):
            scores = (
                contract(head_rows(key_rows, head), head_rows(queries, head), 0, 0) * score_scale
            )
            scores = jnp.where(allowed, scores, masked_score)
            exp_scores = jnp.exp(scores - jnp.max(scores, axis=0, keepdims=True))
            probs = exp_scores * (1.0 / jnp.sum(exp_scores, axis=0, keepdims=True))
            probs_low = probs.astype(low)
            probs_ref[0, 0, head] = probs_low
            parts.append(contract(head_rows(value_rows, head), probs_low, 1, 0))
        out_ref[0] = jnp.concatenate(parts, axis=0).astype(low)

    return call(
        kernel,
        "attention_forward",
        (blocks, shape.panels),
        [
            (qkv, (1, qkv.shape[1], BLOCK), lambda b, n: (n, 0, b)),
            (in_clip[None, :], (1, BLOCK), lambda b, n: (0, b)),
            (in_clip[:, None], (BLOCK, 1), lambda b, n: (b, 0)),
        ],
        [
            (
                (shape.panels, shape.out_rows, shape.tokens),
                low,
                (1, shape.out_rows, BLOCK),
                lambda b, n: (n, 0, b),
            ),
            (
                (blocks, shape.panels, heads, BLOCK, BLOCK),
                low,
                (1, 1, heads, BLOCK, BLOCK),
                lambda b, n: (b, n, 0, 0, 0),
            ),
        ],
    )


def attention_backward(shape, qkv, probs, grad_attended):
    width = shape.local
    heads = width // HEAD_DIM
    blocks = shape.tokens // BLOCK
    score_scale = 1.0 / math.sqrt(HEAD_DIM)

    def kernel(qkv_ref, probs_ref, grad_ref, out_ref):
        queries = qkv_ref[0, :width].astype(high)
        key_rows = qkv_ref[0, width : 2 * width].astype(high)
        value_rows = qkv_ref[0, 2 * width : 3 * width].astype(high)
        grads = grad_ref[0].astype(high)[shape.out_skip :]
        query_parts, key_parts, value_parts = [], [], []
        for head in range(heads):
            probs_low = probs_ref[0, 0, head]
            grad_head = head_rows(grads, head)
            value_parts.append(contract(grad_head, probs_low, 1, 1))
            grad_probs = contract(head_rows(value_rows, head), grad_head, 0, 0)
            probs = probs_low.astype(high)
            crossed = jnp.sum(grad_probs * probs, axis=0, keepdims=True)
            grad_scores = (probs * (grad_probs - crossed)).astype(low)
            query_parts.append(contract(head_rows(key_rows, head), grad_scores, 1, 0) * score_scale)
            key_parts.append(contract(head_rows(queries, head), grad_scores, 1, 1) * score_scale)
        rest = [jnp.zeros((shape.qkv_rows - 3 * width, BLOCK), high)]
        out_ref[0] = jnp.concatenate(
            query_parts + key_parts + value_parts + rest, axis=0
        ).astype(low)

    return call(
        kernel,
        "attention_backward",
        (blocks, shape.panels),
        [
            (qkv, (1, qkv.shape[1], BLOCK), lambda b, n: (n, 0, b)),
            (probs, (1, 1, heads, BLOCK, BLOCK), lambda b, n: (b, n, 0, 0, 0)),
            (grad_attended, (1, shape.out_rows, BLOCK), lambda b, n: (n, 0, b)),
        ],
        [
            (
                (shape.panels, shape.qkv_rows, shape.tokens),
                low,
                (1, shape.qkv_rows, BLOCK),
                lambda b, n: (n, 0, b),
            )
        ],
    )[0]


def add_panel(total, step, product):
    @pl.when(step == 0)
    def _():
        total[...] = product

    @pl.when(step > 0)
    def _():
        total[...] += product


def project_out(shape, weights, attended, residual, table):
    count = len(weights.arrays)

    def kernel(*refs):
        weight_refs, rest = refs[:count], refs[count:]
        attended_ref, residual_ref, table_ref, middle_ref, branch_ref, input_ref = rest[:6]
        held, sems, total = rest[6:]
        step = pl.program_id(0)
        panel = weights.panel(weight_refs, held, sems, step)
        add_panel(total, step, contract(panel[...], attended_ref[0], 1, 0))

        @pl.when(step == shape.panels - 1)
        def _():
            table = table_ref[...]
            for block in range(shape.blocks):
                at = slice(block * shape.block, (block + 1) * shape.block)
                branch = total[:, at]
                middle = residual_ref[:, at].astype(high) + branch * spread(shape, table, 2, block)
                normed, _ = normed_rows(middle)
                middle_ref[:, at] = middle
                branch_ref[:, at] = branch.astype(low)
                input_ref[:, at] = (
                    normed * (1.0 + spread(shape, table, 4, block)) + spread(shape, table, 3, block)
                ).astype(low)

    whole = (shape.width, shape.tokens)
    return call(
        kernel,
        "project_out",
        (shape.panels,),
        weights.ins() + [panel_in(attended), (residual, None, None), (table, None, None)],
        [(whole, high, None, None), (whole, low, None, None), (whole, low, None, None)],
        weights.scratch() + [pltpu.VMEM(whole, high)],
    )


def gelu_and_slope(values):
    root = math.sqrt(2.0 / math.pi)
    square = values * values
    bent = jnp.tanh(root * values * (1.0 + 0.044715 * square))
    half = 0.5 * (1.0 + bent)
    slope = half + 0.5 * values * (1.0 - bent * bent) * (root + 3.0 * 0.044715 * root * square)
    return values * half, slope


def project_up(shape, weights, source, bias):
    count = len(weights.arrays)
    inner = weights.stop

    def kernel(*refs):
        weight_refs, rest = refs[:count], refs[count:]
        source_ref, bias_ref, hidden_ref, slope_ref, held, sems = rest
        panel = weights.panel(weight_refs, held, sems, pl.program_id(0))
        values = contract(panel[...], source_ref[...], 0, 0) + bias_ref[0]
        hidden, slope = gelu_and_slope(values)
        hidden_ref[0] = hidden.astype(low)
        slope_ref[0] = slope.astype(low)

    return call(
        kernel,
        "project_up",
        (shape.panels,),
        weights.ins() + [(source, None, None), panel_in(bias)],
        [by_panel(shape, inner, low), by_panel(shape, inner, low)],
        weights.scratch(),
    )


def project_down(shape, there, weights, hidden, middle, upstream, table, wide_count):
    count = len(weights.arrays)
    bias_at = 6 * shape.seqs

    def kernel(at_ref, *refs):
        weight_refs, rest = refs[:count], refs[count:]
        hidden_ref, middle_ref, upstream_ref, table_ref, out_ref, gate_ref = rest[:6]
        held, sems, total, block_held = rest[6:]
        step = pl.program_id(0)
        panel = weights.panel(weight_refs, held, sems, step)
        add_panel(total, step, contract(panel[...], hidden_ref[0], 1, 0))

        @pl.when(step == shape.panels - 1)
        def _():
            table = table_ref[...]
            bias = pick(table, bias_at)
            sums = []
            for block in range(shape.blocks):
                at = slice(block * shape.block, (block + 1) * shape.block)
                mlp = total[:, at] + bias
                out = middle_ref[:, at] + mlp * spread(shape, table, 5, block)
                block_held[...] = out.reshape(block_held.shape)
                take_pieces(shape, at_ref, block_held, out_ref, block)
                sums += seq_sums(shape, upstream_ref[:, at].astype(high) * mlp)
            gate_ref[...] = jnp.concatenate(sums, axis=1)

    whole = (shape.width, shape.tokens)
    return call(
        kernel,
        "project_down",
        (shape.panels,),
        weights.ins()
        + [panel_in(hidden)]
        + [(middle, None, None), (upstream, None, None), (table, None, None)],
        [pieces_out(shape), ((shape.width, shape.seqs), high, None, None)],
        weights.scratch()
        + [
            pltpu.VMEM(whole, high),
            pltpu.VMEM((wide_count, shape.width // wide_count, shape.block), high),
        ],
        [there],
    )


def grad_outs(shape, columns):
    tall = shape.panels // 2
    half = shape.width // 2
    return [((tall, half, columns), low, (1, half, columns), lambda n, *_: (n, 0, 0))] * 2


def core_panels(shape, array, core):
    tall = shape.panels // 2
    return (array, (1, *array.shape[1:]), lambda n, *_: (n + core * tall, 0, 0))


def weight_grad(shape, name, source, grad, core):
    columns = grad.shape[1]
    half = shape.width // 2

    def kernel(source_ref, grad_ref, near_ref, beside_ref):
        product = contract(source_ref[...], grad_ref[0], 1, 1).astype(low)
        near_ref[0] = product[:half]
        beside_ref[0] = product[half:]

    return call(
        kernel,
        name,
        (shape.panels // 2,),
        [(source, None, None), core_panels(shape, grad, core)],
        grad_outs(shape, columns),
    )


def first_weight_grad(shape, source, grad_qkv, grad_branch, attended, core):
    columns = 4 * shape.local
    begin = shape.out_from
    half = shape.width // 2

    def kernel(source_ref, qkv_ref, branch_ref, attended_ref, near_ref, beside_ref, held):
        held[:, : shape.qkv_rows] = contract(source_ref[...], qkv_ref[0], 1, 1)
        late = contract(branch_ref[...], attended_ref[0], 1, 1)
        both_there = shape.qkv_rows - begin
        if both_there:
            held[:, begin : shape.qkv_rows] += late[:, :both_there]
        held[:, shape.qkv_rows :] = late[:, both_there:]
        near_ref[0] = held[:half].astype(low)
        beside_ref[0] = held[half:].astype(low)

    return call(
        kernel,
        "first_weight_grad",
        (shape.panels // 2,),
        [
            (source, None, None),
            core_panels(shape, grad_qkv, core),
            (grad_branch, None, None),
            core_panels(shape, attended, core),
        ],
        grad_outs(shape, columns),
        [pltpu.VMEM((shape.width, columns), high)],
    )


def hidden_backward(shape, weights, grad_mlp, slope):
    count = len(weights.arrays)
    inner = weights.stop

    def kernel(*refs):
        weight_refs, rest = refs[:count], refs[count:]
        grad_ref, slope_ref, out_ref, bias_ref, held, sems = rest
        panel = weights.panel(weight_refs, held, sems, pl.program_id(0))
        values = contract(panel[...], grad_ref[...], 0, 0) * slope_ref[0].astype(high)
        values = values.astype(low)
        out_ref[0] = values
        bias_ref[0] = jnp.sum(values.astype(high), axis=1, keepdims=True)

    return call(
        kernel,
        "hidden_backward",
        (shape.panels,),
        weights.ins() + [(grad_mlp, None, None), panel_in(slope)],
        [
            by_panel(shape, inner, low),
            ((shape.panels, inner, 1), high, (1, inner, 1), lambda n, *_: (n, 0, 0)),
        ],
        weights.scratch(),
    )


def middle_backward(shape, weights, grad_up, middle, upstream, branch, table):
    count = len(weights.arrays)

    def kernel(*refs):
        weight_refs, rest = refs[:count], refs[count:]
        grad_ref, middle_ref, upstream_ref, branch_ref, table_ref = rest[:5]
        out_ref, low_ref, sums_ref, held, sems, total = rest[5:]
        step = pl.program_id(0)
        panel = weights.panel(weight_refs, held, sems, step)
        add_panel(total, step, contract(panel[...], grad_ref[0], 1, 0))

        @pl.when(step == shape.panels - 1)
        def _():
            table = table_ref[...]
            gates, shifts, scales = [], [], []
            for block in range(shape.blocks):
                at = slice(block * shape.block, (block + 1) * shape.block)
                grad = total[:, at]
                normed, inverse = normed_rows(middle_ref[:, at])
                shifts += seq_sums(shape, grad)
                scales += seq_sums(shape, grad * normed)
                grad = upstream_ref[:, at].astype(high) + norm_backward(
                    grad * (1.0 + spread(shape, table, 4, block)), normed, inverse
                )
                gates += seq_sums(shape, grad * branch_ref[:, at].astype(high))
                out_ref[:, at] = grad
                low_ref[:, at] = (grad * spread(shape, table, 2, block)).astype(low)
            sums_ref[...] = jnp.concatenate(gates + shifts + scales, axis=1)

    whole = (shape.width, shape.tokens)
    return call(
        kernel,
        "middle_backward",
        (shape.panels,),
        weights.ins()
        + [panel_in(grad_up)]
        + [(v, None, None) for v in (middle, upstream, branch, table)],
        [
            (whole, high, None, None),
            (whole, low, None, None),
            ((shape.width, 3 * shape.seqs), high, None, None),
        ],
        weights.scratch() + [pltpu.VMEM(whole, high)],
    )


def attended_backward(shape, weights, grad_branch):
    count = len(weights.arrays)

    def kernel(*refs):
        weight_refs, (grad_ref, out_ref, held, sems) = refs[:count], refs[count:]
        panel = weights.panel(weight_refs, held, sems, pl.program_id(0))
        out_ref[0] = contract(panel[...], grad_ref[...], 0, 0).astype(low)

    return call(
        kernel,
        "attended_backward",
        (shape.panels,),
        weights.ins() + [(grad_branch, None, None)],
        [by_panel(shape, shape.out_rows, low)],
        weights.scratch(),
    )[0]


def input_backward(shape, there, weights, grad_qkv, residual, grad_middle, table, wide_count):
    count = len(weights.arrays)

    def kernel(at_ref, *refs):
        weight_refs, rest = refs[:count], refs[count:]
        qkv_ref, residual_ref, middle_ref, table_ref, out_ref, sums_ref = rest[:6]
        held, sems, total, block_held = rest[6:]
        step = pl.program_id(0)
        panel = weights.panel(weight_refs, held, sems, step)
        add_panel(total, step, contract(panel[...], qkv_ref[0], 1, 0))

        @pl.when(step == shape.panels - 1)
        def _():
            table = table_ref[...]
            shifts, scales = [], []
            for block in range(shape.blocks):
                at = slice(block * shape.block, (block + 1) * shape.block)
                grad = total[:, at]
                normed, inverse = normed_rows(residual_ref[:, at].astype(high))
                shifts += seq_sums(shape, grad)
                scales += seq_sums(shape, grad * normed)
                grad = middle_ref[:, at] + norm_backward(
                    grad * (1.0 + spread(shape, table, 1, block)), normed, inverse
                )
                block_held[...] = grad.reshape(block_held.shape)
                take_pieces(shape, at_ref, block_held, out_ref, block)
            sums_ref[...] = jnp.concatenate(shifts + scales, axis=1)

    whole = (shape.width, shape.tokens)
    return call(
        kernel,
        "input_backward",
        (shape.panels,),
        weights.ins()
        + [panel_in(grad_qkv)]
        + [(v, None, None) for v in (residual, grad_middle, table)],
        [pieces_out(shape), ((shape.width, 2 * shape.seqs), high, None, None)],
        weights.scratch()
        + [
            pltpu.VMEM(whole, high),
            pltpu.VMEM((wide_count, shape.width // wide_count, shape.block), high),
        ],
        [there],
    )


def on_device(
    tokens,
    ada_weight,
    ada_bias,
    class_table,
    query_weight,
    key_weight,
    value_weight,
    out_weight,
    up_weight,
    up_bias,
    down_weight,
    down_bias,
    cotangent,
    clip_frames,
    time_ids,
    class_ids,
):
    micro_count, seq_count, local_width, seq_tokens = tokens.shape
    class_count, full_width = class_table.shape
    panels, wide_count = lax.axis_size("narrow"), lax.axis_size("wide")
    wide_at = lax.axis_index("wide")
    seqs = micro_count * seq_count
    shape = Shape(seqs, seq_tokens // panels, full_width, panels)
    own_rows = ada_weight.shape[0]
    highest = lax.Precision.HIGHEST
    local_shape = (seqs, local_width, seq_tokens)
    there, came, goes = orders()

    class_hot = (class_ids.reshape(seqs)[:, None] == jnp.arange(class_count)[None, :]).astype(low)
    condition = time_embedding(time_ids.reshape(seqs), full_width) + jnp.einsum(
        "sc,cd->sd", class_hot, class_table, preferred_element_type=high
    )
    sigmoid_cond = jax.nn.sigmoid(condition)
    cond_act = (condition * sigmoid_cond).astype(low)
    silu_slope = sigmoid_cond * (1.0 + condition * (1.0 - sigmoid_cond))
    own_cond = lax.dynamic_slice_in_dim(cond_act, wide_at * own_rows, own_rows, axis=1)
    own_slope = lax.dynamic_slice_in_dim(silu_slope, wide_at * own_rows, own_rows, axis=1)

    first_piece = jnp.concatenate([query_weight, key_weight, value_weight, out_weight.T], axis=1)
    first, up, down = Gather(first_piece), Gather(up_weight), LateGather(down_weight.T)
    deep = first.deep
    token_cut = cut_tokens(shape, tokens.reshape(local_shape))
    token_parts = swap_narrow(token_cut)
    down_line = down.side()
    first.step()
    mod_part = jnp.einsum("sd,dje->jse", own_cond, ada_weight, preferred_element_type=high)
    mod_part = mod_part.reshape(6 * seqs, local_width)
    hops = [{"side_by": 1}]
    while 2 ** len(hops) <= deep:
        hops.append({"deep_by": 2 ** (len(hops) - 1)})
    earlier = (down_line, first.ring[-1])
    for at in range(max(deep - 2, len(hops))):
        if at < deep - 2:
            if at + 2 == deep // 2 + 1:
                first.front_side(*earlier)
            first.step(*earlier)
        if at < len(hops):
            mod_part = mod_part + send(after(mod_part, *earlier), **hops[at])
        earlier = (first.ring[-1],) if at + 1 < deep - 2 else ()
    mod_own = (
        mod_part.reshape(6, seqs, local_width) + ada_bias.astype(high)[:, None, :]
    ).reshape(6 * seqs, local_width)
    round_three = (first.ring[-1], first.front)
    first.rear_tall(*round_three, token_parts)
    up.step(*round_three)
    small = gather_narrow(
        after(
            jnp.concatenate(
                [
                    mod_own,
                    down_bias.astype(high)[None, :],
                    up_bias.astype(high).reshape(-1, local_width),
                ]
            ),
            first.ring[-1],
        )
    )
    round_four = (first.rear, up.ring[-1], small)
    first.rear_side(*round_four)
    first.front_tall(*round_four)
    for _ in range(2, deep):
        up.step(*round_four)
    table, up_bias_full = lay_small(shape, came, small, wide_count)
    frame_at = jnp.arange(shape.part) % FRAMES
    in_clip = (frame_at[None, :] < clip_frames.reshape(seqs)[:, None]).astype(jnp.int32).reshape(-1)
    residual, input_one = prepare_tokens(shape, there, token_parts, table, wide_count)
    first_got = first.early_cores(*round_four)
    first_all = first.cores()
    round_five = (first.beside, *first.fronts, *first_got, up.ring[-1], input_one)
    up.front_side(*round_five)
    down.along_tall(*round_five)

    qkv_weights = Weights(first_all, 0, shape.qkv_rows)
    out_weights = Weights(first_all, shape.out_from)
    qkv = project_qkv(shape, qkv_weights, input_one)
    round_six = (up.front, down.ring[0])
    qkv = after(qkv, *round_six)
    up.rear_tall(*round_six, qkv)
    down.step(*round_six, qkv)
    attended, probs = attention_forward(shape, qkv, in_clip)
    round_seven = (up.rear, down.ring[1])
    attended = after(attended, *round_seven)
    up.rear_side(*round_seven, attended)
    up.front_tall(*round_seven, attended)
    for _ in range(2, deep - 1):
        down.step(*round_seven, attended)
    middle, branch, input_two = project_out(shape, out_weights, attended, residual, table)
    up_got = up.early_cores(*round_seven, attended)
    round_eight = (up.beside, *up.fronts, *up_got, down.ring[-1], input_two)
    up_all = Weights(up.cores(input_two))
    upstream_cut = cut_tokens(shape, after(cotangent.reshape(local_shape), *round_eight))
    upstream_parts = swap_narrow(upstream_cut)
    down.step(*round_eight)
    down_got = [down.core(*round_eight) for _ in range(deep - 1)]
    hidden, slope = project_up(shape, up_all, after(input_two, upstream_cut), up_bias_full)
    upstream, grad_mlp, down_bias_part = prepare_upstream(
        shape, there, upstream_parts, after(table, hidden, down.ring[-1], *down_got), wide_count
    )
    down.core(grad_mlp)
    down_all = Weights(down.cores())

    other = weight_grad(shape, "down_weight_grad", grad_mlp, hidden, 1)
    down_sum = GradSum(other)
    near = weight_grad(shape, "down_weight_grad", after(grad_mlp, *other), hidden, 0)
    down_sum.near(near)
    sums = down_sum.sums_side()
    down_sum.side(sums)
    grad_up, up_bias_part = hidden_backward(shape, down_all, after(grad_mlp, *near, *sums), slope)
    other = weight_grad(shape, "up_weight_grad", input_two, grad_up, 1)
    up_sum = GradSum(other)
    near = weight_grad(shape, "up_weight_grad", after(input_two, *other), grad_up, 0)
    up_sum.near(near)
    sums = up_sum.sums_tall()
    up_sum.along_tall(sums)
    grad_middle, grad_branch, middle_sums = middle_backward(
        shape, up_all, after(grad_up, *near, *sums), middle, upstream, branch, table
    )
    down_sum.hold(grad_branch)
    sums = down_sum.sums_deep()
    down_sum.along_deep(sums)
    grad_attended = attended_backward(shape, out_weights, after(grad_branch, *sums))
    grad_qkv = attention_backward(shape, qkv, probs, grad_attended)
    up_sum.hold(grad_qkv)
    sums = up_sum.sums_side()
    up_sum.side(sums)
    grad_qkv = after(grad_qkv, *sums)
    other = first_weight_grad(shape, input_one, grad_qkv, grad_branch, attended, 1)
    first_sum = GradSum(other)
    near = first_weight_grad(
        shape, after(input_one, *other), grad_qkv, grad_branch, attended, 0
    )
    first_sum.near(near)
    down_sum.hold(*near)
    down_sums = down_sum.sums_late_tall()
    first_sum.hold(*near, *down_sums)
    side_half, tall_half = first_sum.split(deep // 2)
    side_sums, tall_sums = side_half.sums_side(), tall_half.sums_tall()
    side_half.side(side_sums)
    tall_half.along_tall(tall_sums)
    down_sum.late_tall(down_sums, *side_sums, *tall_sums)
    grad_qkv = after(grad_qkv, *side_sums, *tall_sums, *down_sums)
    input_parts, input_sums = input_backward(
        shape, there, qkv_weights, grad_qkv, residual, grad_middle, table, wide_count
    )
    for one in (up_sum, side_half, tall_half):
        one.hold(input_sums)
    up_sums = up_sum.sums_each_deep()
    side_sums, tall_sums = tall_half.sums_side(), side_half.sums_tall()
    side_half.along_tall(tall_sums, input_sums)
    tall_half.side(side_sums, input_sums)
    up_sum.along_each_deep(up_sums, *side_sums, *tall_sums)
    output_parts, gate_two_part = project_down(
        shape,
        there,
        down_all,
        hidden,
        middle,
        upstream,
        after(table, input_sums, *side_sums, *tall_sums, *up_sums),
        wide_count,
    )
    for one in (side_half, tall_half):
        one.hold(gate_two_part)
    first_sum.parts = [
        [
            jnp.concatenate(
                [added(half.parts[0], slice(None)) for half in (side_half, tall_half)], axis=1
            )
        ]
    ]
    sums = first_sum.sums_each_deep()
    first_got = first_sum.along_each_deep(sums)
    input_got = swap_narrow(input_parts)
    gate_two_part = after(gate_two_part, input_got, *sums)
    output_got = swap_narrow(after(output_parts, input_got))
    input_grad = join_tokens(shape, input_got, high)
    output = join_tokens(shape, output_got, low)
    down_grad = down_sum.result()
    up_grad = up_sum.result()
    first_grad = first_sum.result()

    small_grad = sum_wide(
        scatter_narrow(
            lay_small_grads(
                shape,
                goes,
                input_sums,
                middle_sums,
                gate_two_part,
                down_bias_part,
                up_bias_part,
                wide_count,
            )
        )
    )
    own_mod = small_grad[: 6 * seqs].reshape(6, seqs, local_width)
    down_bias_grad = small_grad[6 * seqs]
    up_bias_grad = small_grad[6 * seqs + 1 :].reshape(-1)
    ada_grad = jnp.einsum("sd,jse->dje", own_cond.astype(high), own_mod, precision=highest)
    ada_bias_grad = jnp.sum(own_mod, axis=1)
    own_mod = after(own_mod, *first_got)
    cond_local = sum_narrow(
        own_slope * jnp.einsum("jse,dje->sd", own_mod, ada_weight.astype(high), precision=highest)
    )
    cond_grad = sum_wide(
        lax.dynamic_update_slice_in_dim(
            jnp.zeros((seqs, full_width), high), cond_local, wide_at * own_rows, axis=1
        )
    )
    table_grad = jnp.einsum("sc,sd->cd", class_hot.astype(high), cond_grad, precision=highest)
    return (
        output.reshape(tokens.shape),
        input_grad.reshape(tokens.shape),
        ada_grad,
        ada_bias_grad,
        table_grad,
        first_grad[:, :local_width],
        first_grad[:, local_width : 2 * local_width],
        first_grad[:, 2 * local_width : 3 * local_width],
        first_grad[:, 3 * local_width :].T,
        up_grad,
        up_bias_grad,
        down_grad.T,
        down_bias_grad,
    )


def solution(mesh):
    return jax.shard_map(
        on_device,
        mesh=mesh,
        in_specs=(
            P(None, None, "narrow", "wide"),
            P("wide", None, "narrow"),
            P(None, "narrow"),
            P(),
            P("wide", "narrow"),
            P("wide", "narrow"),
            P("wide", "narrow"),
            P("narrow", "wide"),
            P("wide", "narrow"),
            P("narrow"),
            P("narrow", "wide"),
            P("narrow"),
            P(None, None, "narrow", "wide"),
            P(),
            P(),
            P(),
        ),
        out_specs=(
            P(None, None, "narrow", "wide"),
            P(None, None, "narrow", "wide"),
            P("wide", None, "narrow"),
            P(None, "narrow"),
            P(),
            P("wide", "narrow"),
            P("wide", "narrow"),
            P("wide", "narrow"),
            P("narrow", "wide"),
            P("wide", "narrow"),
            P("narrow"),
            P("narrow", "wide"),
            P("narrow"),
        ),
        check_vma=False,
    )
```

```python
import functools
import math

import jax
import jax.numpy as jnp
from jax import lax
from jax.experimental import pallas as pl
from jax.experimental.pallas import tpu as pltpu
from jax.sharding import PartitionSpec as P

HEAD_DIM = 72
FRAMES = 16
BLOCK = 128
MIB = 1024 * 1024
COSTS = {
    "project_qkv": 15,
    "attention_forward": 24,
    "project_out": 17,
    "project_up": 28,
    "project_down": 25,
    "down_weight_grad": 10,
    "up_weight_grad": 10,
    "first_weight_grad": 12,
    "hidden_backward": 21,
    "middle_backward": 30,
    "attended_backward": 9,
    "attention_backward": 33,
    "input_backward": 25,
}
COST_SCALE = 1e8

norm_epsilon = 1e-06
masked_score = -1e30
both = ("wide", "narrow")
low = jnp.bfloat16
high = jnp.float32


def time_embedding(time_ids, full_width):
    half_width = full_width // 2
    frequency = jnp.exp(-math.log(10000.0) * jnp.arange(half_width, dtype=jnp.float32) / half_width)
    angles = time_ids.astype(jnp.float32)[..., None] * frequency
    return jnp.concatenate([jnp.cos(angles), jnp.sin(angles)], axis=-1)


def place():
    deep, tall = lax.axis_size("wide") // 2, lax.axis_size("narrow") // 2
    wide_at, narrow_at = lax.axis_index("wide"), lax.axis_index("narrow")
    return deep, tall, wide_at // 2, wide_at % 2, narrow_at // 2, narrow_at % 2


def send(value, deep_by=0, side_by=0, tall_by=0, core_by=0):
    deep, tall = lax.axis_size("wide") // 2, lax.axis_size("narrow") // 2
    pairs = []
    for z in range(deep):
        for x in range(2):
            for y in range(tall):
                for c in range(2):
                    source = ((z * 2 + x) * tall + y) * 2 + c
                    target = (
                        ((z + deep_by) % deep * 2 + (x + side_by) % 2) * tall + (y + tall_by) % tall
                    ) * 2 + (c + core_by) % 2
                    pairs.append((source, target))
    return lax.ppermute(value, both, pairs)


def after(value, *earlier):
    return lax.optimization_barrier((value, earlier))[0]


def sync(*values):
    arrays = []
    for value in values:
        if isinstance(value, GradSum):
            arrays += [array for array, _ in value.terms]
        elif isinstance(value, (list, tuple)):
            arrays += value
        else:
            arrays.append(value)
    arrays = iter(lax.optimization_barrier(tuple(arrays)))
    results = []
    for value in values:
        if isinstance(value, GradSum):
            value.terms = [(next(arrays), cuts) for _, cuts in value.terms]
            results.append(value)
        elif isinstance(value, (list, tuple)):
            results.append([next(arrays) for _ in value])
        else:
            results.append(next(arrays))
    return results


class Gather:
    def __init__(self, piece):
        self.deep = lax.axis_size("wide") // 2
        self.tall = lax.axis_size("narrow") // 2
        self.ring = [piece]
        self.rows = piece.shape[0]

    def step(self):
        self.ring.append(send(self.ring[-1], deep_by=1))

    def front_side(self):
        self.front = jnp.concatenate(self.ring[: self.deep // 2], axis=0)
        self.front_got = [send(self.front, side_by=1)]

    def rear_tall(self):
        self.rear = jnp.concatenate(self.ring[self.deep // 2 :], axis=0)
        self.rear_got = [send(self.rear, tall_by=k) for k in range(1, self.tall)]

    def second(self):
        self.front = jnp.concatenate([self.front] + self.front_got, axis=0)
        self.rear = jnp.concatenate([self.rear] + self.rear_got, axis=0)
        self.arrays = [self.rear, send(self.rear, side_by=1), self.front]
        self.arrays += [send(self.front, tall_by=k) for k in range(1, self.tall)]
        self.cores = [None] * len(self.arrays)

    def core(self, *at):
        for k in at:
            self.cores[k] = send(self.arrays[k], core_by=1)

    def result(self):
        count = len(self.arrays)
        near = self.deep // 2 * self.rows
        far = self.deep * self.rows - near
        panels = []
        for c in range(2):
            for y in range(self.tall):
                panels.append(
                    [
                        (c * count + 2 + y, (), 0, 0, near),
                        (c * count, (), y * far, near, far),
                        (c * count + 2 + y, (), near, near + far, near),
                        (c * count + 1, (), y * far, 2 * near + far, far),
                    ]
                )
        return self.arrays + self.cores, panels


class LateGather:
    def __init__(self, piece):
        self.deep = lax.axis_size("wide") // 2
        self.tall = lax.axis_size("narrow") // 2
        self.piece = piece
        self.cores = []

    def side(self):
        self.line = [self.piece, send(self.piece, side_by=1)]

    def along_tall(self):
        line = jnp.stack(self.line)
        self.plane = [line] + [send(line, tall_by=k) for k in range(1, self.tall)]

    def step(self):
        if not hasattr(self, "ring"):
            self.ring = [jnp.stack(self.plane)]
        self.ring.append(send(self.ring[-1], deep_by=1))

    def core(self, *at):
        self.cores += [send(self.ring[k], core_by=1) for k in at]

    def result(self):
        tall, deep, rows = self.tall, self.deep, self.piece.shape[0]
        arrays = self.ring + self.cores
        if rows % 16:
            whole = [
                jnp.concatenate([arrays[c * deep + k][y, x] for x in range(2) for k in range(deep)])
                for c in range(2)
                for y in range(tall)
            ]
            return whole, [[(at, (), 0, 0, 2 * deep * rows)] for at in range(2 * tall)]
        panels = [
            [
                (c * deep + k, (y, x), 0, (x * deep + k) * rows, rows)
                for x in range(2)
                for k in range(deep)
            ]
            for c in range(2)
            for y in range(tall)
        ]
        return arrays, panels


def device_order():
    deep, tall, z, x, y, c = place()
    order = []
    for core in range(2):
        for k in range(tall):
            n = (y - k) % tall * 2 + (c - core) % 2
            for side in range(2):
                for far in range(deep):
                    w = (z - far) % deep * 2 + (x - side) % 2
                    order.append(w * 2 * tall + n)
    return jnp.stack(order).astype(jnp.int32)


class GradSum:
    def __init__(self, other):
        self.sizes = {"x": 2, "y": lax.axis_size("narrow") // 2, "z": lax.axis_size("wide") // 2}
        self.got = send(other, core_by=-1)

    def near(self, near):
        _, tall, rows, columns = near.shape
        deep = self.sizes["z"]
        shape = (2, tall, deep, rows // deep, columns)
        self.terms = [(near.reshape(shape), ()), (self.got.reshape(shape), ())]
        self.axes = "xyz"

    def copy(self, cuts):
        one = GradSum.__new__(GradSum)
        one.sizes, one.axes = dict(self.sizes), self.axes
        one.terms = [(array, earlier + cuts) for array, earlier in self.terms]
        return one

    def split(self, *ends):
        parts = []
        for start, end in zip((0, *ends), (*ends, self.sizes["z"])):
            part = self.copy((self.at("z", slice(start, end)),))
            part.sizes["z"] = end - start
            parts.append(part)
        return parts

    def at(self, axis, k):
        return (slice(None),) * self.axes.index(axis) + (k,)

    def hold(self, *earlier):
        self.terms = [(after(array, *earlier), cuts) for array, cuts in self.terms]
        return self

    def total(self, *cuts):
        total = 0.0
        for array, earlier in self.terms:
            for one in earlier + cuts:
                array = array[one]
            total = total + array.astype(high)
        return total

    def sums(self, axis):
        return [self.total(self.at(axis, k)).astype(low) for k in range(1, self.sizes[axis])]

    def along(self, axis, sums, *earlier):
        by = {"x": "side_by", "y": "tall_by", "z": "deep_by"}[axis]
        gots = [send(after(v, *earlier), **{by: -k}) for k, v in enumerate(sums, 1)]
        self.receive(axis, gots)
        return gots

    def receive(self, axis, gots):
        own = self.at(axis, 0)
        self.terms = [(array, cuts + (own,)) for array, cuts in self.terms] + [(v, ()) for v in gots]
        self.axes = self.axes.replace(axis, "")


def deep_sums(parts):
    return [
        part.total(part.at("z", k)).astype(low) for part in parts for k in range(part.sizes["z"])
    ][1:]


def along_deep(parts, sums, *earlier):
    first = parts[0]
    gots = [send(after(v, *earlier), deep_by=-k) for k, v in enumerate(sums, 1)]
    first.receive("z", gots)
    return gots


def swap_narrow(parts):
    return lax.all_to_all(parts, "narrow", 0, 0, tiled=True)


class NarrowSwap:
    def __init__(self, parts):
        self.tall = lax.axis_size("narrow") // 2
        self.parts = parts
        _, _, _, _, self.y, self.c = place()
        self.own = [self.pick(0, core) for core in range(2)]

    def pick(self, k, core):
        target = (self.y + k) % self.tall * 2 + (self.c + core) % 2
        part = self.parts.shape[2] // (2 * self.tall)
        return lax.dynamic_slice_in_dim(self.parts, target * part, part, axis=2)[None]

    def step(self, core):
        return [send(self.pick(k, core), tall_by=k) for k in range(1, self.tall)]

    def pieces(self, same, other):
        other = send(jnp.concatenate([self.own[1]] + other, axis=0), core_by=1)
        return [self.own[0]] + same, other


def orders():
    deep, tall, z, x, y, c = place()
    wide_count, narrow_count = 2 * deep, 2 * tall
    ratio = wide_count // narrow_count

    def stands(n, h):
        w = n * ratio + h
        return (x - w % 2) % 2 * deep + (z - w // 2) % deep

    there = [stands(n, h) for n in range(narrow_count) for h in range(ratio)]
    came, goes = [], []
    for core_by in range(2):
        for tall_by in range(tall):
            source = (y - tall_by) % tall * 2 + (c - core_by) % 2
            target = (y + tall_by) % tall * 2 + (c + core_by) % 2
            came += [stands(source, h) for h in range(ratio)]
            goes += [stands(target, h) for h in range(ratio)]
    return [jnp.stack(v).astype(jnp.int32) for v in (there, came, goes)]


def sum_wide(value):
    deep = lax.axis_size("wide") // 2
    value = value + send(value, side_by=1)
    step = 1
    while step < deep:
        value = value + send(value, deep_by=step)
        step *= 2
    return value


def sum_narrow(value):
    tall = lax.axis_size("narrow") // 2
    value = value + send(value, core_by=1)
    step = 1
    while step < tall:
        value = value + send(value, tall_by=step)
        step *= 2
    return value


def gather_narrow(value):
    tall = lax.axis_size("narrow") // 2
    own = jnp.stack([value] + [send(value, tall_by=k) for k in range(1, tall)])
    return jnp.concatenate([own, send(own, core_by=1)])


def scatter_narrow(value):
    tall = lax.axis_size("narrow") // 2
    value = value.reshape(2, tall, *value.shape[1:])
    total = value[0] + send(value[1], core_by=1)
    return sum([total[0]] + [send(total[k], tall_by=k) for k in range(1, tall)])


def contract(left, right, left_dim, right_dim):
    return lax.dot_general(
        left, right, (((left_dim,), (right_dim,)), ((), ())), preferred_element_type=jnp.float32
    )


def call(kernel, name, grid, ins, outs, scratch=(), prefetch=(), vmem=60):
    in_specs = []
    for array, block, index in ins:
        if block == "any":
            in_specs.append(pl.BlockSpec(memory_space=pl.ANY))
        elif block is None:
            in_specs.append(pl.BlockSpec(array.shape, lambda *_, r=array.ndim: (0,) * r))
        else:
            in_specs.append(pl.BlockSpec(block, index))
    out_specs = []
    for shape, _, block, index in outs:
        if block is None:
            out_specs.append(pl.BlockSpec(shape, lambda *_, r=len(shape): (0,) * r))
        else:
            out_specs.append(pl.BlockSpec(block, index))
    return pl.pallas_call(
        kernel,
        grid_spec=pltpu.PrefetchScalarGridSpec(
            num_scalar_prefetch=len(prefetch),
            grid=grid,
            in_specs=in_specs,
            out_specs=out_specs,
            scratch_shapes=list(scratch),
        ),
        out_shape=[jax.ShapeDtypeStruct(shape, kind) for shape, kind, _, _ in outs],
        compiler_params=pltpu.CompilerParams(vmem_limit_bytes=vmem * MIB),
        cost_estimate=pl.CostEstimate(
            flops=int(COSTS.get(name, 4) * COST_SCALE), bytes_accessed=0, transcendentals=0
        ),
        name=name,
    )(*prefetch, *[array for array, _, _ in ins])


class Weights:
    def __init__(self, gathered, start=0, stop=None):
        self.arrays, self.panels = gathered
        self.columns = self.arrays[0].shape[-1]
        self.start, self.stop = start, self.columns if stop is None else stop
        self.rows = sum(size for *_, size in self.panels[0])
        self.prefetch = []

    def ins(self):
        return [(array, "any", None) for array in self.arrays]

    def scratch(self, wide=False):
        count, columns = len(self.panels), self.stop - self.start
        self.wide = wide and columns % BLOCK == 0
        return [
            pltpu.VMEM(
                (self.rows, count * columns) if self.wide else (count, self.rows, columns), low
            ),
            pltpu.SemaphoreType.DMA((count, len(self.panels[0]))),
        ]

    def source(self, refs, panel, piece):
        array, lead, begin, row, size = self.panels[panel][piece]
        source = refs[array].at[(*lead, pl.ds(begin, size), slice(self.start, self.stop))]
        return source, row, size

    def copies(self, refs, held, sems, panel):
        copies = []
        columns = self.stop - self.start
        for piece in range(len(self.panels[0])):
            source, row, size = self.source(refs, panel, piece)
            if self.wide:
                target = held.at[pl.ds(row, size), pl.ds(panel * columns, columns)]
            else:
                target = held.at[panel, pl.ds(row, size)]
            copies.append(pltpu.make_async_copy(source, target, sems.at[panel, piece]))
        return copies

    def start_all(self, refs, held, sems, at):
        @pl.when(at == 0)
        def _():
            for panel in range(len(self.panels)):
                for copy in self.copies(refs, held, sems, panel):
                    copy.start()

    def wait(self, refs, held, sems, at, panel, step=0):
        @pl.when(at == step)
        def _():
            for copy in self.copies(refs, held, sems, panel):
                copy.wait()

    def panel(self, refs, held, sems, at):
        self.start_all(refs, held, sems, at)
        for panel in range(len(self.panels)):
            self.wait(refs, held, sems, at, panel, panel)
        return held.at[at]


class GatheredWeights(Weights):
    def __init__(self, gathered, order, panel_count):
        devices, rows, columns = gathered.shape
        blocks = devices // panel_count
        if rows % 16:
            whole = jnp.take(gathered, order, axis=0).reshape(panel_count, blocks * rows, columns)
            super().__init__(([whole], [[(0, (p,), 0, 0, blocks * rows)] for p in range(panel_count)]))
            return
        panels = [
            [(p * blocks + b, (), 0, b * rows, rows) for b in range(blocks)]
            for p in range(panel_count)
        ]
        super().__init__(([gathered], panels))
        self.prefetch = [order]

    def source(self, refs, panel, piece):
        if not self.prefetch:
            return super().source(refs, panel, piece)
        at, _, _, row, size = self.panels[panel][piece]
        return refs[1].at[refs[0][at]], row, size


class Shape:
    def __init__(self, seqs, part, width, panels):
        self.seqs, self.part, self.width, self.panels = seqs, part, width, panels
        self.tokens = seqs * part
        self.block = part if part % BLOCK == 0 else self.tokens
        self.blocks = self.tokens // self.block
        self.share = self.block // part
        local = width // panels
        self.local = local
        self.qkv_rows = min(-(-3 * local // BLOCK) * BLOCK, 4 * local)
        self.out_from = 3 * local // BLOCK * BLOCK
        self.out_rows = 4 * local - self.out_from
        self.out_skip = 3 * local - self.out_from


def pick(table, at):
    lane = lax.broadcasted_iota(jnp.int32, table.shape, 1)
    return jnp.sum(jnp.where(lane == at, table, 0.0), axis=1, keepdims=True)


def spread(shape, table, slot, block):
    picked = [pick(table, slot * shape.seqs + block * shape.share + j) for j in range(shape.share)]
    if shape.share == 1:
        return picked[0]
    return jnp.concatenate(
        [jnp.broadcast_to(one, (one.shape[0], shape.part)) for one in picked], axis=1
    )


def seq_sums(shape, values):
    return [
        jnp.sum(values[:, j * shape.part : (j + 1) * shape.part], axis=1, keepdims=True)
        for j in range(shape.share)
    ]


def normed_rows(values):
    width = values.shape[0]
    center = jnp.sum(values, axis=0, keepdims=True) * (1.0 / width)
    shifted = values - center
    variance = jnp.sum(shifted * shifted, axis=0, keepdims=True) * (1.0 / width)
    inverse = lax.rsqrt(variance + norm_epsilon)
    return shifted * inverse, inverse


def norm_backward(grad_hat, normed, inverse):
    width = normed.shape[0]
    totals = jnp.sum(grad_hat, axis=0, keepdims=True) * (1.0 / width)
    crossed = jnp.sum(grad_hat * normed, axis=0, keepdims=True) * (1.0 / width)
    return inverse * (grad_hat - totals - normed * crossed)


def put_pieces(shape, at_ref, piece_refs, held):
    rows = held.shape[1]
    ratio = shape.local // rows
    for n in range(shape.panels):
        for h in range(ratio):
            for j in range(shape.share):
                ref, lead = (piece_refs[0], n) if len(piece_refs) == 1 else (piece_refs[n], 0)
                held[at_ref[n * ratio + h], :, j * shape.part : (j + 1) * shape.part] = ref[
                    lead, j, h * rows : (h + 1) * rows
                ].astype(high)


def take_pieces(shape, at_ref, held, pieces_ref):
    rows = held.shape[1]
    ratio = shape.local // rows
    for n in range(shape.panels):
        for h in range(ratio):
            for j in range(shape.share):
                pieces_ref[n, j, h * rows : (h + 1) * rows, :] = held[
                    at_ref[n * ratio + h], :, j * shape.part : (j + 1) * shape.part
                ].astype(pieces_ref.dtype)


def pieces_in(shape, pieces):
    if isinstance(pieces, list):
        block = (1, shape.share, shape.local, shape.part)
        return [(piece, block, lambda b, *_: (0, b, 0, 0)) for piece in pieces]
    return [pieces_by_device(shape, pieces)]


def pieces_by_device(shape, pieces):
    return (
        pieces,
        (shape.panels, shape.share, shape.local, shape.part),
        lambda b, *_: (0, b, 0, 0),
    )


def token_out(shape, kind):
    return (
        (shape.width, shape.tokens),
        kind,
        (shape.width, shape.block),
        lambda b, *_: (0, b),
    )


def prepare_tokens(shape, there, pieces, table, wide_count):
    def kernel(at_ref, *refs):
        *piece_refs, table_ref, whole_ref, input_ref, held = refs
        block = pl.program_id(0)
        put_pieces(shape, at_ref, piece_refs, held)
        values = held[...].reshape(shape.width, shape.block)
        normed, _ = normed_rows(values)
        table = table_ref[...]
        whole_ref[...] = values.astype(low)
        input_ref[...] = (
            normed * (1.0 + spread(shape, table, 1, block)) + spread(shape, table, 0, block)
        ).astype(low)

    return call(
        kernel,
        "prepare_tokens",
        (shape.blocks,),
        pieces_in(shape, pieces) + [(table, None, None)],
        [token_out(shape, low), token_out(shape, low)],
        [pltpu.VMEM((wide_count, shape.width // wide_count, shape.block), high)],
        [there],
    )


def prepare_upstream(shape, there, pieces, table, wide_count):
    def kernel(at_ref, pieces_ref, table_ref, whole_ref, grad_ref, bias_ref, held):
        block = pl.program_id(0)
        put_pieces(shape, at_ref, [pieces_ref], held)
        values = held[...].reshape(shape.width, shape.block)
        whole_ref[...] = values.astype(low)
        grad_low = (values * spread(shape, table_ref[...], 5, block)).astype(low)
        grad_ref[...] = grad_low
        total = jnp.sum(grad_low.astype(high), axis=1, keepdims=True)

        @pl.when(block == 0)
        def _():
            bias_ref[...] = total

        @pl.when(block > 0)
        def _():
            bias_ref[...] += total

    return call(
        kernel,
        "prepare_upstream",
        (shape.blocks,),
        pieces_in(shape, pieces) + [(table, None, None)],
        [token_out(shape, low), token_out(shape, low), ((shape.width, 1), high, None, None)],
        [pltpu.VMEM((wide_count, shape.width // wide_count, shape.block), high)],
        [there],
    )


def lay_small(shape, came, small, wide_count):
    rows = shape.width // wide_count
    ratio = shape.local // rows
    first = 6 * shape.seqs + 1
    count = small.shape[1]
    ups = count - first

    def kernel(at_ref, small_ref, table_ref, bias_ref, held):
        for p in range(shape.panels):
            turned = small_ref[p].T
            for h in range(ratio):
                held[at_ref[p * ratio + h]] = turned[h * rows : (h + 1) * rows]
            bias_ref[p] = jnp.concatenate(
                [turned[:, first + k : first + k + 1] for k in range(ups)], axis=0
            )
        table_ref[...] = held[...].reshape(shape.width, count)

    return call(
        kernel,
        "lay_small",
        (1,),
        [(small, None, None)],
        [
            ((shape.width, count), high, None, None),
            ((shape.panels, ups * shape.local, 1), high, None, None),
        ],
        [pltpu.VMEM((wide_count, rows, count), high)],
        [came],
    )


def lay_small_grads(shape, goes, late, middle, gate_two, down_bias, up_bias, wide_count):
    rows = shape.width // wide_count
    ratio = shape.local // rows
    seqs = shape.seqs
    ups = up_bias.shape[1] // shape.local
    count = 6 * seqs + 1 + ups

    def kernel(at_ref, late_ref, middle_ref, gate_ref, down_ref, up_ref, small_ref, held):
        table = jnp.concatenate(
            [late_ref[...], middle_ref[...], gate_ref[...], down_ref[...]], axis=1
        )
        held[...] = table.reshape(wide_count, rows, 6 * seqs + 1)
        for p in range(shape.panels):
            parts = [held[at_ref[p * ratio + h]] for h in range(ratio)]
            column = jnp.concatenate(parts, axis=0) if ratio > 1 else parts[0]
            bias = up_ref[p]
            column = jnp.concatenate(
                [column] + [bias[k * shape.local : (k + 1) * shape.local] for k in range(ups)],
                axis=1,
            )
            small_ref[p] = column.T

    return call(
        kernel,
        "lay_small_grads",
        (1,),
        [(v, None, None) for v in (late, middle, gate_two, down_bias, up_bias)],
        [((shape.panels, count, shape.local), high, None, None)],
        [pltpu.VMEM((wide_count, rows, 6 * seqs + 1), high)],
        [goes],
    )[0]


def cut_tokens(shape, local):
    def kernel(local_ref, out_ref):
        for n in range(shape.panels):
            out_ref[n, 0] = local_ref[0, :, n * shape.part : (n + 1) * shape.part]

    return call(
        kernel,
        "cut_tokens",
        (shape.seqs,),
        [(local, (1, *local.shape[1:]), lambda s, *_: (s, 0, 0))],
        [
            (
                (shape.panels, shape.seqs, shape.local, shape.part),
                low,
                (shape.panels, 1, shape.local, shape.part),
                lambda s, *_: (0, s, 0, 0),
            )
        ],
    )[0]


def join_tokens(shape, pieces, kind):
    def kernel(pieces_ref, out_ref):
        for n in range(shape.panels):
            out_ref[0, :, n * shape.part : (n + 1) * shape.part] = pieces_ref[n, 0].astype(kind)

    return call(
        kernel,
        "join_tokens",
        (shape.seqs,),
        [
            (
                pieces,
                (shape.panels, 1, shape.local, shape.part),
                lambda s, *_: (0, s, 0, 0),
            )
        ],
        [
            (
                (shape.seqs, shape.local, shape.panels * shape.part),
                kind,
                (1, shape.local, shape.panels * shape.part),
                lambda s, *_: (s, 0, 0),
            )
        ],
    )[0]


def by_panel(shape, rows, kind):
    return (
        (shape.panels, rows, shape.tokens),
        kind,
        (1, rows, shape.tokens),
        lambda n, *_: (n, 0, 0),
    )


def panel_in(array):
    return (array, (1, *array.shape[1:]), lambda n, *_: (n, 0, 0))


def project_qkv(shape, weights, source):
    order = weights.prefetch
    count = len(weights.arrays)

    def kernel(*refs):
        refs, order_refs = refs[len(order) :], refs[: len(order)]
        weight_refs, (source_ref, out_ref, held, sems) = refs[:count], refs[count:]
        panel = weights.panel((*order_refs, *weight_refs), held, sems, pl.program_id(0))
        out_ref[0] = contract(panel[...], source_ref[...], 0, 0).astype(low)

    return call(
        kernel,
        "project_qkv",
        (shape.panels,),
        weights.ins() + [(source, None, None)],
        [by_panel(shape, shape.qkv_rows, low)],
        weights.scratch(),
        prefetch=order,
    )[0]


def head_rows(block, head):
    return block[head * HEAD_DIM : (head + 1) * HEAD_DIM].astype(low)


def attention_forward(shape, qkv, in_clip):
    width = shape.local
    heads = width // HEAD_DIM
    blocks = shape.tokens // BLOCK
    score_scale = 1.0 / math.sqrt(HEAD_DIM)

    def kernel(qkv_ref, row_ref, column_ref, out_ref, probs_ref):
        rows_at = lax.broadcasted_iota(jnp.int32, (BLOCK, BLOCK), 0)
        columns_at = lax.broadcasted_iota(jnp.int32, (BLOCK, BLOCK), 1)
        allowed = (rows_at // FRAMES == columns_at // FRAMES) & (
            ((column_ref[...] > 0) & (row_ref[...] > 0)) | (rows_at == columns_at)
        )
        queries = qkv_ref[0, :width].astype(high)
        key_rows = qkv_ref[0, width : 2 * width].astype(high)
        value_rows = qkv_ref[0, 2 * width : 3 * width].astype(high)
        parts = [jnp.zeros((shape.out_skip, BLOCK), high)]
        for head in range(heads):
            scores = (
                contract(head_rows(key_rows, head), head_rows(queries, head), 0, 0) * score_scale
            )
            scores = jnp.where(allowed, scores, masked_score)
            exp_scores = jnp.exp(scores - jnp.max(scores, axis=0, keepdims=True))
            probs = exp_scores * (1.0 / jnp.sum(exp_scores, axis=0, keepdims=True))
            probs_low = probs.astype(low)
            probs_ref[0, 0, head] = probs_low
            parts.append(contract(head_rows(value_rows, head), probs_low, 1, 0))
        out_ref[0] = jnp.concatenate(parts, axis=0).astype(low)

    return call(
        kernel,
        "attention_forward",
        (blocks, shape.panels),
        [
            (qkv, (1, qkv.shape[1], BLOCK), lambda b, n: (n, 0, b)),
            (in_clip[None, :], (1, BLOCK), lambda b, n: (0, b)),
            (in_clip[:, None], (BLOCK, 1), lambda b, n: (b, 0)),
        ],
        [
            (
                (shape.panels, shape.out_rows, shape.tokens),
                low,
                (1, shape.out_rows, BLOCK),
                lambda b, n: (n, 0, b),
            ),
            (
                (blocks, shape.panels, heads, BLOCK, BLOCK),
                low,
                (1, 1, heads, BLOCK, BLOCK),
                lambda b, n: (b, n, 0, 0, 0),
            ),
        ],
    )


def attention_backward(shape, qkv, probs, grad_attended):
    width = shape.local
    heads = width // HEAD_DIM
    blocks = shape.tokens // BLOCK
    score_scale = 1.0 / math.sqrt(HEAD_DIM)

    def kernel(qkv_ref, probs_ref, grad_ref, out_ref):
        queries = qkv_ref[0, :width].astype(high)
        key_rows = qkv_ref[0, width : 2 * width].astype(high)
        value_rows = qkv_ref[0, 2 * width : 3 * width].astype(high)
        grads = grad_ref[0].astype(high)[shape.out_skip :]
        query_parts, key_parts, value_parts = [], [], []
        for head in range(heads):
            probs_low = probs_ref[0, 0, head]
            grad_head = head_rows(grads, head)
            value_parts.append(contract(grad_head, probs_low, 1, 1))
            grad_probs = contract(head_rows(value_rows, head), grad_head, 0, 0)
            probs = probs_low.astype(high)
            crossed = jnp.sum(grad_probs * probs, axis=0, keepdims=True)
            grad_scores = (probs * (grad_probs - crossed)).astype(low)
            query_parts.append(contract(head_rows(key_rows, head), grad_scores, 1, 0) * score_scale)
            key_parts.append(contract(head_rows(queries, head), grad_scores, 1, 1) * score_scale)
        rest = [jnp.zeros((shape.qkv_rows - 3 * width, BLOCK), high)]
        out_ref[0] = jnp.concatenate(
            query_parts + key_parts + value_parts + rest, axis=0
        ).astype(low)

    return call(
        kernel,
        "attention_backward",
        (blocks, shape.panels),
        [
            (qkv, (1, qkv.shape[1], BLOCK), lambda b, n: (n, 0, b)),
            (probs, (1, 1, heads, BLOCK, BLOCK), lambda b, n: (b, n, 0, 0, 0)),
            (grad_attended, (1, shape.out_rows, BLOCK), lambda b, n: (n, 0, b)),
        ],
        [
            (
                (shape.panels, shape.qkv_rows, shape.tokens),
                low,
                (1, shape.qkv_rows, BLOCK),
                lambda b, n: (n, 0, b),
            )
        ],
    )[0]


def weighted(weights, refs, held, sems, source_ref):
    block = pl.program_id(0)
    count = len(weights.panels)
    weights.start_all(refs, held, sems, block)
    for panel in range(count):
        weights.wait(refs, held, sems, block, panel)
    if weights.wide:
        source = source_ref[...]
        return contract(held[...], source.reshape(-1, source.shape[2]), 1, 0)
    return sum(contract(held[panel], source_ref[panel], 1, 0) for panel in range(count))


def store_sums(shape, sums_ref, rows, slot, block, values):
    lane = lax.broadcasted_iota(jnp.int32, (values[0].shape[0], sums_ref.shape[1]), 1)
    kept = sums_ref[rows]
    for j, value in enumerate(values):
        kept = jnp.where(lane == slot * shape.seqs + block * shape.share + j, value, kept)
    sums_ref[rows] = kept


def row_chunks(shape):
    rows = shape.width // 8
    return [slice(k * rows, (k + 1) * rows) for k in range(8)]


def moments(shape, first, second):
    center = first * (1.0 / shape.width)
    return center, lax.rsqrt(second * (1.0 / shape.width) - center * center + norm_epsilon)


def down_rows(values):
    return jnp.sum(values, axis=0, keepdims=True)


def panel_blocks(shape, array):
    return (array, (*array.shape[:2], shape.block), lambda b, *_: (0, 0, b))


def token_blocks(shape, array):
    return (array, (shape.width, shape.block), lambda b, *_: (0, b))


def sums_out(shape, slots):
    return ((shape.width, slots * shape.seqs), high, None, None)


def total_scratch(shape):
    return [pltpu.VMEM((shape.width, shape.block), high)]


def pieces_out(shape):
    return (
        (shape.panels, shape.seqs, shape.local, shape.part),
        low,
        (shape.panels, shape.share, shape.local, shape.part),
        lambda b, *_: (0, b, 0, 0),
    )


def norm_grads(shape, grad_ref, values_ref, table_ref, slot, block, sums_ref, sums_slot):
    first, second = 0.0, 0.0
    for rows in row_chunks(shape):
        values = values_ref[rows].astype(high)
        first, second = first + down_rows(values), second + down_rows(values * values)
    center, inverse = moments(shape, first, second)
    totals, crossed = 0.0, 0.0
    for rows in row_chunks(shape):
        grad = grad_ref[rows]
        normed = (values_ref[rows].astype(high) - center) * inverse
        store_sums(shape, sums_ref, rows, sums_slot, block, seq_sums(shape, grad))
        store_sums(shape, sums_ref, rows, sums_slot + 1, block, seq_sums(shape, grad * normed))
        hat = grad * (1.0 + spread(shape, table_ref[rows], slot, block))
        totals, crossed = totals + down_rows(hat), crossed + down_rows(hat * normed)

    def third(rows):
        normed = (values_ref[rows].astype(high) - center) * inverse
        hat = grad_ref[rows] * (1.0 + spread(shape, table_ref[rows], slot, block))
        return inverse * (hat - totals * (1.0 / shape.width) - normed * (crossed * (1.0 / shape.width)))

    return third


def project_out(shape, weights, attended, residual, table):
    order = weights.prefetch
    count = len(weights.arrays)

    def kernel(*refs):
        refs, order_refs = refs[len(order) :], refs[: len(order)]
        weight_refs, rest = refs[:count], refs[count:]
        attended_ref, residual_ref, table_ref, middle_ref, branch_ref, input_ref = rest[:6]
        held, sems, total = rest[6:]
        block = pl.program_id(0)
        total[...] = weighted(weights, (*order_refs, *weight_refs), held, sems, attended_ref)
        first, second = 0.0, 0.0
        for rows in row_chunks(shape):
            branch = total[rows]
            middle = residual_ref[rows].astype(high) + branch * spread(
                shape, table_ref[rows], 2, block
            )
            middle_ref[rows] = middle
            branch_ref[rows] = branch.astype(low)
            first, second = first + down_rows(middle), second + down_rows(middle * middle)
        center, inverse = moments(shape, first, second)
        for rows in row_chunks(shape):
            table = table_ref[rows]
            normed = (middle_ref[rows] - center) * inverse
            input_ref[rows] = (
                normed * (1.0 + spread(shape, table, 4, block)) + spread(shape, table, 3, block)
            ).astype(low)

    return call(
        kernel,
        "project_out",
        (shape.blocks,),
        weights.ins()
        + [panel_blocks(shape, attended), token_blocks(shape, residual), (table, None, None)],
        [token_out(shape, high), token_out(shape, low), token_out(shape, low)],
        weights.scratch(True) + total_scratch(shape),
        prefetch=order,
    )


def gelu_and_slope(values):
    root = math.sqrt(2.0 / math.pi)
    square = values * values
    bent = jnp.tanh(root * values * (1.0 + 0.044715 * square))
    half = 0.5 * (1.0 + bent)
    slope = half + 0.5 * values * (1.0 - bent * bent) * (root + 3.0 * 0.044715 * root * square)
    return values * half, slope


def project_up(shape, weights, source, bias):
    order = weights.prefetch
    count = len(weights.arrays)
    inner = weights.stop

    def kernel(*refs):
        refs, order_refs = refs[len(order) :], refs[: len(order)]
        weight_refs, rest = refs[:count], refs[count:]
        source_ref, bias_ref, hidden_ref, slope_ref, held, sems = rest
        panel = weights.panel((*order_refs, *weight_refs), held, sems, pl.program_id(0))
        values = contract(panel[...], source_ref[...], 0, 0) + bias_ref[0]
        hidden, slope = gelu_and_slope(values)
        hidden_ref[0] = hidden.astype(low)
        slope_ref[0] = slope.astype(low)

    return call(
        kernel,
        "project_up",
        (shape.panels,),
        weights.ins() + [(source, None, None), panel_in(bias)],
        [by_panel(shape, inner, low), by_panel(shape, inner, low)],
        weights.scratch(),
        prefetch=order,
    )


def project_down(shape, there, weights, hidden, middle, upstream, table, wide_count):
    order = weights.prefetch
    count = len(weights.arrays)
    bias_at = 6 * shape.seqs
    depth = shape.width // wide_count

    def kernel(at_ref, *refs):
        refs, order_refs = refs[len(order) :], refs[: len(order)]
        weight_refs, rest = refs[:count], refs[count:]
        hidden_ref, middle_ref, upstream_ref, table_ref, out_ref, gate_ref = rest[:6]
        held, sems, total, block_held = rest[6:]
        block = pl.program_id(0)
        total[...] = weighted(weights, (*order_refs, *weight_refs), held, sems, hidden_ref)
        for k in range(wide_count):
            rows = slice(k * depth, (k + 1) * depth)
            table = table_ref[rows]
            mlp = total[rows] + pick(table, bias_at)
            block_held[k] = middle_ref[rows] + mlp * spread(shape, table, 5, block)
            store_sums(
                shape, gate_ref, rows, 0, block, seq_sums(shape, upstream_ref[rows].astype(high) * mlp)
            )
        take_pieces(shape, at_ref, block_held, out_ref)

    return call(
        kernel,
        "project_down",
        (shape.blocks,),
        weights.ins()
        + [panel_blocks(shape, hidden), token_blocks(shape, middle)]
        + [token_blocks(shape, upstream), (table, None, None)],
        [pieces_out(shape), sums_out(shape, 1)],
        weights.scratch(True)
        + [
            *total_scratch(shape),
            pltpu.VMEM((wide_count, depth, shape.block), high),
        ],
        [there, *order],
    )


def grad_outs(shape, columns):
    tall = shape.panels // 2
    half = shape.width // 2
    return [((2, tall, half, columns), low, (2, 1, half, columns), lambda n, *_: (0, n, 0, 0))]


def core_panels(shape, array, core):
    tall = shape.panels // 2
    return (array, (1, *array.shape[1:]), lambda n, *_: (n + core * tall, 0, 0))


def weight_grad(shape, name, source, grad, core):
    columns = grad.shape[1]
    half = shape.width // 2

    def kernel(source_ref, grad_ref, out_ref):
        product = contract(source_ref[...], grad_ref[0], 1, 1).astype(low)
        out_ref[...] = product.reshape(2, 1, half, columns)

    return call(
        kernel,
        name,
        (shape.panels // 2,),
        [(source, None, None), core_panels(shape, grad, core)],
        grad_outs(shape, columns),
    )[0]


def device_weight_grad(shape, name, source, grad, order, wide_count):
    columns = grad.shape[1]
    rows = shape.width // wide_count

    def kernel(order_ref, source_ref, grad_ref, out_ref):
        product = contract(source_ref[...], grad_ref[0], 1, 1).astype(low)
        panel = pl.program_id(0)
        for block in range(wide_count):
            device = order_ref[panel * wide_count + block]
            out_ref[0, device // shape.panels] = product[block * rows : (block + 1) * rows]

    out = call(
        kernel,
        name,
        (shape.panels,),
        [(source, None, None), panel_in(grad)],
        [
            (
                (shape.panels, wide_count, rows, columns),
                low,
                (1, wide_count, rows, columns),
                lambda n, order_ref: (order_ref[n * wide_count] % shape.panels, 0, 0, 0),
            )
        ],
        prefetch=[order],
    )[0]
    return out.reshape(shape.panels * wide_count, rows, columns)


def first_weight_grad(shape, source, grad_qkv, grad_branch, attended, core):
    columns = 4 * shape.local
    begin = shape.out_from
    half = shape.width // 2

    def kernel(source_ref, qkv_ref, branch_ref, attended_ref, out_ref, held):
        held[:, : shape.qkv_rows] = contract(source_ref[...], qkv_ref[0], 1, 1)
        late = contract(branch_ref[...], attended_ref[0], 1, 1)
        both_there = shape.qkv_rows - begin
        if both_there:
            held[:, begin : shape.qkv_rows] += late[:, :both_there]
        held[:, shape.qkv_rows :] = late[:, both_there:]
        out_ref[...] = held[...].astype(low).reshape(2, 1, half, columns)

    return call(
        kernel,
        "first_weight_grad",
        (shape.panels // 2,),
        [
            (source, None, None),
            core_panels(shape, grad_qkv, core),
            (grad_branch, None, None),
            core_panels(shape, attended, core),
        ],
        grad_outs(shape, columns),
        [pltpu.VMEM((shape.width, columns), high)],
    )[0]


def hidden_backward(shape, weights, grad_mlp, slope):
    order = weights.prefetch
    count = len(weights.arrays)
    inner = weights.stop

    def kernel(*refs):
        refs, order_refs = refs[len(order) :], refs[: len(order)]
        weight_refs, rest = refs[:count], refs[count:]
        grad_ref, slope_ref, out_ref, bias_ref, held, sems = rest
        panel = weights.panel((*order_refs, *weight_refs), held, sems, pl.program_id(0))
        values = contract(panel[...], grad_ref[...], 0, 0) * slope_ref[0].astype(high)
        values = values.astype(low)
        out_ref[0] = values
        bias_ref[0] = jnp.sum(values.astype(high), axis=1, keepdims=True)

    return call(
        kernel,
        "hidden_backward",
        (shape.panels,),
        weights.ins() + [(grad_mlp, None, None), panel_in(slope)],
        [
            by_panel(shape, inner, low),
            ((shape.panels, inner, 1), high, (1, inner, 1), lambda n, *_: (n, 0, 0)),
        ],
        weights.scratch(),
        prefetch=order,
    )


def middle_backward(shape, weights, grad_up, middle, upstream, branch, table):
    order = weights.prefetch
    count = len(weights.arrays)

    def kernel(*refs):
        refs, order_refs = refs[len(order) :], refs[: len(order)]
        weight_refs, rest = refs[:count], refs[count:]
        grad_ref, middle_ref, upstream_ref, branch_ref, table_ref = rest[:5]
        out_ref, low_ref, sums_ref, held, sems, total = rest[5:]
        block = pl.program_id(0)
        total[...] = weighted(weights, (*order_refs, *weight_refs), held, sems, grad_ref)
        third = norm_grads(
            shape, total, middle_ref, table_ref, 4, block, sums_ref, 1
        )
        for rows in row_chunks(shape):
            grad = upstream_ref[rows].astype(high) + third(rows)
            store_sums(
                shape, sums_ref, rows, 0, block, seq_sums(shape, grad * branch_ref[rows].astype(high))
            )
            out_ref[rows] = grad
            low_ref[rows] = (grad * spread(shape, table_ref[rows], 2, block)).astype(low)

    return call(
        kernel,
        "middle_backward",
        (shape.blocks,),
        weights.ins()
        + [panel_blocks(shape, grad_up)]
        + [token_blocks(shape, v) for v in (middle, upstream, branch)]
        + [(table, None, None)],
        [token_out(shape, high), token_out(shape, low), sums_out(shape, 3)],
        weights.scratch(True) + total_scratch(shape),
        prefetch=order,
    )


def attended_backward(shape, weights, grad_branch):
    order = weights.prefetch
    count = len(weights.arrays)

    def kernel(*refs):
        refs, order_refs = refs[len(order) :], refs[: len(order)]
        weight_refs, (grad_ref, out_ref, held, sems) = refs[:count], refs[count:]
        panel = weights.panel((*order_refs, *weight_refs), held, sems, pl.program_id(0))
        out_ref[0] = contract(panel[...], grad_ref[...], 0, 0).astype(low)

    return call(
        kernel,
        "attended_backward",
        (shape.panels,),
        weights.ins() + [(grad_branch, None, None)],
        [by_panel(shape, shape.out_rows, low)],
        weights.scratch(),
        prefetch=order,
    )[0]


def input_backward(shape, there, weights, grad_qkv, residual, grad_middle, table, wide_count):
    order = weights.prefetch
    count = len(weights.arrays)
    depth = shape.width // wide_count

    def kernel(at_ref, *refs):
        refs, order_refs = refs[len(order) :], refs[: len(order)]
        weight_refs, rest = refs[:count], refs[count:]
        qkv_ref, residual_ref, middle_ref, table_ref, out_ref, sums_ref = rest[:6]
        held, sems, total, block_held = rest[6:]
        block = pl.program_id(0)
        total[...] = weighted(weights, (*order_refs, *weight_refs), held, sems, qkv_ref)
        third = norm_grads(shape, total, residual_ref, table_ref, 1, block, sums_ref, 0)
        for k in range(wide_count):
            rows = slice(k * depth, (k + 1) * depth)
            block_held[k] = middle_ref[rows] + third(rows)
        take_pieces(shape, at_ref, block_held, out_ref)

    return call(
        kernel,
        "input_backward",
        (shape.blocks,),
        weights.ins()
        + [panel_blocks(shape, grad_qkv)]
        + [token_blocks(shape, v) for v in (residual, grad_middle)]
        + [(table, None, None)],
        [pieces_out(shape), sums_out(shape, 2)],
        weights.scratch(True)
        + [
            *total_scratch(shape),
            pltpu.VMEM((wide_count, depth, shape.block), high),
        ],
        [there, *order],
    )


def on_device(
    tokens,
    ada_weight,
    ada_bias,
    class_table,
    query_weight,
    key_weight,
    value_weight,
    out_weight,
    up_weight,
    up_bias,
    down_weight,
    down_bias,
    cotangent,
    clip_frames,
    time_ids,
    class_ids,
):
    micro_count, seq_count, local_width, seq_tokens = tokens.shape
    class_count, full_width = class_table.shape
    panels, wide_count = lax.axis_size("narrow"), lax.axis_size("wide")
    wide_at = lax.axis_index("wide")
    seqs = micro_count * seq_count
    shape = Shape(seqs, seq_tokens // panels, full_width, panels)
    own_rows = ada_weight.shape[0]
    deep = wide_count // 2
    highest = lax.Precision.HIGHEST
    local_shape = (seqs, local_width, seq_tokens)
    there, came, goes = orders()

    class_hot = (class_ids.reshape(seqs)[:, None] == jnp.arange(class_count)[None, :]).astype(low)
    condition = time_embedding(time_ids.reshape(seqs), full_width) + jnp.einsum(
        "sc,cd->sd", class_hot, class_table, preferred_element_type=high
    )
    sigmoid_cond = jax.nn.sigmoid(condition)
    cond_act = (condition * sigmoid_cond).astype(low)
    silu_slope = sigmoid_cond * (1.0 + condition * (1.0 - sigmoid_cond))
    own_cond = lax.dynamic_slice_in_dim(cond_act, wide_at * own_rows, own_rows, axis=1)
    own_slope = lax.dynamic_slice_in_dim(silu_slope, wide_at * own_rows, own_rows, axis=1)

    first_piece = jnp.concatenate([query_weight, key_weight, value_weight, out_weight.T], axis=1)
    first, down = Gather(first_piece), LateGather(down_weight.T)
    order = device_order()
    mod_part = jnp.einsum("sd,dje->jse", own_cond, ada_weight, preferred_element_type=high)
    mod_part = mod_part.reshape(6 * seqs, local_width)
    hops = [{"side_by": 1}]
    while 2 ** len(hops) <= deep:
        hops.append({"deep_by": 2 ** (len(hops) - 1)})

    first.step()
    token_swap = NarrowSwap(tokens.reshape(local_shape))
    token_same = token_swap.step(0)
    mod_part = mod_part + send(mod_part, **hops[0])
    down.side()
    first.ring, token_same, mod_part, down.line, token_swap.parts = sync(
        first.ring, token_same, mod_part, down.line, token_swap.parts
    )

    first.step()
    token_other = token_swap.step(1)
    mod_part = mod_part + send(mod_part, **hops[1])
    first.ring, token_other, mod_part, down.line = sync(
        first.ring, token_other, mod_part, down.line
    )

    for at in range(2, max(deep - 1, len(hops))):
        if at < len(hops):
            mod_part = mod_part + send(mod_part, **hops[at])
        if at < deep - 1:
            first.step()
        if at == 2:
            token_near, token_far = token_swap.pieces(token_same, token_other)
        if at == max(deep - 1, len(hops)) - 1:
            first.front_side()
            first.front, first.front_got = sync(first.front, first.front_got)
        first.ring, mod_part = sync(first.ring, mod_part)

    first.rear_tall()
    mod_own = (
        mod_part.reshape(6, seqs, local_width) + ada_bias.astype(high)[:, None, :]
    ).reshape(6 * seqs, local_width)
    small = gather_narrow(
        jnp.concatenate(
            [
                mod_own,
                down_bias.astype(high)[None, :],
                up_bias.astype(high).reshape(-1, local_width),
            ]
        )
    )
    first.rear, first.rear_got, first.front, first.front_got, token_far, small = sync(
        first.rear, first.rear_got, first.front, first.front_got, token_far, small
    )

    first.second()
    first.core(0, 2)
    up_full = lax.all_gather(after(up_weight, small), both, axis=0, tiled=False)
    table, up_bias_full = lay_small(shape, came, small, wide_count)
    token_parts = token_near + [token_far[k : k + 1] for k in range(panels // 2)]
    frame_at = jnp.arange(shape.part) % FRAMES
    in_clip = (frame_at[None, :] < clip_frames.reshape(seqs)[:, None]).astype(jnp.int32).reshape(-1)
    residual, input_one = prepare_tokens(shape, came, token_parts, table, wide_count)
    first.arrays, input_one, down.line = sync(first.arrays, input_one, down.line)

    first.core(*[k for k in range(len(first.arrays)) if k not in (0, 2)])
    qkv_weights = Weights(first.result(), 0, shape.qkv_rows)
    out_weights = Weights(first.result(), shape.out_from)
    down.along_tall()
    upstream_cut = cut_tokens(shape, after(cotangent.reshape(local_shape), input_one))
    upstream_parts = swap_narrow(upstream_cut)
    qkv = project_qkv(shape, qkv_weights, after(input_one, upstream_cut))
    qkv, down.plane = sync(qkv, down.plane)

    down.step()
    attended, probs = attention_forward(shape, qkv, in_clip)
    (attended,) = sync(attended)

    middle, branch, input_two = project_out(shape, out_weights, attended, residual, table)
    middle, input_two, down.ring, upstream_parts = sync(
        middle, input_two, down.ring, upstream_parts
    )

    upstream, grad_mlp, down_bias_part = prepare_upstream(
        shape, there, upstream_parts, table, wide_count
    )
    down.step()
    down.core(0, 1)
    up_all = GatheredWeights(up_full, order, panels)
    hidden, slope = project_up(shape, up_all, after(input_two, grad_mlp), up_bias_full)
    hidden, slope, down.cores, down.ring = sync(hidden, slope, down.cores, down.ring)

    for k in range(3, deep):
        down.step()
    down.core(*range(2, deep - 1))
    down_grads = device_weight_grad(
        shape, "down_weight_grad", grad_mlp, hidden, order, wide_count
    )
    down_grad = lax.psum_scatter(
        down_grads, ("narrow", "wide"), scatter_dimension=0, tiled=False
    ).astype(high)
    down_grads, down.ring = sync(down_grads, down.ring)
    down.core(deep - 1)
    down_all = Weights(down.result())
    output_parts, gate_two_part = project_down(
        shape, there, down_all, after(hidden, down_grads), middle, upstream, table, wide_count
    )
    output_parts, gate_two_part = sync(output_parts, gate_two_part)

    output_got = swap_narrow(output_parts)
    grad_up, up_bias_part = hidden_backward(
        shape, down_all, after(grad_mlp, gate_two_part), slope
    )
    other = weight_grad(shape, "up_weight_grad", input_two, grad_up, 1)
    other, output_got = sync(other, output_got)

    up_sum = GradSum(other)
    near = weight_grad(shape, "up_weight_grad", after(input_two, other), grad_up, 0)
    near, up_sum.got = sync(near, up_sum.got)
    up_sum.near(near)
    half = deep // 2
    up_parts = up_sum.split(half)
    sums = up_parts[0].sums("y")
    up_parts[0].along("y", sums)
    grad_middle, grad_branch, middle_sums = middle_backward(
        shape, up_all, after(grad_up, near, *sums), middle, upstream, branch, table
    )
    *_, grad_branch = sync(*up_parts, grad_branch)

    tall_sums, side_sums = up_parts[1].sums("y"), up_parts[0].sums("x")
    up_parts[1].along("y", tall_sums)
    up_parts[0].along("x", side_sums)
    grad_attended = attended_backward(
        shape, out_weights, after(grad_branch, *tall_sums, *side_sums)
    )
    grad_qkv = attention_backward(shape, qkv, probs, grad_attended)
    *_, grad_qkv = sync(*up_parts, grad_qkv)

    side_sums = up_parts[1].sums("x")
    up_parts[1].along("x", side_sums)
    grad_qkv = after(grad_qkv, *side_sums)
    other = first_weight_grad(shape, input_one, grad_qkv, grad_branch, attended, 1)
    *_, other = sync(up_parts[0], other)

    first_sum = GradSum(other)
    near = first_weight_grad(shape, after(input_one, other), grad_qkv, grad_branch, attended, 0)
    near, first_sum.got, _ = sync(near, first_sum.got, up_parts[1])
    first_sum.near(near)
    first_parts = first_sum.split(half)
    side_sums, tall_sums = first_parts[0].sums("x"), first_parts[1].sums("y")
    first_parts[0].along("x", side_sums)
    first_parts[1].along("y", tall_sums)
    up_sums = deep_sums(up_parts)
    along_deep(up_parts, up_sums)
    input_parts, input_sums = input_backward(
        shape,
        there,
        qkv_weights,
        after(grad_qkv, *side_sums, *tall_sums, *up_sums),
        residual,
        grad_middle,
        table,
        wide_count,
    )
    *_, input_parts, input_sums = sync(*first_parts, up_parts[0], input_parts, input_sums)

    tall_sums, side_sums = first_parts[0].sums("y"), first_parts[1].sums("x")
    first_parts[0].along("y", tall_sums)
    first_parts[1].along("x", side_sums)
    small_grad = lay_small_grads(
        shape,
        goes,
        input_sums,
        middle_sums,
        after(gate_two_part, *side_sums, *tall_sums),
        down_bias_part,
        up_bias_part,
        wide_count,
    )
    small_grad = small_grad.reshape(2, panels // 2, *small_grad.shape[1:])
    small_grad = small_grad[0] + send(small_grad[1], core_by=1)
    by = 1
    while by < deep:
        small_grad = small_grad + send(small_grad, deep_by=by)
        by *= 2
    *_, small_grad = sync(*first_parts, small_grad)
    sums = deep_sums(first_parts)
    first_got = along_deep(first_parts, sums)
    output = join_tokens(shape, after(output_got, small_grad), low)
    small_grad = after(small_grad, *sums)
    small_grad = small_grad + send(small_grad, side_by=1)
    small_grad = after(small_grad, first_got[0], output)
    small_grad = sum(
        [small_grad[0]] + [send(small_grad[k], tall_by=k) for k in range(1, panels // 2)]
    )
    own_mod = small_grad[: 6 * seqs].reshape(6, seqs, local_width)
    down_bias_grad = small_grad[6 * seqs]
    up_bias_grad = small_grad[6 * seqs + 1 :].reshape(-1)
    ada_grad = jnp.einsum("sd,jse->dje", own_cond.astype(high), own_mod, precision=highest)
    ada_bias_grad = jnp.sum(own_mod, axis=1)
    own_mod = after(own_mod, *first_got[1:2])
    cond_local = sum_narrow(
        own_slope * jnp.einsum("jse,dje->sd", own_mod, ada_weight.astype(high), precision=highest)
    )
    input_got = swap_narrow(after(input_parts, cond_local))
    cond_local = after(cond_local, *first_got)
    cond_grad = sum_wide(
        lax.dynamic_update_slice_in_dim(
            jnp.zeros((seqs, full_width), high), cond_local, wide_at * own_rows, axis=1
        )
    )
    input_grad = join_tokens(shape, after(input_got, cond_grad), high)
    up_grad = up_parts[0].total()
    first_grad = first_parts[0].total()
    table_grad = jnp.einsum("sc,sd->cd", class_hot.astype(high), cond_grad, precision=highest)
    return (
        output.reshape(tokens.shape),
        input_grad.reshape(tokens.shape),
        ada_grad,
        ada_bias_grad,
        table_grad,
        first_grad[:, :local_width],
        first_grad[:, local_width : 2 * local_width],
        first_grad[:, 2 * local_width : 3 * local_width],
        first_grad[:, 3 * local_width :].T,
        up_grad,
        up_bias_grad,
        down_grad.T,
        down_bias_grad,
    )


def solution(mesh):
    return jax.shard_map(
        on_device,
        mesh=mesh,
        in_specs=(
            P(None, None, "narrow", "wide"),
            P("wide", None, "narrow"),
            P(None, "narrow"),
            P(),
            P("wide", "narrow"),
            P("wide", "narrow"),
            P("wide", "narrow"),
            P("narrow", "wide"),
            P("wide", "narrow"),
            P("narrow"),
            P("narrow", "wide"),
            P("narrow"),
            P(None, None, "narrow", "wide"),
            P(),
            P(),
            P(),
        ),
        out_specs=(
            P(None, None, "narrow", "wide"),
            P(None, None, "narrow", "wide"),
            P("wide", None, "narrow"),
            P(None, "narrow"),
            P(),
            P("wide", "narrow"),
            P("wide", "narrow"),
            P("wide", "narrow"),
            P("narrow", "wide"),
            P("wide", "narrow"),
            P("narrow"),
            P("narrow", "wide"),
            P("narrow"),
        ),
        check_vma=False,
    )
```

```python
import functools
import math

import jax
import jax.numpy as jnp
from jax import lax
from jax.experimental import pallas as pl
from jax.experimental.pallas import tpu as pltpu
from jax.sharding import PartitionSpec as P

HEAD_DIM = 72
FRAMES = 16
BLOCK = 128
MIB = 1024 * 1024
FORWARD_SHARE = 8
BACKWARD_SHARE = 4
COSTS = {
    "project_qkv": 15,
    "attention_forward": 24,
    "project_out": 17,
    "project_up": 28,
    "project_down": 25,
    "down_weight_grad": 10,
    "up_weight_grad": 10,
    "first_weight_grad": 12,
    "hidden_backward": 21,
    "middle_backward": 30,
    "attended_backward": 9,
    "attention_backward": 33,
    "input_backward": 25,
}
COST_SCALE = 1e8

norm_epsilon = 1e-06
masked_score = -1e30
both = ("wide", "narrow")
low = jnp.bfloat16
high = jnp.float32


def time_embedding(time_ids, full_width):
    half_width = full_width // 2
    frequency = jnp.exp(-math.log(10000.0) * jnp.arange(half_width, dtype=jnp.float32) / half_width)
    angles = time_ids.astype(jnp.float32)[..., None] * frequency
    return jnp.concatenate([jnp.cos(angles), jnp.sin(angles)], axis=-1)


def place():
    deep, tall = lax.axis_size("wide") // 2, lax.axis_size("narrow") // 2
    wide_at, narrow_at = lax.axis_index("wide"), lax.axis_index("narrow")
    return deep, tall, wide_at // 2, wide_at % 2, narrow_at // 2, narrow_at % 2


def send(value, deep_by=0, side_by=0, tall_by=0, core_by=0):
    deep, tall = lax.axis_size("wide") // 2, lax.axis_size("narrow") // 2
    pairs = []
    for z in range(deep):
        for x in range(2):
            for y in range(tall):
                for c in range(2):
                    source = ((z * 2 + x) * tall + y) * 2 + c
                    target = (
                        ((z + deep_by) % deep * 2 + (x + side_by) % 2) * tall + (y + tall_by) % tall
                    ) * 2 + (c + core_by) % 2
                    pairs.append((source, target))
    return lax.ppermute(value, both, pairs)


def after(value, *earlier):
    return lax.optimization_barrier((value, earlier))[0]


def sync(*values):
    arrays = []
    for value in values:
        if isinstance(value, GradSum):
            arrays += [array for array, _ in value.terms]
        elif isinstance(value, (list, tuple)):
            arrays += value
        else:
            arrays.append(value)
    arrays = iter(lax.optimization_barrier(tuple(arrays)))
    results = []
    for value in values:
        if isinstance(value, GradSum):
            value.terms = [(next(arrays), cuts) for _, cuts in value.terms]
            results.append(value)
        elif isinstance(value, (list, tuple)):
            results.append([next(arrays) for _ in value])
        else:
            results.append(next(arrays))
    return results


class Gather:
    def __init__(self, piece):
        self.deep = lax.axis_size("wide") // 2
        self.tall = lax.axis_size("narrow") // 2
        self.ring = [piece]
        self.rows = piece.shape[0]

    def step(self):
        self.ring.append(send(self.ring[-1], deep_by=1))

    def front_side(self):
        self.front = jnp.concatenate(self.ring[: self.deep // 2], axis=0)
        self.front_got = [send(self.front, side_by=1)]

    def rear_tall(self):
        self.rear = jnp.concatenate(self.ring[self.deep // 2 :], axis=0)
        self.rear_got = [send(self.rear, tall_by=k) for k in range(1, self.tall)]

    def second(self):
        self.front = jnp.concatenate([self.front] + self.front_got, axis=0)
        self.rear = jnp.concatenate([self.rear] + self.rear_got, axis=0)
        self.arrays = [self.rear, send(self.rear, side_by=1), self.front]
        self.arrays += [send(self.front, tall_by=k) for k in range(1, self.tall)]
        self.cores = [None] * len(self.arrays)

    def core(self, *at):
        for k in at:
            self.cores[k] = send(self.arrays[k], core_by=1)

    def result(self):
        count = len(self.arrays)
        near = self.deep // 2 * self.rows
        far = self.deep * self.rows - near
        panels = []
        for c in range(2):
            for y in range(self.tall):
                panels.append(
                    [
                        (c * count + 2 + y, (), 0, 0, near),
                        (c * count, (), y * far, near, far),
                        (c * count + 2 + y, (), near, near + far, near),
                        (c * count + 1, (), y * far, 2 * near + far, far),
                    ]
                )
        return self.arrays + self.cores, panels


class LateGather:
    def __init__(self, piece):
        self.deep = lax.axis_size("wide") // 2
        self.tall = lax.axis_size("narrow") // 2
        self.piece = piece
        self.cores = []

    def side(self):
        self.line = [self.piece, send(self.piece, side_by=1)]

    def along_tall(self):
        line = jnp.stack(self.line)
        self.plane = [line] + [send(line, tall_by=k) for k in range(1, self.tall)]

    def step(self):
        if not hasattr(self, "ring"):
            self.ring = [jnp.stack(self.plane)]
        self.ring.append(send(self.ring[-1], deep_by=1))

    def core(self, *at):
        self.cores += [send(self.ring[k], core_by=1) for k in at]

    def result(self):
        tall, deep, rows = self.tall, self.deep, self.piece.shape[0]
        arrays = self.ring + self.cores
        if rows % 16:
            whole = [
                jnp.concatenate([arrays[c * deep + k][y, x] for x in range(2) for k in range(deep)])
                for c in range(2)
                for y in range(tall)
            ]
            return whole, [[(at, (), 0, 0, 2 * deep * rows)] for at in range(2 * tall)]
        panels = [
            [
                (c * deep + k, (y, x), 0, (x * deep + k) * rows, rows)
                for x in range(2)
                for k in range(deep)
            ]
            for c in range(2)
            for y in range(tall)
        ]
        return arrays, panels


def device_order():
    deep, tall, z, x, y, c = place()
    order = []
    for core in range(2):
        for k in range(tall):
            n = (y - k) % tall * 2 + (c - core) % 2
            for side in range(2):
                for far in range(deep):
                    w = (z - far) % deep * 2 + (x - side) % 2
                    order.append(w * 2 * tall + n)
    return jnp.stack(order).astype(jnp.int32)


class GradSum:
    def __init__(self, other):
        self.sizes = {"x": 2, "y": lax.axis_size("narrow") // 2, "z": lax.axis_size("wide") // 2}
        self.got = send(other, core_by=-1)

    def near(self, near):
        _, tall, rows, columns = near.shape
        deep = self.sizes["z"]
        shape = (2, tall, deep, rows // deep, columns)
        self.terms = [(near.reshape(shape), ()), (self.got.reshape(shape), ())]
        self.axes = "xyz"

    def copy(self, cuts):
        one = GradSum.__new__(GradSum)
        one.sizes, one.axes = dict(self.sizes), self.axes
        one.terms = [(array, earlier + cuts) for array, earlier in self.terms]
        return one

    def split(self, *ends):
        parts = []
        for start, end in zip((0, *ends), (*ends, self.sizes["z"])):
            part = self.copy((self.at("z", slice(start, end)),))
            part.sizes["z"] = end - start
            parts.append(part)
        return parts

    def at(self, axis, k):
        return (slice(None),) * self.axes.index(axis) + (k,)

    def hold(self, *earlier):
        self.terms = [(after(array, *earlier), cuts) for array, cuts in self.terms]
        return self

    def total(self, *cuts):
        total = 0.0
        for array, earlier in self.terms:
            for one in earlier + cuts:
                array = array[one]
            total = total + array.astype(high)
        return total

    def sums(self, axis):
        return [self.total(self.at(axis, k)).astype(low) for k in range(1, self.sizes[axis])]

    def along(self, axis, sums, *earlier):
        by = {"x": "side_by", "y": "tall_by", "z": "deep_by"}[axis]
        gots = [send(after(v, *earlier), **{by: -k}) for k, v in enumerate(sums, 1)]
        self.receive(axis, gots)
        return gots

    def receive(self, axis, gots):
        own = self.at(axis, 0)
        self.terms = [(array, cuts + (own,)) for array, cuts in self.terms] + [(v, ()) for v in gots]
        self.axes = self.axes.replace(axis, "")


def deep_sums(parts):
    return [
        part.total(part.at("z", k)).astype(low) for part in parts for k in range(part.sizes["z"])
    ][1:]


def along_deep(parts, sums, *earlier):
    first = parts[0]
    gots = [send(after(v, *earlier), deep_by=-k) for k, v in enumerate(sums, 1)]
    first.receive("z", gots)
    return gots


def swap_narrow(parts):
    return lax.all_to_all(parts, "narrow", 0, 0, tiled=True)


class NarrowSwap:
    def __init__(self, parts):
        self.tall = lax.axis_size("narrow") // 2
        self.parts = parts
        _, _, _, _, self.y, self.c = place()
        self.own = [self.pick(0, core) for core in range(2)]

    def pick(self, k, core):
        target = (self.y + k) % self.tall * 2 + (self.c + core) % 2
        part = self.parts.shape[2] // (2 * self.tall)
        return lax.dynamic_slice_in_dim(self.parts, target * part, part, axis=2)[None]

    def step(self, core):
        return [send(self.pick(k, core), tall_by=k) for k in range(1, self.tall)]

    def pieces(self, same, other):
        other = send(jnp.concatenate([self.own[1]] + other, axis=0), core_by=1)
        return [self.own[0]] + same, other


def orders():
    deep, tall, z, x, y, c = place()
    wide_count, narrow_count = 2 * deep, 2 * tall
    ratio = wide_count // narrow_count

    def stands(n, h):
        w = n * ratio + h
        return (x - w % 2) % 2 * deep + (z - w // 2) % deep

    there = [stands(n, h) for n in range(narrow_count) for h in range(ratio)]
    came, goes = [], []
    for core_by in range(2):
        for tall_by in range(tall):
            source = (y - tall_by) % tall * 2 + (c - core_by) % 2
            target = (y + tall_by) % tall * 2 + (c + core_by) % 2
            came += [stands(source, h) for h in range(ratio)]
            goes += [stands(target, h) for h in range(ratio)]
    return [jnp.stack(v).astype(jnp.int32) for v in (there, came, goes)]


def sum_wide(value):
    deep = lax.axis_size("wide") // 2
    value = value + send(value, side_by=1)
    step = 1
    while step < deep:
        value = value + send(value, deep_by=step)
        step *= 2
    return value


def sum_narrow(value):
    tall = lax.axis_size("narrow") // 2
    value = value + send(value, core_by=1)
    step = 1
    while step < tall:
        value = value + send(value, tall_by=step)
        step *= 2
    return value


def gather_narrow(value):
    tall = lax.axis_size("narrow") // 2
    own = jnp.stack([value] + [send(value, tall_by=k) for k in range(1, tall)])
    return jnp.concatenate([own, send(own, core_by=1)])


def scatter_narrow(value):
    tall = lax.axis_size("narrow") // 2
    value = value.reshape(2, tall, *value.shape[1:])
    total = value[0] + send(value[1], core_by=1)
    return sum([total[0]] + [send(total[k], tall_by=k) for k in range(1, tall)])


def contract(left, right, left_dim, right_dim):
    return lax.dot_general(
        left, right, (((left_dim,), (right_dim,)), ((), ())), preferred_element_type=jnp.float32
    )


def call(kernel, name, grid, ins, outs, scratch=(), prefetch=(), vmem=60):
    in_specs = []
    for array, block, index in ins:
        if block == "any":
            in_specs.append(pl.BlockSpec(memory_space=pl.ANY))
        elif block is None:
            in_specs.append(pl.BlockSpec(array.shape, lambda *_, r=array.ndim: (0,) * r))
        else:
            in_specs.append(pl.BlockSpec(block, index))
    out_specs = []
    for shape, _, block, index in outs:
        if block is None:
            out_specs.append(pl.BlockSpec(shape, lambda *_, r=len(shape): (0,) * r))
        else:
            out_specs.append(pl.BlockSpec(block, index))
    return pl.pallas_call(
        kernel,
        grid_spec=pltpu.PrefetchScalarGridSpec(
            num_scalar_prefetch=len(prefetch),
            grid=grid,
            in_specs=in_specs,
            out_specs=out_specs,
            scratch_shapes=list(scratch),
        ),
        out_shape=[jax.ShapeDtypeStruct(shape, kind) for shape, kind, _, _ in outs],
        compiler_params=pltpu.CompilerParams(vmem_limit_bytes=vmem * MIB),
        cost_estimate=pl.CostEstimate(
            flops=int(COSTS.get(name, 4) * COST_SCALE), bytes_accessed=0, transcendentals=0
        ),
        name=name,
    )(*prefetch, *[array for array, _, _ in ins])


class Weights:
    def __init__(self, gathered, start=0, stop=None):
        self.arrays, self.panels = gathered
        self.columns = self.arrays[0].shape[-1]
        self.start, self.stop = start, self.columns if stop is None else stop
        self.rows = sum(size for *_, size in self.panels[0])
        self.prefetch = []

    def ins(self):
        return [(array, "any", None) for array in self.arrays]

    def scratch(self, wide=False):
        count, columns = len(self.panels), self.stop - self.start
        self.wide = wide and columns % BLOCK == 0
        return [
            pltpu.VMEM(
                (self.rows, count * columns) if self.wide else (count, self.rows, columns), low
            ),
            pltpu.SemaphoreType.DMA((count, len(self.panels[0]))),
        ]

    def source(self, refs, panel, piece):
        array, lead, begin, row, size = self.panels[panel][piece]
        source = refs[array].at[(*lead, pl.ds(begin, size), slice(self.start, self.stop))]
        return source, row, size

    def copies(self, refs, held, sems, panel):
        copies = []
        columns = self.stop - self.start
        for piece in range(len(self.panels[0])):
            source, row, size = self.source(refs, panel, piece)
            if self.wide:
                target = held.at[pl.ds(row, size), pl.ds(panel * columns, columns)]
            else:
                target = held.at[panel, pl.ds(row, size)]
            copies.append(pltpu.make_async_copy(source, target, sems.at[panel, piece]))
        return copies

    def start_all(self, refs, held, sems, at):
        @pl.when(at == 0)
        def _():
            for panel in range(len(self.panels)):
                for copy in self.copies(refs, held, sems, panel):
                    copy.start()

    def wait(self, refs, held, sems, at, panel, step=0):
        @pl.when(at == step)
        def _():
            for copy in self.copies(refs, held, sems, panel):
                copy.wait()

    def panel(self, refs, held, sems, at):
        self.start_all(refs, held, sems, at)
        for panel in range(len(self.panels)):
            self.wait(refs, held, sems, at, panel, panel)
        return held.at[at]


class GatheredWeights(Weights):
    def __init__(self, gathered, order, panel_count):
        devices, rows, columns = gathered.shape
        blocks = devices // panel_count
        if rows % 16:
            whole = jnp.take(gathered, order, axis=0).reshape(panel_count, blocks * rows, columns)
            super().__init__(([whole], [[(0, (p,), 0, 0, blocks * rows)] for p in range(panel_count)]))
            return
        panels = [
            [(p * blocks + b, (), 0, b * rows, rows) for b in range(blocks)]
            for p in range(panel_count)
        ]
        super().__init__(([gathered], panels))
        self.prefetch = [order]

    def source(self, refs, panel, piece):
        if not self.prefetch:
            return super().source(refs, panel, piece)
        at, _, _, row, size = self.panels[panel][piece]
        return refs[1].at[refs[0][at]], row, size


class Shape:
    def __init__(self, seqs, part, width, panels):
        self.seqs, self.part, self.width, self.panels = seqs, part, width, panels
        self.tokens = seqs * part
        self.block = part if part % BLOCK == 0 else self.tokens
        self.blocks = self.tokens // self.block
        self.share = self.block // part
        local = width // panels
        self.local = local
        self.qkv_rows = min(-(-3 * local // BLOCK) * BLOCK, 4 * local)
        self.out_from = 3 * local // BLOCK * BLOCK
        self.out_rows = 4 * local - self.out_from
        self.out_skip = 3 * local - self.out_from


def pick(table, at):
    lane = lax.broadcasted_iota(jnp.int32, table.shape, 1)
    return jnp.sum(jnp.where(lane == at, table, 0.0), axis=1, keepdims=True)


def spread(shape, table, slot, block):
    picked = [pick(table, slot * shape.seqs + block * shape.share + j) for j in range(shape.share)]
    if shape.share == 1:
        return picked[0]
    return jnp.concatenate(
        [jnp.broadcast_to(one, (one.shape[0], shape.part)) for one in picked], axis=1
    )


def seq_sums(shape, values):
    return [
        jnp.sum(values[:, j * shape.part : (j + 1) * shape.part], axis=1, keepdims=True)
        for j in range(shape.share)
    ]


def normed_rows(values):
    width = values.shape[0]
    center = jnp.sum(values, axis=0, keepdims=True) * (1.0 / width)
    shifted = values - center
    variance = jnp.sum(shifted * shifted, axis=0, keepdims=True) * (1.0 / width)
    inverse = lax.rsqrt(variance + norm_epsilon)
    return shifted * inverse, inverse


def norm_backward(grad_hat, normed, inverse):
    width = normed.shape[0]
    totals = jnp.sum(grad_hat, axis=0, keepdims=True) * (1.0 / width)
    crossed = jnp.sum(grad_hat * normed, axis=0, keepdims=True) * (1.0 / width)
    return inverse * (grad_hat - totals - normed * crossed)


def put_pieces(shape, at_ref, piece_refs, held):
    rows = held.shape[1]
    ratio = shape.local // rows
    for n in range(shape.panels):
        for h in range(ratio):
            for j in range(shape.share):
                ref, lead = (piece_refs[0], n) if len(piece_refs) == 1 else (piece_refs[n], 0)
                held[at_ref[n * ratio + h], :, j * shape.part : (j + 1) * shape.part] = ref[
                    lead, j, h * rows : (h + 1) * rows
                ].astype(high)


def take_pieces(shape, at_ref, held, pieces_ref):
    rows = held.shape[1]
    ratio = shape.local // rows
    for n in range(shape.panels):
        for h in range(ratio):
            for j in range(shape.share):
                pieces_ref[n, j, h * rows : (h + 1) * rows, :] = held[
                    at_ref[n * ratio + h], :, j * shape.part : (j + 1) * shape.part
                ].astype(pieces_ref.dtype)


def pieces_in(shape, pieces):
    if isinstance(pieces, list):
        block = (1, shape.share, shape.local, shape.part)
        return [(piece, block, lambda b, *_: (0, b, 0, 0)) for piece in pieces]
    return [pieces_by_device(shape, pieces)]


def pieces_by_device(shape, pieces):
    return (
        pieces,
        (shape.panels, shape.share, shape.local, shape.part),
        lambda b, *_: (0, b, 0, 0),
    )


def token_out(shape, kind):
    return (
        (shape.width, shape.tokens),
        kind,
        (shape.width, shape.block),
        lambda b, *_: (0, b),
    )


def prepare_tokens(shape, there, pieces, table, wide_count):
    def kernel(at_ref, *refs):
        *piece_refs, table_ref, whole_ref, input_ref, held = refs
        block = pl.program_id(0)
        put_pieces(shape, at_ref, piece_refs, held)
        values = held[...].reshape(shape.width, shape.block)
        normed, _ = normed_rows(values)
        table = table_ref[...]
        whole_ref[...] = values.astype(low)
        input_ref[...] = (
            normed * (1.0 + spread(shape, table, 1, block)) + spread(shape, table, 0, block)
        ).astype(low)

    return call(
        kernel,
        "prepare_tokens",
        (shape.blocks,),
        pieces_in(shape, pieces) + [(table, None, None)],
        [token_out(shape, low), token_out(shape, low)],
        [pltpu.VMEM((wide_count, shape.width // wide_count, shape.block), high)],
        [there],
    )


def prepare_upstream(shape, there, pieces, table, wide_count):
    def kernel(at_ref, pieces_ref, table_ref, whole_ref, grad_ref, bias_ref, held):
        block = pl.program_id(0)
        put_pieces(shape, at_ref, [pieces_ref], held)
        values = held[...].reshape(shape.width, shape.block)
        whole_ref[...] = values.astype(low)
        grad_low = (values * spread(shape, table_ref[...], 5, block)).astype(low)
        grad_ref[...] = grad_low
        total = jnp.sum(grad_low.astype(high), axis=1, keepdims=True)

        @pl.when(block == 0)
        def _():
            bias_ref[...] = total

        @pl.when(block > 0)
        def _():
            bias_ref[...] += total

    return call(
        kernel,
        "prepare_upstream",
        (shape.blocks,),
        pieces_in(shape, pieces) + [(table, None, None)],
        [token_out(shape, low), token_out(shape, low), ((shape.width, 1), high, None, None)],
        [pltpu.VMEM((wide_count, shape.width // wide_count, shape.block), high)],
        [there],
    )


def lay_small(shape, came, small, wide_count):
    rows = shape.width // wide_count
    ratio = shape.local // rows
    first = 6 * shape.seqs + 1
    count = small.shape[1]
    ups = count - first

    def kernel(at_ref, small_ref, table_ref, bias_ref, held):
        for p in range(shape.panels):
            turned = small_ref[p].T
            for h in range(ratio):
                held[at_ref[p * ratio + h]] = turned[h * rows : (h + 1) * rows]
            bias_ref[p] = jnp.concatenate(
                [turned[:, first + k : first + k + 1] for k in range(ups)], axis=0
            )
        table_ref[...] = held[...].reshape(shape.width, count)

    return call(
        kernel,
        "lay_small",
        (1,),
        [(small, None, None)],
        [
            ((shape.width, count), high, None, None),
            ((shape.panels, ups * shape.local, 1), high, None, None),
        ],
        [pltpu.VMEM((wide_count, rows, count), high)],
        [came],
    )


def lay_small_grads(shape, goes, late, middle, gate_two, down_bias, up_bias, wide_count):
    rows = shape.width // wide_count
    ratio = shape.local // rows
    seqs = shape.seqs
    ups = up_bias.shape[1] // shape.local
    count = 6 * seqs + 1 + ups

    def kernel(at_ref, late_ref, middle_ref, gate_ref, down_ref, up_ref, small_ref, held):
        table = jnp.concatenate(
            [late_ref[...], middle_ref[...], gate_ref[...], down_ref[...]], axis=1
        )
        held[...] = table.reshape(wide_count, rows, 6 * seqs + 1)
        for p in range(shape.panels):
            parts = [held[at_ref[p * ratio + h]] for h in range(ratio)]
            column = jnp.concatenate(parts, axis=0) if ratio > 1 else parts[0]
            bias = up_ref[p]
            column = jnp.concatenate(
                [column] + [bias[k * shape.local : (k + 1) * shape.local] for k in range(ups)],
                axis=1,
            )
            small_ref[p] = column.T

    return call(
        kernel,
        "lay_small_grads",
        (1,),
        [(v, None, None) for v in (late, middle, gate_two, down_bias, up_bias)],
        [((shape.panels, count, shape.local), high, None, None)],
        [pltpu.VMEM((wide_count, rows, 6 * seqs + 1), high)],
        [goes],
    )[0]


def cut_tokens(shape, local):
    def kernel(local_ref, out_ref):
        for n in range(shape.panels):
            out_ref[n, 0] = local_ref[0, :, n * shape.part : (n + 1) * shape.part]

    return call(
        kernel,
        "cut_tokens",
        (shape.seqs,),
        [(local, (1, *local.shape[1:]), lambda s, *_: (s, 0, 0))],
        [
            (
                (shape.panels, shape.seqs, shape.local, shape.part),
                low,
                (shape.panels, 1, shape.local, shape.part),
                lambda s, *_: (0, s, 0, 0),
            )
        ],
    )[0]


def join_tokens(shape, pieces, kind):
    def kernel(pieces_ref, out_ref):
        for n in range(shape.panels):
            out_ref[0, :, n * shape.part : (n + 1) * shape.part] = pieces_ref[n, 0].astype(kind)

    return call(
        kernel,
        "join_tokens",
        (shape.seqs,),
        [
            (
                pieces,
                (shape.panels, 1, shape.local, shape.part),
                lambda s, *_: (0, s, 0, 0),
            )
        ],
        [
            (
                (shape.seqs, shape.local, shape.panels * shape.part),
                kind,
                (1, shape.local, shape.panels * shape.part),
                lambda s, *_: (s, 0, 0),
            )
        ],
    )[0]


def by_panel(shape, rows, kind):
    return (
        (shape.panels, rows, shape.tokens),
        kind,
        (1, rows, shape.tokens),
        lambda n, *_: (n, 0, 0),
    )


def panel_in(array):
    return (array, (1, *array.shape[1:]), lambda n, *_: (n, 0, 0))


def project_qkv(shape, weights, source):
    order = weights.prefetch
    count = len(weights.arrays)

    def kernel(*refs):
        refs, order_refs = refs[len(order) :], refs[: len(order)]
        weight_refs, (source_ref, out_ref, held, sems) = refs[:count], refs[count:]
        panel = weights.panel((*order_refs, *weight_refs), held, sems, pl.program_id(0))
        out_ref[0] = contract(panel[...], source_ref[...], 0, 0).astype(low)

    return call(
        kernel,
        "project_qkv",
        (shape.panels,),
        weights.ins() + [(source, None, None)],
        [by_panel(shape, shape.qkv_rows, low)],
        weights.scratch(),
        prefetch=order,
    )[0]


def head_rows(block, head):
    return block[head * HEAD_DIM : (head + 1) * HEAD_DIM].astype(low)


def attention_forward(shape, qkv, in_clip):
    width = shape.local
    heads = width // HEAD_DIM
    blocks = shape.tokens // BLOCK
    score_scale = 1.0 / math.sqrt(HEAD_DIM)

    share = math.gcd(blocks, FORWARD_SHARE)

    def kernel(qkv_ref, row_ref, column_ref, out_ref, probs_ref):
        for sub in range(share):
            one_block(qkv_ref, row_ref, column_ref, out_ref, probs_ref, sub)

    def one_block(qkv_ref, row_ref, column_ref, out_ref, probs_ref, sub):
        at = slice(sub * BLOCK, (sub + 1) * BLOCK)
        rows_at = lax.broadcasted_iota(jnp.int32, (BLOCK, BLOCK), 0)
        columns_at = lax.broadcasted_iota(jnp.int32, (BLOCK, BLOCK), 1)
        allowed = (rows_at // FRAMES == columns_at // FRAMES) & (
            ((column_ref[at] > 0) & (row_ref[:, at] > 0)) | (rows_at == columns_at)
        )
        queries = qkv_ref[0, :width, at].astype(high)
        key_rows = qkv_ref[0, width : 2 * width, at].astype(high)
        value_rows = qkv_ref[0, 2 * width : 3 * width, at].astype(high)
        parts = [jnp.zeros((shape.out_skip, BLOCK), high)]
        for head in range(heads):
            scores = (
                contract(head_rows(key_rows, head), head_rows(queries, head), 0, 0) * score_scale
            )
            scores = jnp.where(allowed, scores, masked_score)
            exp_scores = jnp.exp(scores - jnp.max(scores, axis=0, keepdims=True))
            probs = exp_scores * (1.0 / jnp.sum(exp_scores, axis=0, keepdims=True))
            probs_low = probs.astype(low)
            probs_ref[sub, 0, head] = probs_low
            parts.append(contract(head_rows(value_rows, head), probs_low, 1, 0))
        out_ref[0, :, at] = jnp.concatenate(parts, axis=0).astype(low)

    return call(
        kernel,
        "attention_forward",
        (blocks // share, shape.panels),
        [
            (qkv, (1, qkv.shape[1], share * BLOCK), lambda b, n: (n, 0, b)),
            (in_clip[None, :], (1, share * BLOCK), lambda b, n: (0, b)),
            (in_clip[:, None], (share * BLOCK, 1), lambda b, n: (b, 0)),
        ],
        [
            (
                (shape.panels, shape.out_rows, shape.tokens),
                low,
                (1, shape.out_rows, share * BLOCK),
                lambda b, n: (n, 0, b),
            ),
            (
                (blocks, shape.panels, heads, BLOCK, BLOCK),
                low,
                (share, 1, heads, BLOCK, BLOCK),
                lambda b, n: (b, n, 0, 0, 0),
            ),
        ],
    )


def attention_backward(shape, qkv, probs, grad_attended):
    width = shape.local
    heads = width // HEAD_DIM
    blocks = shape.tokens // BLOCK
    score_scale = 1.0 / math.sqrt(HEAD_DIM)

    share = math.gcd(blocks, BACKWARD_SHARE)

    def kernel(qkv_ref, probs_ref, grad_ref, out_ref):
        for sub in range(share):
            one_block(qkv_ref, probs_ref, grad_ref, out_ref, sub)

    def one_block(qkv_ref, probs_ref, grad_ref, out_ref, sub):
        at = slice(sub * BLOCK, (sub + 1) * BLOCK)
        queries = qkv_ref[0, :width, at].astype(high)
        key_rows = qkv_ref[0, width : 2 * width, at].astype(high)
        value_rows = qkv_ref[0, 2 * width : 3 * width, at].astype(high)
        grads = grad_ref[0, :, at].astype(high)[shape.out_skip :]
        query_parts, key_parts, value_parts = [], [], []
        for head in range(heads):
            probs_low = probs_ref[sub, 0, head]
            grad_head = head_rows(grads, head)
            value_parts.append(contract(grad_head, probs_low, 1, 1))
            grad_probs = contract(head_rows(value_rows, head), grad_head, 0, 0)
            probs = probs_low.astype(high)
            crossed = jnp.sum(grad_probs * probs, axis=0, keepdims=True)
            grad_scores = (probs * (grad_probs - crossed)).astype(low)
            query_parts.append(contract(head_rows(key_rows, head), grad_scores, 1, 0) * score_scale)
            key_parts.append(contract(head_rows(queries, head), grad_scores, 1, 1) * score_scale)
        rest = [jnp.zeros((shape.qkv_rows - 3 * width, BLOCK), high)]
        out_ref[0, :, at] = jnp.concatenate(
            query_parts + key_parts + value_parts + rest, axis=0
        ).astype(low)

    return call(
        kernel,
        "attention_backward",
        (blocks // share, shape.panels),
        [
            (qkv, (1, qkv.shape[1], share * BLOCK), lambda b, n: (n, 0, b)),
            (probs, (share, 1, heads, BLOCK, BLOCK), lambda b, n: (b, n, 0, 0, 0)),
            (grad_attended, (1, shape.out_rows, share * BLOCK), lambda b, n: (n, 0, b)),
        ],
        [
            (
                (shape.panels, shape.qkv_rows, shape.tokens),
                low,
                (1, shape.qkv_rows, share * BLOCK),
                lambda b, n: (n, 0, b),
            )
        ],
    )[0]


def weighted(weights, refs, held, sems, source_ref):
    block = pl.program_id(0)
    count = len(weights.panels)
    weights.start_all(refs, held, sems, block)
    for panel in range(count):
        weights.wait(refs, held, sems, block, panel)
    if weights.wide:
        source = source_ref[...]
        return contract(held[...], source.reshape(-1, source.shape[2]), 1, 0)
    return sum(contract(held[panel], source_ref[panel], 1, 0) for panel in range(count))


def store_sums(shape, sums_ref, rows, slot, block, values):
    lane = lax.broadcasted_iota(jnp.int32, (values[0].shape[0], sums_ref.shape[1]), 1)
    kept = sums_ref[rows]
    for j, value in enumerate(values):
        kept = jnp.where(lane == slot * shape.seqs + block * shape.share + j, value, kept)
    sums_ref[rows] = kept


def row_chunks(shape):
    rows = shape.width // 8
    return [slice(k * rows, (k + 1) * rows) for k in range(8)]


def moments(shape, first, second):
    center = first * (1.0 / shape.width)
    return center, lax.rsqrt(second * (1.0 / shape.width) - center * center + norm_epsilon)


def down_rows(values):
    return jnp.sum(values, axis=0, keepdims=True)


def panel_blocks(shape, array):
    return (array, (*array.shape[:2], shape.block), lambda b, *_: (0, 0, b))


def token_blocks(shape, array):
    return (array, (shape.width, shape.block), lambda b, *_: (0, b))


def sums_out(shape, slots):
    return ((shape.width, slots * shape.seqs), high, None, None)


def total_scratch(shape):
    return [pltpu.VMEM((shape.width, shape.block), high)]


def pieces_out(shape):
    return (
        (shape.panels, shape.seqs, shape.local, shape.part),
        low,
        (shape.panels, shape.share, shape.local, shape.part),
        lambda b, *_: (0, b, 0, 0),
    )


def norm_grads(shape, grad_ref, values_ref, table_ref, slot, block, sums_ref, sums_slot):
    first, second = 0.0, 0.0
    for rows in row_chunks(shape):
        values = values_ref[rows].astype(high)
        first, second = first + down_rows(values), second + down_rows(values * values)
    center, inverse = moments(shape, first, second)
    totals, crossed = 0.0, 0.0
    for rows in row_chunks(shape):
        grad = grad_ref[rows]
        normed = (values_ref[rows].astype(high) - center) * inverse
        store_sums(shape, sums_ref, rows, sums_slot, block, seq_sums(shape, grad))
        store_sums(shape, sums_ref, rows, sums_slot + 1, block, seq_sums(shape, grad * normed))
        hat = grad * (1.0 + spread(shape, table_ref[rows], slot, block))
        totals, crossed = totals + down_rows(hat), crossed + down_rows(hat * normed)

    def third(rows):
        normed = (values_ref[rows].astype(high) - center) * inverse
        hat = grad_ref[rows] * (1.0 + spread(shape, table_ref[rows], slot, block))
        return inverse * (hat - totals * (1.0 / shape.width) - normed * (crossed * (1.0 / shape.width)))

    return third


def project_out(shape, weights, attended, residual, table):
    order = weights.prefetch
    count = len(weights.arrays)

    def kernel(*refs):
        refs, order_refs = refs[len(order) :], refs[: len(order)]
        weight_refs, rest = refs[:count], refs[count:]
        attended_ref, residual_ref, table_ref, middle_ref, branch_ref, input_ref = rest[:6]
        held, sems, total = rest[6:]
        block = pl.program_id(0)
        total[...] = weighted(weights, (*order_refs, *weight_refs), held, sems, attended_ref)
        first, second = 0.0, 0.0
        for rows in row_chunks(shape):
            branch = total[rows]
            middle = residual_ref[rows].astype(high) + branch * spread(
                shape, table_ref[rows], 2, block
            )
            middle_ref[rows] = middle
            branch_ref[rows] = branch.astype(low)
            first, second = first + down_rows(middle), second + down_rows(middle * middle)
        center, inverse = moments(shape, first, second)
        for rows in row_chunks(shape):
            table = table_ref[rows]
            normed = (middle_ref[rows] - center) * inverse
            input_ref[rows] = (
                normed * (1.0 + spread(shape, table, 4, block)) + spread(shape, table, 3, block)
            ).astype(low)

    return call(
        kernel,
        "project_out",
        (shape.blocks,),
        weights.ins()
        + [panel_blocks(shape, attended), token_blocks(shape, residual), (table, None, None)],
        [token_out(shape, high), token_out(shape, low), token_out(shape, low)],
        weights.scratch(True) + total_scratch(shape),
        prefetch=order,
    )


def gelu_and_slope(values):
    root = math.sqrt(2.0 / math.pi)
    square = values * values
    bent = jnp.tanh(root * values * (1.0 + 0.044715 * square))
    half = 0.5 * (1.0 + bent)
    slope = half + 0.5 * values * (1.0 - bent * bent) * (root + 3.0 * 0.044715 * root * square)
    return values * half, slope


def project_up(shape, weights, source, bias):
    order = weights.prefetch
    count = len(weights.arrays)
    inner = weights.stop

    def kernel(*refs):
        refs, order_refs = refs[len(order) :], refs[: len(order)]
        weight_refs, rest = refs[:count], refs[count:]
        source_ref, bias_ref, hidden_ref, slope_ref, held, sems = rest
        panel = weights.panel((*order_refs, *weight_refs), held, sems, pl.program_id(0))
        values = contract(panel[...], source_ref[...], 0, 0) + bias_ref[0]
        hidden, slope = gelu_and_slope(values)
        hidden_ref[0] = hidden.astype(low)
        slope_ref[0] = slope.astype(low)

    return call(
        kernel,
        "project_up",
        (shape.panels,),
        weights.ins() + [(source, None, None), panel_in(bias)],
        [by_panel(shape, inner, low), by_panel(shape, inner, low)],
        weights.scratch(),
        prefetch=order,
    )


def project_down(shape, there, weights, hidden, middle, upstream, table, wide_count):
    order = weights.prefetch
    count = len(weights.arrays)
    bias_at = 6 * shape.seqs
    depth = shape.width // wide_count

    def kernel(at_ref, *refs):
        refs, order_refs = refs[len(order) :], refs[: len(order)]
        weight_refs, rest = refs[:count], refs[count:]
        hidden_ref, middle_ref, upstream_ref, table_ref, out_ref, gate_ref = rest[:6]
        held, sems, total, block_held = rest[6:]
        block = pl.program_id(0)
        total[...] = weighted(weights, (*order_refs, *weight_refs), held, sems, hidden_ref)
        for k in range(wide_count):
            rows = slice(k * depth, (k + 1) * depth)
            table = table_ref[rows]
            mlp = total[rows] + pick(table, bias_at)
            block_held[k] = middle_ref[rows] + mlp * spread(shape, table, 5, block)
            store_sums(
                shape, gate_ref, rows, 0, block, seq_sums(shape, upstream_ref[rows].astype(high) * mlp)
            )
        take_pieces(shape, at_ref, block_held, out_ref)

    return call(
        kernel,
        "project_down",
        (shape.blocks,),
        weights.ins()
        + [panel_blocks(shape, hidden), token_blocks(shape, middle)]
        + [token_blocks(shape, upstream), (table, None, None)],
        [pieces_out(shape), sums_out(shape, 1)],
        weights.scratch(True)
        + [
            *total_scratch(shape),
            pltpu.VMEM((wide_count, depth, shape.block), high),
        ],
        [there, *order],
    )


def grad_outs(shape, columns):
    tall = shape.panels // 2
    half = shape.width // 2
    return [((2, tall, half, columns), low, (2, 1, half, columns), lambda n, *_: (0, n, 0, 0))]


def core_panels(shape, array, core):
    tall = shape.panels // 2
    return (array, (1, *array.shape[1:]), lambda n, *_: (n + core * tall, 0, 0))


def weight_grad(shape, name, source, grad, core):
    columns = grad.shape[1]
    half = shape.width // 2

    def kernel(source_ref, grad_ref, out_ref):
        product = contract(source_ref[...], grad_ref[0], 1, 1).astype(low)
        out_ref[...] = product.reshape(2, 1, half, columns)

    return call(
        kernel,
        name,
        (shape.panels // 2,),
        [(source, None, None), core_panels(shape, grad, core)],
        grad_outs(shape, columns),
    )[0]


def device_weight_grad(shape, name, source, grad, order, wide_count):
    columns = grad.shape[1]
    rows = shape.width // wide_count

    def kernel(order_ref, source_ref, grad_ref, out_ref):
        product = contract(source_ref[...], grad_ref[0], 1, 1).astype(low)
        panel = pl.program_id(0)
        for block in range(wide_count):
            device = order_ref[panel * wide_count + block]
            out_ref[0, device // shape.panels] = product[block * rows : (block + 1) * rows]

    out = call(
        kernel,
        name,
        (shape.panels,),
        [(source, None, None), panel_in(grad)],
        [
            (
                (shape.panels, wide_count, rows, columns),
                low,
                (1, wide_count, rows, columns),
                lambda n, order_ref: (order_ref[n * wide_count] % shape.panels, 0, 0, 0),
            )
        ],
        prefetch=[order],
    )[0]
    return out.reshape(shape.panels * wide_count, rows, columns)


def first_weight_grad(shape, source, grad_qkv, grad_branch, attended, core):
    columns = 4 * shape.local
    begin = shape.out_from
    half = shape.width // 2

    def kernel(source_ref, qkv_ref, branch_ref, attended_ref, out_ref, held):
        held[:, : shape.qkv_rows] = contract(source_ref[...], qkv_ref[0], 1, 1)
        late = contract(branch_ref[...], attended_ref[0], 1, 1)
        both_there = shape.qkv_rows - begin
        if both_there:
            held[:, begin : shape.qkv_rows] += late[:, :both_there]
        held[:, shape.qkv_rows :] = late[:, both_there:]
        out_ref[...] = held[...].astype(low).reshape(2, 1, half, columns)

    return call(
        kernel,
        "first_weight_grad",
        (shape.panels // 2,),
        [
            (source, None, None),
            core_panels(shape, grad_qkv, core),
            (grad_branch, None, None),
            core_panels(shape, attended, core),
        ],
        grad_outs(shape, columns),
        [pltpu.VMEM((shape.width, columns), high)],
    )[0]


def hidden_backward(shape, weights, grad_mlp, slope):
    order = weights.prefetch
    count = len(weights.arrays)
    inner = weights.stop

    def kernel(*refs):
        refs, order_refs = refs[len(order) :], refs[: len(order)]
        weight_refs, rest = refs[:count], refs[count:]
        grad_ref, slope_ref, out_ref, bias_ref, held, sems = rest
        panel = weights.panel((*order_refs, *weight_refs), held, sems, pl.program_id(0))
        values = contract(panel[...], grad_ref[...], 0, 0) * slope_ref[0].astype(high)
        values = values.astype(low)
        out_ref[0] = values
        bias_ref[0] = jnp.sum(values.astype(high), axis=1, keepdims=True)

    return call(
        kernel,
        "hidden_backward",
        (shape.panels,),
        weights.ins() + [(grad_mlp, None, None), panel_in(slope)],
        [
            by_panel(shape, inner, low),
            ((shape.panels, inner, 1), high, (1, inner, 1), lambda n, *_: (n, 0, 0)),
        ],
        weights.scratch(),
        prefetch=order,
    )


def middle_backward(shape, weights, grad_up, middle, upstream, branch, table):
    order = weights.prefetch
    count = len(weights.arrays)

    def kernel(*refs):
        refs, order_refs = refs[len(order) :], refs[: len(order)]
        weight_refs, rest = refs[:count], refs[count:]
        grad_ref, middle_ref, upstream_ref, branch_ref, table_ref = rest[:5]
        out_ref, low_ref, sums_ref, held, sems, total = rest[5:]
        block = pl.program_id(0)
        total[...] = weighted(weights, (*order_refs, *weight_refs), held, sems, grad_ref)
        third = norm_grads(
            shape, total, middle_ref, table_ref, 4, block, sums_ref, 1
        )
        for rows in row_chunks(shape):
            grad = upstream_ref[rows].astype(high) + third(rows)
            store_sums(
                shape, sums_ref, rows, 0, block, seq_sums(shape, grad * branch_ref[rows].astype(high))
            )
            out_ref[rows] = grad
            low_ref[rows] = (grad * spread(shape, table_ref[rows], 2, block)).astype(low)

    return call(
        kernel,
        "middle_backward",
        (shape.blocks,),
        weights.ins()
        + [panel_blocks(shape, grad_up)]
        + [token_blocks(shape, v) for v in (middle, upstream, branch)]
        + [(table, None, None)],
        [token_out(shape, high), token_out(shape, low), sums_out(shape, 3)],
        weights.scratch(True) + total_scratch(shape),
        prefetch=order,
    )


def attended_backward(shape, weights, grad_branch):
    order = weights.prefetch
    count = len(weights.arrays)

    def kernel(*refs):
        refs, order_refs = refs[len(order) :], refs[: len(order)]
        weight_refs, (grad_ref, out_ref, held, sems) = refs[:count], refs[count:]
        panel = weights.panel((*order_refs, *weight_refs), held, sems, pl.program_id(0))
        out_ref[0] = contract(panel[...], grad_ref[...], 0, 0).astype(low)

    return call(
        kernel,
        "attended_backward",
        (shape.panels,),
        weights.ins() + [(grad_branch, None, None)],
        [by_panel(shape, shape.out_rows, low)],
        weights.scratch(),
        prefetch=order,
    )[0]


def input_backward(shape, there, weights, grad_qkv, residual, grad_middle, table, wide_count):
    order = weights.prefetch
    count = len(weights.arrays)
    depth = shape.width // wide_count

    def kernel(at_ref, *refs):
        refs, order_refs = refs[len(order) :], refs[: len(order)]
        weight_refs, rest = refs[:count], refs[count:]
        qkv_ref, residual_ref, middle_ref, table_ref, out_ref, sums_ref = rest[:6]
        held, sems, total, block_held = rest[6:]
        block = pl.program_id(0)
        total[...] = weighted(weights, (*order_refs, *weight_refs), held, sems, qkv_ref)
        third = norm_grads(shape, total, residual_ref, table_ref, 1, block, sums_ref, 0)
        for k in range(wide_count):
            rows = slice(k * depth, (k + 1) * depth)
            block_held[k] = middle_ref[rows] + third(rows)
        take_pieces(shape, at_ref, block_held, out_ref)

    return call(
        kernel,
        "input_backward",
        (shape.blocks,),
        weights.ins()
        + [panel_blocks(shape, grad_qkv)]
        + [token_blocks(shape, v) for v in (residual, grad_middle)]
        + [(table, None, None)],
        [pieces_out(shape), sums_out(shape, 2)],
        weights.scratch(True)
        + [
            *total_scratch(shape),
            pltpu.VMEM((wide_count, depth, shape.block), high),
        ],
        [there, *order],
    )


def on_device(
    tokens,
    ada_weight,
    ada_bias,
    class_table,
    query_weight,
    key_weight,
    value_weight,
    out_weight,
    up_weight,
    up_bias,
    down_weight,
    down_bias,
    cotangent,
    clip_frames,
    time_ids,
    class_ids,
):
    micro_count, seq_count, local_width, seq_tokens = tokens.shape
    class_count, full_width = class_table.shape
    panels, wide_count = lax.axis_size("narrow"), lax.axis_size("wide")
    wide_at = lax.axis_index("wide")
    seqs = micro_count * seq_count
    shape = Shape(seqs, seq_tokens // panels, full_width, panels)
    own_rows = ada_weight.shape[0]
    deep = wide_count // 2
    highest = lax.Precision.HIGHEST
    local_shape = (seqs, local_width, seq_tokens)
    there, came, goes = orders()

    class_hot = (class_ids.reshape(seqs)[:, None] == jnp.arange(class_count)[None, :]).astype(low)
    condition = time_embedding(time_ids.reshape(seqs), full_width) + jnp.einsum(
        "sc,cd->sd", class_hot, class_table, preferred_element_type=high
    )
    sigmoid_cond = jax.nn.sigmoid(condition)
    cond_act = (condition * sigmoid_cond).astype(low)
    silu_slope = sigmoid_cond * (1.0 + condition * (1.0 - sigmoid_cond))
    own_cond = lax.dynamic_slice_in_dim(cond_act, wide_at * own_rows, own_rows, axis=1)
    own_slope = lax.dynamic_slice_in_dim(silu_slope, wide_at * own_rows, own_rows, axis=1)

    first_piece = jnp.concatenate([query_weight, key_weight, value_weight, out_weight.T], axis=1)
    first, up = Gather(first_piece), Gather(up_weight)
    order = device_order()
    mod_part = jnp.einsum("sd,dje->jse", own_cond, ada_weight, preferred_element_type=high)
    mod_part = mod_part.reshape(6 * seqs, local_width)
    hops = [{"side_by": 1}]
    while 2 ** len(hops) <= deep:
        hops.append({"deep_by": 2 ** (len(hops) - 1)})

    first.step()
    token_swap = NarrowSwap(tokens.reshape(local_shape))
    token_same = token_swap.step(0)
    mod_part = mod_part + send(mod_part, **hops[0])
    first.ring, token_same, mod_part, token_swap.parts = sync(
        first.ring, token_same, mod_part, token_swap.parts
    )

    first.step()
    token_other = token_swap.step(1)
    mod_part = mod_part + send(mod_part, **hops[1])
    first.ring, token_other, mod_part = sync(first.ring, token_other, mod_part)

    for at in range(2, max(deep - 1, len(hops))):
        if at < len(hops):
            mod_part = mod_part + send(mod_part, **hops[at])
        if at < deep - 1:
            first.step()
        if at == 2:
            token_near, token_far = token_swap.pieces(token_same, token_other)
        if at == max(deep - 1, len(hops)) - 1:
            first.front_side()
            first.front, first.front_got = sync(first.front, first.front_got)
        first.ring, mod_part = sync(first.ring, mod_part)

    first.rear_tall()
    up.step()
    mod_own = (
        mod_part.reshape(6, seqs, local_width) + ada_bias.astype(high)[:, None, :]
    ).reshape(6 * seqs, local_width)
    small = gather_narrow(
        jnp.concatenate(
            [
                mod_own,
                down_bias.astype(high)[None, :],
                up_bias.astype(high).reshape(-1, local_width),
            ]
        )
    )
    first.rear, first.rear_got, first.front, first.front_got, token_far, small, up.ring = sync(
        first.rear, first.rear_got, first.front, first.front_got, token_far, small, up.ring
    )

    first.second()
    first.core(0, 2)
    for _ in range(2, deep):
        up.step()
    table, up_bias_full = lay_small(shape, came, small, wide_count)
    token_parts = token_near + [token_far[k : k + 1] for k in range(panels // 2)]
    frame_at = jnp.arange(shape.part) % FRAMES
    in_clip = (frame_at[None, :] < clip_frames.reshape(seqs)[:, None]).astype(jnp.int32).reshape(-1)
    residual, input_one = prepare_tokens(shape, came, token_parts, table, wide_count)
    upstream_cut = cut_tokens(shape, after(cotangent.reshape(local_shape), input_one))
    first.arrays, input_one, up.ring, upstream_cut = sync(
        first.arrays, input_one, up.ring, upstream_cut
    )

    first.core(*[k for k in range(len(first.arrays)) if k not in (0, 2)])
    qkv_weights = Weights(first.result(), 0, shape.qkv_rows)
    out_weights = Weights(first.result(), shape.out_from)
    up.front_side()
    up.rear_tall()
    qkv = project_qkv(shape, qkv_weights, input_one)
    qkv, up.front, up.front_got, up.rear, up.rear_got = sync(
        qkv, up.front, up.front_got, up.rear, up.rear_got
    )

    up.second()
    up.core(0, 2)
    down_full = lax.all_gather(after(down_weight.T, qkv), both, axis=0, tiled=False)
    attended, probs = attention_forward(shape, qkv, in_clip)
    attended, up.arrays = sync(attended, up.arrays)

    up.core(*[k for k in range(len(up.arrays)) if k not in (0, 2)])
    upstream_parts = swap_narrow(upstream_cut)
    middle, branch, input_two = project_out(shape, out_weights, attended, residual, table)
    middle, input_two, up.cores = sync(middle, input_two, up.cores)

    up_all = Weights(up.result())
    hidden, slope = project_up(shape, up_all, input_two, up_bias_full)
    hidden, slope, upstream_parts = sync(hidden, slope, upstream_parts)

    upstream, grad_mlp, down_bias_part = prepare_upstream(
        shape, there, upstream_parts, table, wide_count
    )
    down_grads = device_weight_grad(
        shape, "down_weight_grad", grad_mlp, hidden, order, wide_count
    )
    down_grad = lax.psum_scatter(
        down_grads, ("narrow", "wide"), scatter_dimension=0, tiled=False
    ).astype(high)
    down_all = GatheredWeights(down_full, order, panels)
    output_parts, gate_two_part = project_down(
        shape, there, down_all, after(hidden, down_grads), middle, upstream, table, wide_count
    )
    output_parts, gate_two_part = sync(output_parts, gate_two_part)

    output_got = swap_narrow(output_parts)
    grad_up, up_bias_part = hidden_backward(
        shape, down_all, after(grad_mlp, gate_two_part), slope
    )
    other = weight_grad(shape, "up_weight_grad", input_two, grad_up, 1)
    other, output_got = sync(other, output_got)

    up_sum = GradSum(other)
    near = weight_grad(shape, "up_weight_grad", after(input_two, other), grad_up, 0)
    near, up_sum.got = sync(near, up_sum.got)
    up_sum.near(near)
    half = deep // 2
    up_parts = up_sum.split(half)
    sums = up_parts[0].sums("y")
    up_parts[0].along("y", sums)
    grad_middle, grad_branch, middle_sums = middle_backward(
        shape, up_all, after(grad_up, near, *sums), middle, upstream, branch, table
    )
    *_, grad_branch = sync(*up_parts, grad_branch)

    tall_sums, side_sums = up_parts[1].sums("y"), up_parts[0].sums("x")
    up_parts[1].along("y", tall_sums)
    up_parts[0].along("x", side_sums)
    grad_attended = attended_backward(
        shape, out_weights, after(grad_branch, *tall_sums, *side_sums)
    )
    grad_qkv = attention_backward(shape, qkv, probs, grad_attended)
    *_, grad_qkv = sync(*up_parts, grad_qkv)

    side_sums = up_parts[1].sums("x")
    up_parts[1].along("x", side_sums)
    grad_qkv = after(grad_qkv, *side_sums)
    other = first_weight_grad(shape, input_one, grad_qkv, grad_branch, attended, 1)
    *_, other = sync(*up_parts, other)

    first_sum = GradSum(other)
    up_sums = deep_sums(up_parts)
    along_deep(up_parts, up_sums)
    near = first_weight_grad(
        shape, after(input_one, other, *up_sums), grad_qkv, grad_branch, attended, 0
    )
    near, first_sum.got = sync(near, first_sum.got)
    first_sum.near(near)
    first_parts = first_sum.split(half)
    side_sums, tall_sums = first_parts[0].sums("x"), first_parts[1].sums("y")
    first_parts[0].along("x", side_sums)
    first_parts[1].along("y", tall_sums)
    input_parts, input_sums = input_backward(
        shape,
        there,
        qkv_weights,
        after(grad_qkv, *side_sums, *tall_sums),
        residual,
        grad_middle,
        table,
        wide_count,
    )
    *_, input_parts, input_sums = sync(*first_parts, up_parts[0], input_parts, input_sums)
    input_got = swap_narrow(input_parts)

    tall_sums, side_sums = first_parts[0].sums("y"), first_parts[1].sums("x")
    first_parts[0].along("y", tall_sums)
    first_parts[1].along("x", side_sums)
    small_grad = lay_small_grads(
        shape,
        goes,
        input_sums,
        middle_sums,
        after(gate_two_part, *side_sums, *tall_sums),
        down_bias_part,
        up_bias_part,
        wide_count,
    )
    small_grad = small_grad.reshape(2, panels // 2, *small_grad.shape[1:])
    small_grad = small_grad[0] + send(small_grad[1], core_by=1)
    by = 1
    while by < deep:
        small_grad = small_grad + send(small_grad, deep_by=by)
        by *= 2
    *_, small_grad = sync(*first_parts, small_grad)
    sums = deep_sums(first_parts)
    first_got = along_deep(first_parts, sums)
    output = join_tokens(shape, after(output_got, small_grad), low)
    small_grad = after(small_grad, *sums)
    small_grad = small_grad + send(small_grad, side_by=1)
    small_grad = after(small_grad, output, input_got)
    small_grad = sum(
        [small_grad[0]] + [send(small_grad[k], tall_by=k) for k in range(1, panels // 2)]
    )
    own_mod = small_grad[: 6 * seqs].reshape(6, seqs, local_width)
    down_bias_grad = small_grad[6 * seqs]
    up_bias_grad = small_grad[6 * seqs + 1 :].reshape(-1)
    ada_grad = jnp.einsum("sd,jse->dje", own_cond.astype(high), own_mod, precision=highest)
    ada_bias_grad = jnp.sum(own_mod, axis=1)
    input_grad = join_tokens(shape, after(input_got, own_mod), high)
    own_mod = after(own_mod, *first_got[:1], input_grad)
    cond_local = sum_narrow(
        own_slope * jnp.einsum("jse,dje->sd", own_mod, ada_weight.astype(high), precision=highest)
    )
    cond_local = after(cond_local, *first_got)
    cond_grad = sum_wide(
        lax.dynamic_update_slice_in_dim(
            jnp.zeros((seqs, full_width), high), cond_local, wide_at * own_rows, axis=1
        )
    )
    up_grad = up_parts[0].total()
    first_grad = first_parts[0].total()
    table_grad = jnp.einsum("sc,sd->cd", class_hot.astype(high), cond_grad, precision=highest)
    return (
        output.reshape(tokens.shape),
        input_grad.reshape(tokens.shape),
        ada_grad,
        ada_bias_grad,
        table_grad,
        first_grad[:, :local_width],
        first_grad[:, local_width : 2 * local_width],
        first_grad[:, 2 * local_width : 3 * local_width],
        first_grad[:, 3 * local_width :].T,
        up_grad,
        up_bias_grad,
        down_grad.T,
        down_bias_grad,
    )


def solution(mesh):
    return jax.shard_map(
        on_device,
        mesh=mesh,
        in_specs=(
            P(None, None, "narrow", "wide"),
            P("wide", None, "narrow"),
            P(None, "narrow"),
            P(),
            P("wide", "narrow"),
            P("wide", "narrow"),
            P("wide", "narrow"),
            P("narrow", "wide"),
            P("wide", "narrow"),
            P("narrow"),
            P("narrow", "wide"),
            P("narrow"),
            P(None, None, "narrow", "wide"),
            P(),
            P(),
            P(),
        ),
        out_specs=(
            P(None, None, "narrow", "wide"),
            P(None, None, "narrow", "wide"),
            P("wide", None, "narrow"),
            P(None, "narrow"),
            P(),
            P("wide", "narrow"),
            P("wide", "narrow"),
            P("wide", "narrow"),
            P("narrow", "wide"),
            P("wide", "narrow"),
            P("narrow"),
            P("narrow", "wide"),
            P("narrow"),
        ),
        check_vma=False,
    )
```

```python
import functools
import math

import jax
import jax.numpy as jnp
from jax import lax
from jax.experimental import pallas as pl
from jax.experimental.pallas import tpu as pltpu
from jax.sharding import PartitionSpec as P

HEAD_DIM = 72
FRAMES = 16
BLOCK = 128
MIB = 1024 * 1024
FORWARD_SHARE = 8
BACKWARD_SHARE = 4
COSTS = {
    "project_qkv": 15,
    "attention_forward": 24,
    "project_out": 17,
    "project_up": 28,
    "project_down": 25,
    "down_weight_grad": 10,
    "up_weight_grad": 10,
    "first_weight_grad": 12,
    "hidden_backward": 21,
    "middle_backward": 30,
    "attended_backward": 9,
    "attention_backward": 33,
    "input_backward": 25,
}
COST_SCALE = 1e8

norm_epsilon = 1e-06
masked_score = -1e30
both = ("wide", "narrow")
low = jnp.bfloat16
high = jnp.float32


def time_embedding(time_ids, full_width):
    half_width = full_width // 2
    frequency = jnp.exp(-math.log(10000.0) * jnp.arange(half_width, dtype=jnp.float32) / half_width)
    angles = time_ids.astype(jnp.float32)[..., None] * frequency
    return jnp.concatenate([jnp.cos(angles), jnp.sin(angles)], axis=-1)


def place():
    deep, tall = lax.axis_size("wide") // 2, lax.axis_size("narrow") // 2
    wide_at, narrow_at = lax.axis_index("wide"), lax.axis_index("narrow")
    return deep, tall, wide_at // 2, wide_at % 2, narrow_at // 2, narrow_at % 2


def send(value, deep_by=0, side_by=0, tall_by=0, core_by=0):
    deep, tall = lax.axis_size("wide") // 2, lax.axis_size("narrow") // 2
    pairs = []
    for z in range(deep):
        for x in range(2):
            for y in range(tall):
                for c in range(2):
                    source = ((z * 2 + x) * tall + y) * 2 + c
                    target = (
                        ((z + deep_by) % deep * 2 + (x + side_by) % 2) * tall + (y + tall_by) % tall
                    ) * 2 + (c + core_by) % 2
                    pairs.append((source, target))
    return lax.ppermute(value, both, pairs)


def after(value, *earlier):
    return lax.optimization_barrier((value, earlier))[0]


def sync(*values):
    arrays = []
    for value in values:
        if isinstance(value, GradSum):
            arrays += [array for array, _ in value.terms]
        elif isinstance(value, (list, tuple)):
            arrays += value
        else:
            arrays.append(value)
    arrays = iter(lax.optimization_barrier(tuple(arrays)))
    results = []
    for value in values:
        if isinstance(value, GradSum):
            value.terms = [(next(arrays), cuts) for _, cuts in value.terms]
            results.append(value)
        elif isinstance(value, (list, tuple)):
            results.append([next(arrays) for _ in value])
        else:
            results.append(next(arrays))
    return results


class Gather:
    def __init__(self, piece):
        self.deep = lax.axis_size("wide") // 2
        self.tall = lax.axis_size("narrow") // 2
        self.ring = [piece]
        self.rows = piece.shape[0]

    def step(self):
        self.ring.append(send(self.ring[-1], deep_by=1))

    def front_side(self):
        self.front = jnp.concatenate(self.ring[: self.deep // 2], axis=0)
        self.front_got = [send(self.front, side_by=1)]

    def rear_tall(self):
        self.rear = jnp.concatenate(self.ring[self.deep // 2 :], axis=0)
        self.rear_got = [send(self.rear, tall_by=k) for k in range(1, self.tall)]

    def second(self):
        self.front = jnp.concatenate([self.front] + self.front_got, axis=0)
        self.rear = jnp.concatenate([self.rear] + self.rear_got, axis=0)
        self.arrays = [self.rear, send(self.rear, side_by=1), self.front]
        self.arrays += [send(self.front, tall_by=k) for k in range(1, self.tall)]
        self.cores = [None] * len(self.arrays)

    def core(self, *at):
        for k in at:
            self.cores[k] = send(self.arrays[k], core_by=1)

    def result(self):
        count = len(self.arrays)
        near = self.deep // 2 * self.rows
        far = self.deep * self.rows - near
        panels = []
        for c in range(2):
            for y in range(self.tall):
                panels.append(
                    [
                        (c * count + 2 + y, (), 0, 0, near),
                        (c * count, (), y * far, near, far),
                        (c * count + 2 + y, (), near, near + far, near),
                        (c * count + 1, (), y * far, 2 * near + far, far),
                    ]
                )
        return self.arrays + self.cores, panels


class LateGather:
    def __init__(self, piece):
        self.deep = lax.axis_size("wide") // 2
        self.tall = lax.axis_size("narrow") // 2
        self.piece = piece
        self.cores = []

    def side(self):
        self.line = [self.piece, send(self.piece, side_by=1)]

    def along_tall(self):
        line = jnp.stack(self.line)
        self.plane = [line] + [send(line, tall_by=k) for k in range(1, self.tall)]

    def step(self):
        if not hasattr(self, "ring"):
            self.ring = [jnp.stack(self.plane)]
        self.ring.append(send(self.ring[-1], deep_by=1))

    def core(self, *at):
        self.cores += [send(self.ring[k], core_by=1) for k in at]

    def result(self):
        tall, deep, rows = self.tall, self.deep, self.piece.shape[0]
        arrays = self.ring + self.cores
        if rows % 16:
            whole = [
                jnp.concatenate([arrays[c * deep + k][y, x] for x in range(2) for k in range(deep)])
                for c in range(2)
                for y in range(tall)
            ]
            return whole, [[(at, (), 0, 0, 2 * deep * rows)] for at in range(2 * tall)]
        panels = [
            [
                (c * deep + k, (y, x), 0, (x * deep + k) * rows, rows)
                for x in range(2)
                for k in range(deep)
            ]
            for c in range(2)
            for y in range(tall)
        ]
        return arrays, panels


def device_order():
    deep, tall, z, x, y, c = place()
    order = []
    for core in range(2):
        for k in range(tall):
            n = (y - k) % tall * 2 + (c - core) % 2
            for side in range(2):
                for far in range(deep):
                    w = (z - far) % deep * 2 + (x - side) % 2
                    order.append(w * 2 * tall + n)
    return jnp.stack(order).astype(jnp.int32)


class GradSum:
    def __init__(self, other):
        self.sizes = {"x": 2, "y": lax.axis_size("narrow") // 2, "z": lax.axis_size("wide") // 2}
        self.got = send(other, core_by=-1)

    def near(self, near):
        _, tall, rows, columns = near.shape
        deep = self.sizes["z"]
        shape = (2, tall, deep, rows // deep, columns)
        self.terms = [(near.reshape(shape), ()), (self.got.reshape(shape), ())]
        self.axes = "xyz"

    def copy(self, cuts):
        one = GradSum.__new__(GradSum)
        one.sizes, one.axes = dict(self.sizes), self.axes
        one.terms = [(array, earlier + cuts) for array, earlier in self.terms]
        return one

    def split(self, *ends):
        parts = []
        for start, end in zip((0, *ends), (*ends, self.sizes["z"])):
            part = self.copy((self.at("z", slice(start, end)),))
            part.sizes["z"] = end - start
            parts.append(part)
        return parts

    def at(self, axis, k):
        return (slice(None),) * self.axes.index(axis) + (k,)

    def hold(self, *earlier):
        self.terms = [(after(array, *earlier), cuts) for array, cuts in self.terms]
        return self

    def total(self, *cuts):
        total = 0.0
        for array, earlier in self.terms:
            for one in earlier + cuts:
                array = array[one]
            total = total + array.astype(high)
        return total

    def sums(self, axis):
        return [self.total(self.at(axis, k)).astype(low) for k in range(1, self.sizes[axis])]

    def along(self, axis, sums, *earlier):
        by = {"x": "side_by", "y": "tall_by", "z": "deep_by"}[axis]
        gots = [send(after(v, *earlier), **{by: -k}) for k, v in enumerate(sums, 1)]
        self.receive(axis, gots)
        return gots

    def receive(self, axis, gots):
        own = self.at(axis, 0)
        self.terms = [(array, cuts + (own,)) for array, cuts in self.terms] + [(v, ()) for v in gots]
        self.axes = self.axes.replace(axis, "")


def deep_sums(parts):
    return [
        part.total(part.at("z", k)).astype(low) for part in parts for k in range(part.sizes["z"])
    ][1:]


def along_deep(parts, sums, *earlier):
    first = parts[0]
    gots = [send(after(v, *earlier), deep_by=-k) for k, v in enumerate(sums, 1)]
    first.receive("z", gots)
    return gots


def swap_narrow(parts):
    return lax.all_to_all(parts, "narrow", 0, 0, tiled=True)


class NarrowSwap:
    def __init__(self, parts):
        self.tall = lax.axis_size("narrow") // 2
        self.parts = parts
        _, _, _, _, self.y, self.c = place()
        self.own = [self.pick(0, core) for core in range(2)]

    def pick(self, k, core):
        target = (self.y + k) % self.tall * 2 + (self.c + core) % 2
        part = self.parts.shape[2] // (2 * self.tall)
        return lax.dynamic_slice_in_dim(self.parts, target * part, part, axis=2)[None]

    def step(self, core):
        return [send(self.pick(k, core), tall_by=k) for k in range(1, self.tall)]

    def pieces(self, same, other):
        other = send(jnp.concatenate([self.own[1]] + other, axis=0), core_by=1)
        return [self.own[0]] + same, other


def orders():
    deep, tall, z, x, y, c = place()
    wide_count, narrow_count = 2 * deep, 2 * tall
    ratio = wide_count // narrow_count

    def stands(n, h):
        w = n * ratio + h
        return (x - w % 2) % 2 * deep + (z - w // 2) % deep

    there = [stands(n, h) for n in range(narrow_count) for h in range(ratio)]
    came, goes = [], []
    for core_by in range(2):
        for tall_by in range(tall):
            source = (y - tall_by) % tall * 2 + (c - core_by) % 2
            target = (y + tall_by) % tall * 2 + (c + core_by) % 2
            came += [stands(source, h) for h in range(ratio)]
            goes += [stands(target, h) for h in range(ratio)]
    return [jnp.stack(v).astype(jnp.int32) for v in (there, came, goes)]


def sum_wide(value):
    deep = lax.axis_size("wide") // 2
    value = value + send(value, side_by=1)
    step = 1
    while step < deep:
        value = value + send(value, deep_by=step)
        step *= 2
    return value


def sum_narrow(value):
    tall = lax.axis_size("narrow") // 2
    value = value + send(value, core_by=1)
    step = 1
    while step < tall:
        value = value + send(value, tall_by=step)
        step *= 2
    return value


def gather_narrow(value):
    tall = lax.axis_size("narrow") // 2
    own = jnp.stack([value] + [send(value, tall_by=k) for k in range(1, tall)])
    return jnp.concatenate([own, send(own, core_by=1)])


def scatter_narrow(value):
    tall = lax.axis_size("narrow") // 2
    value = value.reshape(2, tall, *value.shape[1:])
    total = value[0] + send(value[1], core_by=1)
    return sum([total[0]] + [send(total[k], tall_by=k) for k in range(1, tall)])


def contract(left, right, left_dim, right_dim):
    return lax.dot_general(
        left, right, (((left_dim,), (right_dim,)), ((), ())), preferred_element_type=jnp.float32
    )


def call(kernel, name, grid, ins, outs, scratch=(), prefetch=(), vmem=60):
    in_specs = []
    for array, block, index in ins:
        if block == "any":
            in_specs.append(pl.BlockSpec(memory_space=pl.ANY))
        elif block is None:
            in_specs.append(pl.BlockSpec(array.shape, lambda *_, r=array.ndim: (0,) * r))
        else:
            in_specs.append(pl.BlockSpec(block, index))
    out_specs = []
    for shape, _, block, index in outs:
        if block is None:
            out_specs.append(pl.BlockSpec(shape, lambda *_, r=len(shape): (0,) * r))
        else:
            out_specs.append(pl.BlockSpec(block, index))
    return pl.pallas_call(
        kernel,
        grid_spec=pltpu.PrefetchScalarGridSpec(
            num_scalar_prefetch=len(prefetch),
            grid=grid,
            in_specs=in_specs,
            out_specs=out_specs,
            scratch_shapes=list(scratch),
        ),
        out_shape=[jax.ShapeDtypeStruct(shape, kind) for shape, kind, _, _ in outs],
        compiler_params=pltpu.CompilerParams(vmem_limit_bytes=vmem * MIB),
        cost_estimate=pl.CostEstimate(
            flops=int(COSTS.get(name, 4) * COST_SCALE), bytes_accessed=0, transcendentals=0
        ),
        name=name,
    )(*prefetch, *[array for array, _, _ in ins])


class Weights:
    def __init__(self, gathered, start=0, stop=None):
        self.arrays, self.panels = gathered
        self.columns = self.arrays[0].shape[-1]
        self.start, self.stop = start, self.columns if stop is None else stop
        self.rows = sum(size for *_, size in self.panels[0])
        self.prefetch = []

    def ins(self):
        return [(array, "any", None) for array in self.arrays]

    def scratch(self, wide=False):
        count, columns = len(self.panels), self.stop - self.start
        self.wide = wide and columns % BLOCK == 0
        return [
            pltpu.VMEM(
                (self.rows, count * columns) if self.wide else (count, self.rows, columns), low
            ),
            pltpu.SemaphoreType.DMA((count, len(self.panels[0]))),
        ]

    def source(self, refs, panel, piece):
        array, lead, begin, row, size = self.panels[panel][piece]
        source = refs[array].at[(*lead, pl.ds(begin, size), slice(self.start, self.stop))]
        return source, row, size

    def copies(self, refs, held, sems, panel):
        copies = []
        columns = self.stop - self.start
        for piece in range(len(self.panels[0])):
            source, row, size = self.source(refs, panel, piece)
            if self.wide:
                target = held.at[pl.ds(row, size), pl.ds(panel * columns, columns)]
            else:
                target = held.at[panel, pl.ds(row, size)]
            copies.append(pltpu.make_async_copy(source, target, sems.at[panel, piece]))
        return copies

    def start_all(self, refs, held, sems, at):
        @pl.when(at == 0)
        def _():
            for panel in range(len(self.panels)):
                for copy in self.copies(refs, held, sems, panel):
                    copy.start()

    def wait(self, refs, held, sems, at, panel, step=0):
        @pl.when(at == step)
        def _():
            for copy in self.copies(refs, held, sems, panel):
                copy.wait()

    def panel(self, refs, held, sems, at):
        self.start_all(refs, held, sems, at)
        for panel in range(len(self.panels)):
            self.wait(refs, held, sems, at, panel, panel)
        return held.at[at]


class GatheredWeights(Weights):
    def __init__(self, gathered, order, panel_count):
        devices, rows, columns = gathered.shape
        blocks = devices // panel_count
        if rows % 16:
            whole = jnp.take(gathered, order, axis=0).reshape(panel_count, blocks * rows, columns)
            super().__init__(([whole], [[(0, (p,), 0, 0, blocks * rows)] for p in range(panel_count)]))
            return
        panels = [
            [(p * blocks + b, (), 0, b * rows, rows) for b in range(blocks)]
            for p in range(panel_count)
        ]
        super().__init__(([gathered], panels))
        self.prefetch = [order]

    def source(self, refs, panel, piece):
        if not self.prefetch:
            return super().source(refs, panel, piece)
        at, _, _, row, size = self.panels[panel][piece]
        return refs[1].at[refs[0][at]], row, size


class Shape:
    def __init__(self, seqs, part, width, panels):
        self.seqs, self.part, self.width, self.panels = seqs, part, width, panels
        self.tokens = seqs * part
        self.block = part if part % BLOCK == 0 else self.tokens
        self.blocks = self.tokens // self.block
        self.share = self.block // part
        local = width // panels
        self.local = local
        self.qkv_rows = min(-(-3 * local // BLOCK) * BLOCK, 4 * local)
        self.out_from = 3 * local // BLOCK * BLOCK
        self.out_rows = 4 * local - self.out_from
        self.out_skip = 3 * local - self.out_from


def pick(table, at):
    lane = lax.broadcasted_iota(jnp.int32, table.shape, 1)
    return jnp.sum(jnp.where(lane == at, table, 0.0), axis=1, keepdims=True)


def spread(shape, table, slot, block):
    picked = [pick(table, slot * shape.seqs + block * shape.share + j) for j in range(shape.share)]
    if shape.share == 1:
        return picked[0]
    return jnp.concatenate(
        [jnp.broadcast_to(one, (one.shape[0], shape.part)) for one in picked], axis=1
    )


def seq_sums(shape, values):
    return [
        jnp.sum(values[:, j * shape.part : (j + 1) * shape.part], axis=1, keepdims=True)
        for j in range(shape.share)
    ]


def normed_rows(values):
    width = values.shape[0]
    center = jnp.sum(values, axis=0, keepdims=True) * (1.0 / width)
    shifted = values - center
    variance = jnp.sum(shifted * shifted, axis=0, keepdims=True) * (1.0 / width)
    inverse = lax.rsqrt(variance + norm_epsilon)
    return shifted * inverse, inverse


def norm_backward(grad_hat, normed, inverse):
    width = normed.shape[0]
    totals = jnp.sum(grad_hat, axis=0, keepdims=True) * (1.0 / width)
    crossed = jnp.sum(grad_hat * normed, axis=0, keepdims=True) * (1.0 / width)
    return inverse * (grad_hat - totals - normed * crossed)


def put_pieces(shape, at_ref, piece_refs, held):
    rows = held.shape[1]
    ratio = shape.local // rows
    for n in range(shape.panels):
        for h in range(ratio):
            for j in range(shape.share):
                ref, lead = (piece_refs[0], n) if len(piece_refs) == 1 else (piece_refs[n], 0)
                held[at_ref[n * ratio + h], :, j * shape.part : (j + 1) * shape.part] = ref[
                    lead, j, h * rows : (h + 1) * rows
                ].astype(high)


def take_pieces(shape, at_ref, held, pieces_ref):
    rows = held.shape[1]
    ratio = shape.local // rows
    for n in range(shape.panels):
        for h in range(ratio):
            for j in range(shape.share):
                pieces_ref[n, j, h * rows : (h + 1) * rows, :] = held[
                    at_ref[n * ratio + h], :, j * shape.part : (j + 1) * shape.part
                ].astype(pieces_ref.dtype)


def pieces_in(shape, pieces):
    if isinstance(pieces, list):
        block = (1, shape.share, shape.local, shape.part)
        return [(piece, block, lambda b, *_: (0, b, 0, 0)) for piece in pieces]
    return [pieces_by_device(shape, pieces)]


def pieces_by_device(shape, pieces):
    return (
        pieces,
        (shape.panels, shape.share, shape.local, shape.part),
        lambda b, *_: (0, b, 0, 0),
    )


def token_out(shape, kind):
    return (
        (shape.width, shape.tokens),
        kind,
        (shape.width, shape.block),
        lambda b, *_: (0, b),
    )


def prepare_tokens(shape, there, pieces, table, wide_count):
    def kernel(at_ref, *refs):
        *piece_refs, table_ref, whole_ref, input_ref, held = refs
        block = pl.program_id(0)
        put_pieces(shape, at_ref, piece_refs, held)
        values = held[...].reshape(shape.width, shape.block)
        normed, _ = normed_rows(values)
        table = table_ref[...]
        whole_ref[...] = values.astype(low)
        input_ref[...] = (
            normed * (1.0 + spread(shape, table, 1, block)) + spread(shape, table, 0, block)
        ).astype(low)

    return call(
        kernel,
        "prepare_tokens",
        (shape.blocks,),
        pieces_in(shape, pieces) + [(table, None, None)],
        [token_out(shape, low), token_out(shape, low)],
        [pltpu.VMEM((wide_count, shape.width // wide_count, shape.block), high)],
        [there],
    )


def prepare_upstream(shape, there, pieces, table, wide_count):
    def kernel(at_ref, pieces_ref, table_ref, whole_ref, grad_ref, bias_ref, held):
        block = pl.program_id(0)
        put_pieces(shape, at_ref, [pieces_ref], held)
        values = held[...].reshape(shape.width, shape.block)
        whole_ref[...] = values.astype(low)
        grad_low = (values * spread(shape, table_ref[...], 5, block)).astype(low)
        grad_ref[...] = grad_low
        total = jnp.sum(grad_low.astype(high), axis=1, keepdims=True)

        @pl.when(block == 0)
        def _():
            bias_ref[...] = total

        @pl.when(block > 0)
        def _():
            bias_ref[...] += total

    return call(
        kernel,
        "prepare_upstream",
        (shape.blocks,),
        pieces_in(shape, pieces) + [(table, None, None)],
        [token_out(shape, low), token_out(shape, low), ((shape.width, 1), high, None, None)],
        [pltpu.VMEM((wide_count, shape.width // wide_count, shape.block), high)],
        [there],
    )


def lay_small(shape, came, small, wide_count):
    rows = shape.width // wide_count
    ratio = shape.local // rows
    first = 6 * shape.seqs + 1
    count = small.shape[1]
    ups = count - first

    def kernel(at_ref, small_ref, table_ref, bias_ref, held):
        for p in range(shape.panels):
            turned = small_ref[p].T
            for h in range(ratio):
                held[at_ref[p * ratio + h]] = turned[h * rows : (h + 1) * rows]
            bias_ref[p] = jnp.concatenate(
                [turned[:, first + k : first + k + 1] for k in range(ups)], axis=0
            )
        table_ref[...] = held[...].reshape(shape.width, count)

    return call(
        kernel,
        "lay_small",
        (1,),
        [(small, None, None)],
        [
            ((shape.width, count), high, None, None),
            ((shape.panels, ups * shape.local, 1), high, None, None),
        ],
        [pltpu.VMEM((wide_count, rows, count), high)],
        [came],
    )


def lay_small_grads(shape, goes, late, middle, gate_two, down_bias, up_bias, wide_count):
    rows = shape.width // wide_count
    ratio = shape.local // rows
    seqs = shape.seqs
    ups = up_bias.shape[1] // shape.local
    count = 6 * seqs + 1 + ups

    def kernel(at_ref, late_ref, middle_ref, gate_ref, down_ref, up_ref, small_ref, held):
        table = jnp.concatenate(
            [late_ref[...], middle_ref[...], gate_ref[...], down_ref[...]], axis=1
        )
        held[...] = table.reshape(wide_count, rows, 6 * seqs + 1)
        for p in range(shape.panels):
            parts = [held[at_ref[p * ratio + h]] for h in range(ratio)]
            column = jnp.concatenate(parts, axis=0) if ratio > 1 else parts[0]
            bias = up_ref[p]
            column = jnp.concatenate(
                [column] + [bias[k * shape.local : (k + 1) * shape.local] for k in range(ups)],
                axis=1,
            )
            small_ref[p] = column.T

    return call(
        kernel,
        "lay_small_grads",
        (1,),
        [(v, None, None) for v in (late, middle, gate_two, down_bias, up_bias)],
        [((shape.panels, count, shape.local), high, None, None)],
        [pltpu.VMEM((wide_count, rows, 6 * seqs + 1), high)],
        [goes],
    )[0]


def cut_tokens(shape, local):
    def kernel(local_ref, out_ref):
        for n in range(shape.panels):
            out_ref[n, 0] = local_ref[0, :, n * shape.part : (n + 1) * shape.part]

    return call(
        kernel,
        "cut_tokens",
        (shape.seqs,),
        [(local, (1, *local.shape[1:]), lambda s, *_: (s, 0, 0))],
        [
            (
                (shape.panels, shape.seqs, shape.local, shape.part),
                low,
                (shape.panels, 1, shape.local, shape.part),
                lambda s, *_: (0, s, 0, 0),
            )
        ],
    )[0]


def join_tokens(shape, pieces, kind):
    def kernel(pieces_ref, out_ref):
        for n in range(shape.panels):
            out_ref[0, :, n * shape.part : (n + 1) * shape.part] = pieces_ref[n, 0].astype(kind)

    return call(
        kernel,
        "join_tokens",
        (shape.seqs,),
        [
            (
                pieces,
                (shape.panels, 1, shape.local, shape.part),
                lambda s, *_: (0, s, 0, 0),
            )
        ],
        [
            (
                (shape.seqs, shape.local, shape.panels * shape.part),
                kind,
                (1, shape.local, shape.panels * shape.part),
                lambda s, *_: (s, 0, 0),
            )
        ],
    )[0]


def by_panel(shape, rows, kind):
    return (
        (shape.panels, rows, shape.tokens),
        kind,
        (1, rows, shape.tokens),
        lambda n, *_: (n, 0, 0),
    )


def panel_in(array):
    return (array, (1, *array.shape[1:]), lambda n, *_: (n, 0, 0))


def project_qkv(shape, weights, source):
    order = weights.prefetch
    count = len(weights.arrays)

    def kernel(*refs):
        refs, order_refs = refs[len(order) :], refs[: len(order)]
        weight_refs, (source_ref, out_ref, held, sems) = refs[:count], refs[count:]
        panel = weights.panel((*order_refs, *weight_refs), held, sems, pl.program_id(0))
        out_ref[0] = contract(panel[...], source_ref[...], 0, 0).astype(low)

    return call(
        kernel,
        "project_qkv",
        (shape.panels,),
        weights.ins() + [(source, None, None)],
        [by_panel(shape, shape.qkv_rows, low)],
        weights.scratch(),
        prefetch=order,
    )[0]


def head_rows(block, head):
    return block[head * HEAD_DIM : (head + 1) * HEAD_DIM].astype(low)


def attention_forward(shape, qkv, in_clip):
    width = shape.local
    heads = width // HEAD_DIM
    blocks = shape.tokens // BLOCK
    score_scale = 1.0 / math.sqrt(HEAD_DIM)

    share = math.gcd(blocks, FORWARD_SHARE)

    def kernel(qkv_ref, row_ref, column_ref, out_ref, probs_ref):
        for sub in range(share):
            one_block(qkv_ref, row_ref, column_ref, out_ref, probs_ref, sub)

    def one_block(qkv_ref, row_ref, column_ref, out_ref, probs_ref, sub):
        at = slice(sub * BLOCK, (sub + 1) * BLOCK)
        rows_at = lax.broadcasted_iota(jnp.int32, (BLOCK, BLOCK), 0)
        columns_at = lax.broadcasted_iota(jnp.int32, (BLOCK, BLOCK), 1)
        allowed = (rows_at // FRAMES == columns_at // FRAMES) & (
            ((column_ref[at] > 0) & (row_ref[:, at] > 0)) | (rows_at == columns_at)
        )
        queries = qkv_ref[0, :width, at].astype(high)
        key_rows = qkv_ref[0, width : 2 * width, at].astype(high)
        value_rows = qkv_ref[0, 2 * width : 3 * width, at].astype(high)
        parts = [jnp.zeros((shape.out_skip, BLOCK), high)]
        for head in range(heads):
            scores = (
                contract(head_rows(key_rows, head), head_rows(queries, head), 0, 0) * score_scale
            )
            scores = jnp.where(allowed, scores, masked_score)
            exp_scores = jnp.exp(scores - jnp.max(scores, axis=0, keepdims=True))
            probs = exp_scores * (1.0 / jnp.sum(exp_scores, axis=0, keepdims=True))
            probs_low = probs.astype(low)
            probs_ref[sub, 0, head] = probs_low
            parts.append(contract(head_rows(value_rows, head), probs_low, 1, 0))
        out_ref[0, :, at] = jnp.concatenate(parts, axis=0).astype(low)

    return call(
        kernel,
        "attention_forward",
        (blocks // share, shape.panels),
        [
            (qkv, (1, qkv.shape[1], share * BLOCK), lambda b, n: (n, 0, b)),
            (in_clip[None, :], (1, share * BLOCK), lambda b, n: (0, b)),
            (in_clip[:, None], (share * BLOCK, 1), lambda b, n: (b, 0)),
        ],
        [
            (
                (shape.panels, shape.out_rows, shape.tokens),
                low,
                (1, shape.out_rows, share * BLOCK),
                lambda b, n: (n, 0, b),
            ),
            (
                (blocks, shape.panels, heads, BLOCK, BLOCK),
                low,
                (share, 1, heads, BLOCK, BLOCK),
                lambda b, n: (b, n, 0, 0, 0),
            ),
        ],
    )


def attention_backward(shape, qkv, probs, grad_attended):
    width = shape.local
    heads = width // HEAD_DIM
    blocks = shape.tokens // BLOCK
    score_scale = 1.0 / math.sqrt(HEAD_DIM)

    share = math.gcd(blocks, BACKWARD_SHARE)

    def kernel(qkv_ref, probs_ref, grad_ref, out_ref):
        for sub in range(share):
            one_block(qkv_ref, probs_ref, grad_ref, out_ref, sub)

    def one_block(qkv_ref, probs_ref, grad_ref, out_ref, sub):
        at = slice(sub * BLOCK, (sub + 1) * BLOCK)
        queries = qkv_ref[0, :width, at].astype(high)
        key_rows = qkv_ref[0, width : 2 * width, at].astype(high)
        value_rows = qkv_ref[0, 2 * width : 3 * width, at].astype(high)
        grads = grad_ref[0, :, at].astype(high)[shape.out_skip :]
        query_parts, key_parts, value_parts = [], [], []
        for head in range(heads):
            probs_low = probs_ref[sub, 0, head]
            grad_head = head_rows(grads, head)
            value_parts.append(contract(grad_head, probs_low, 1, 1))
            grad_probs = contract(head_rows(value_rows, head), grad_head, 0, 0)
            probs = probs_low.astype(high)
            crossed = jnp.sum(grad_probs * probs, axis=0, keepdims=True)
            grad_scores = (probs * (grad_probs - crossed)).astype(low)
            query_parts.append(contract(head_rows(key_rows, head), grad_scores, 1, 0) * score_scale)
            key_parts.append(contract(head_rows(queries, head), grad_scores, 1, 1) * score_scale)
        rest = [jnp.zeros((shape.qkv_rows - 3 * width, BLOCK), high)]
        out_ref[0, :, at] = jnp.concatenate(
            query_parts + key_parts + value_parts + rest, axis=0
        ).astype(low)

    return call(
        kernel,
        "attention_backward",
        (blocks // share, shape.panels),
        [
            (qkv, (1, qkv.shape[1], share * BLOCK), lambda b, n: (n, 0, b)),
            (probs, (share, 1, heads, BLOCK, BLOCK), lambda b, n: (b, n, 0, 0, 0)),
            (grad_attended, (1, shape.out_rows, share * BLOCK), lambda b, n: (n, 0, b)),
        ],
        [
            (
                (shape.panels, shape.qkv_rows, shape.tokens),
                low,
                (1, shape.qkv_rows, share * BLOCK),
                lambda b, n: (n, 0, b),
            )
        ],
    )[0]


def weighted(weights, refs, held, sems, source_ref):
    block = pl.program_id(0)
    count = len(weights.panels)
    weights.start_all(refs, held, sems, block)
    for panel in range(count):
        weights.wait(refs, held, sems, block, panel)
    if weights.wide:
        source = source_ref[...]
        return contract(held[...], source.reshape(-1, source.shape[2]), 1, 0)
    return sum(contract(held[panel], source_ref[panel], 1, 0) for panel in range(count))


def store_sums(shape, sums_ref, rows, slot, block, values):
    lane = lax.broadcasted_iota(jnp.int32, (values[0].shape[0], sums_ref.shape[1]), 1)
    kept = sums_ref[rows]
    for j, value in enumerate(values):
        kept = jnp.where(lane == slot * shape.seqs + block * shape.share + j, value, kept)
    sums_ref[rows] = kept


def row_chunks(shape):
    rows = shape.width // 8
    return [slice(k * rows, (k + 1) * rows) for k in range(8)]


def moments(shape, first, second):
    center = first * (1.0 / shape.width)
    return center, lax.rsqrt(second * (1.0 / shape.width) - center * center + norm_epsilon)


def down_rows(values):
    return jnp.sum(values, axis=0, keepdims=True)


def panel_blocks(shape, array):
    return (array, (*array.shape[:2], shape.block), lambda b, *_: (0, 0, b))


def token_blocks(shape, array):
    return (array, (shape.width, shape.block), lambda b, *_: (0, b))


def sums_out(shape, slots):
    return ((shape.width, slots * shape.seqs), high, None, None)


def total_scratch(shape):
    return [pltpu.VMEM((shape.width, shape.block), high)]


def pieces_out(shape):
    return (
        (shape.panels, shape.seqs, shape.local, shape.part),
        low,
        (shape.panels, shape.share, shape.local, shape.part),
        lambda b, *_: (0, b, 0, 0),
    )


def norm_grads(shape, grad_ref, values_ref, table_ref, slot, block, sums_ref, sums_slot):
    first, second = 0.0, 0.0
    for rows in row_chunks(shape):
        values = values_ref[rows].astype(high)
        first, second = first + down_rows(values), second + down_rows(values * values)
    center, inverse = moments(shape, first, second)
    totals, crossed = 0.0, 0.0
    for rows in row_chunks(shape):
        grad = grad_ref[rows]
        normed = (values_ref[rows].astype(high) - center) * inverse
        store_sums(shape, sums_ref, rows, sums_slot, block, seq_sums(shape, grad))
        store_sums(shape, sums_ref, rows, sums_slot + 1, block, seq_sums(shape, grad * normed))
        hat = grad * (1.0 + spread(shape, table_ref[rows], slot, block))
        totals, crossed = totals + down_rows(hat), crossed + down_rows(hat * normed)

    def third(rows):
        normed = (values_ref[rows].astype(high) - center) * inverse
        hat = grad_ref[rows] * (1.0 + spread(shape, table_ref[rows], slot, block))
        return inverse * (hat - totals * (1.0 / shape.width) - normed * (crossed * (1.0 / shape.width)))

    return third


def project_out(shape, weights, attended, residual, table):
    order = weights.prefetch
    count = len(weights.arrays)

    def kernel(*refs):
        refs, order_refs = refs[len(order) :], refs[: len(order)]
        weight_refs, rest = refs[:count], refs[count:]
        attended_ref, residual_ref, table_ref, middle_ref, branch_ref, input_ref = rest[:6]
        held, sems, total = rest[6:]
        block = pl.program_id(0)
        total[...] = weighted(weights, (*order_refs, *weight_refs), held, sems, attended_ref)
        first, second = 0.0, 0.0
        for rows in row_chunks(shape):
            branch = total[rows]
            middle = residual_ref[rows].astype(high) + branch * spread(
                shape, table_ref[rows], 2, block
            )
            middle_ref[rows] = middle
            branch_ref[rows] = branch.astype(low)
            first, second = first + down_rows(middle), second + down_rows(middle * middle)
        center, inverse = moments(shape, first, second)
        for rows in row_chunks(shape):
            table = table_ref[rows]
            normed = (middle_ref[rows] - center) * inverse
            input_ref[rows] = (
                normed * (1.0 + spread(shape, table, 4, block)) + spread(shape, table, 3, block)
            ).astype(low)

    return call(
        kernel,
        "project_out",
        (shape.blocks,),
        weights.ins()
        + [panel_blocks(shape, attended), token_blocks(shape, residual), (table, None, None)],
        [token_out(shape, high), token_out(shape, low), token_out(shape, low)],
        weights.scratch(True) + total_scratch(shape),
        prefetch=order,
    )


def gelu_and_slope(values):
    root = math.sqrt(2.0 / math.pi)
    square = values * values
    bent = jnp.tanh(root * values * (1.0 + 0.044715 * square))
    half = 0.5 * (1.0 + bent)
    slope = half + 0.5 * values * (1.0 - bent * bent) * (root + 3.0 * 0.044715 * root * square)
    return values * half, slope


def project_up(shape, weights, source, bias):
    order = weights.prefetch
    count = len(weights.arrays)
    inner = weights.stop

    def kernel(*refs):
        refs, order_refs = refs[len(order) :], refs[: len(order)]
        weight_refs, rest = refs[:count], refs[count:]
        source_ref, bias_ref, hidden_ref, slope_ref, held, sems = rest
        panel = weights.panel((*order_refs, *weight_refs), held, sems, pl.program_id(0))
        values = contract(panel[...], source_ref[...], 0, 0) + bias_ref[0]
        hidden, slope = gelu_and_slope(values)
        hidden_ref[0] = hidden.astype(low)
        slope_ref[0] = slope.astype(low)

    return call(
        kernel,
        "project_up",
        (shape.panels,),
        weights.ins() + [(source, None, None), panel_in(bias)],
        [by_panel(shape, inner, low), by_panel(shape, inner, low)],
        weights.scratch(),
        prefetch=order,
    )


def project_down(shape, there, weights, hidden, middle, upstream, table, wide_count):
    order = weights.prefetch
    count = len(weights.arrays)
    bias_at = 6 * shape.seqs
    depth = shape.width // wide_count

    def kernel(at_ref, *refs):
        refs, order_refs = refs[len(order) :], refs[: len(order)]
        weight_refs, rest = refs[:count], refs[count:]
        hidden_ref, middle_ref, upstream_ref, table_ref, out_ref, gate_ref = rest[:6]
        held, sems, total, block_held = rest[6:]
        block = pl.program_id(0)
        total[...] = weighted(weights, (*order_refs, *weight_refs), held, sems, hidden_ref)
        for k in range(wide_count):
            rows = slice(k * depth, (k + 1) * depth)
            table = table_ref[rows]
            mlp = total[rows] + pick(table, bias_at)
            block_held[k] = middle_ref[rows] + mlp * spread(shape, table, 5, block)
            store_sums(
                shape, gate_ref, rows, 0, block, seq_sums(shape, upstream_ref[rows].astype(high) * mlp)
            )
        take_pieces(shape, at_ref, block_held, out_ref)

    return call(
        kernel,
        "project_down",
        (shape.blocks,),
        weights.ins()
        + [panel_blocks(shape, hidden), token_blocks(shape, middle)]
        + [token_blocks(shape, upstream), (table, None, None)],
        [pieces_out(shape), sums_out(shape, 1)],
        weights.scratch(True)
        + [
            *total_scratch(shape),
            pltpu.VMEM((wide_count, depth, shape.block), high),
        ],
        [there, *order],
    )


def grad_outs(shape, columns):
    tall = shape.panels // 2
    half = shape.width // 2
    return [((2, tall, half, columns), low, (2, 1, half, columns), lambda n, *_: (0, n, 0, 0))]


def core_panels(shape, array, core):
    tall = shape.panels // 2
    return (array, (1, *array.shape[1:]), lambda n, *_: (n + core * tall, 0, 0))


def weight_grad(shape, name, source, grad, core):
    columns = grad.shape[1]
    half = shape.width // 2

    def kernel(source_ref, grad_ref, out_ref):
        product = contract(source_ref[...], grad_ref[0], 1, 1).astype(low)
        out_ref[...] = product.reshape(2, 1, half, columns)

    return call(
        kernel,
        name,
        (shape.panels // 2,),
        [(source, None, None), core_panels(shape, grad, core)],
        grad_outs(shape, columns),
    )[0]


def device_weight_grad(shape, name, source, grad, order, wide_count):
    columns = grad.shape[1]
    rows = shape.width // wide_count

    def kernel(order_ref, source_ref, grad_ref, out_ref):
        product = contract(source_ref[...], grad_ref[0], 1, 1).astype(low)
        panel = pl.program_id(0)
        for block in range(wide_count):
            device = order_ref[panel * wide_count + block]
            out_ref[0, device // shape.panels] = product[block * rows : (block + 1) * rows]

    out = call(
        kernel,
        name,
        (shape.panels,),
        [(source, None, None), panel_in(grad)],
        [
            (
                (shape.panels, wide_count, rows, columns),
                low,
                (1, wide_count, rows, columns),
                lambda n, order_ref: (order_ref[n * wide_count] % shape.panels, 0, 0, 0),
            )
        ],
        prefetch=[order],
    )[0]
    return out.reshape(shape.panels * wide_count, rows, columns)


def first_weight_grad(shape, source, grad_qkv, grad_branch, attended, core):
    columns = 4 * shape.local
    begin = shape.out_from
    half = shape.width // 2

    def kernel(source_ref, qkv_ref, branch_ref, attended_ref, out_ref, held):
        held[:, : shape.qkv_rows] = contract(source_ref[...], qkv_ref[0], 1, 1)
        late = contract(branch_ref[...], attended_ref[0], 1, 1)
        both_there = shape.qkv_rows - begin
        if both_there:
            held[:, begin : shape.qkv_rows] += late[:, :both_there]
        held[:, shape.qkv_rows :] = late[:, both_there:]
        out_ref[...] = held[...].astype(low).reshape(2, 1, half, columns)

    return call(
        kernel,
        "first_weight_grad",
        (shape.panels // 2,),
        [
            (source, None, None),
            core_panels(shape, grad_qkv, core),
            (grad_branch, None, None),
            core_panels(shape, attended, core),
        ],
        grad_outs(shape, columns),
        [pltpu.VMEM((shape.width, columns), high)],
    )[0]


def hidden_backward(shape, weights, grad_mlp, slope):
    order = weights.prefetch
    count = len(weights.arrays)
    inner = weights.stop

    def kernel(*refs):
        refs, order_refs = refs[len(order) :], refs[: len(order)]
        weight_refs, rest = refs[:count], refs[count:]
        grad_ref, slope_ref, out_ref, bias_ref, held, sems = rest
        panel = weights.panel((*order_refs, *weight_refs), held, sems, pl.program_id(0))
        values = contract(panel[...], grad_ref[...], 0, 0) * slope_ref[0].astype(high)
        values = values.astype(low)
        out_ref[0] = values
        bias_ref[0] = jnp.sum(values.astype(high), axis=1, keepdims=True)

    return call(
        kernel,
        "hidden_backward",
        (shape.panels,),
        weights.ins() + [(grad_mlp, None, None), panel_in(slope)],
        [
            by_panel(shape, inner, low),
            ((shape.panels, inner, 1), high, (1, inner, 1), lambda n, *_: (n, 0, 0)),
        ],
        weights.scratch(),
        prefetch=order,
    )


def middle_backward(shape, weights, grad_up, middle, upstream, branch, table):
    order = weights.prefetch
    count = len(weights.arrays)

    def kernel(*refs):
        refs, order_refs = refs[len(order) :], refs[: len(order)]
        weight_refs, rest = refs[:count], refs[count:]
        grad_ref, middle_ref, upstream_ref, branch_ref, table_ref = rest[:5]
        out_ref, low_ref, sums_ref, held, sems, total = rest[5:]
        block = pl.program_id(0)
        total[...] = weighted(weights, (*order_refs, *weight_refs), held, sems, grad_ref)
        third = norm_grads(
            shape, total, middle_ref, table_ref, 4, block, sums_ref, 1
        )
        for rows in row_chunks(shape):
            grad = upstream_ref[rows].astype(high) + third(rows)
            store_sums(
                shape, sums_ref, rows, 0, block, seq_sums(shape, grad * branch_ref[rows].astype(high))
            )
            out_ref[rows] = grad
            low_ref[rows] = (grad * spread(shape, table_ref[rows], 2, block)).astype(low)

    return call(
        kernel,
        "middle_backward",
        (shape.blocks,),
        weights.ins()
        + [panel_blocks(shape, grad_up)]
        + [token_blocks(shape, v) for v in (middle, upstream, branch)]
        + [(table, None, None)],
        [token_out(shape, high), token_out(shape, low), sums_out(shape, 3)],
        weights.scratch(True) + total_scratch(shape),
        prefetch=order,
    )


def attended_backward(shape, weights, grad_branch):
    order = weights.prefetch
    count = len(weights.arrays)

    def kernel(*refs):
        refs, order_refs = refs[len(order) :], refs[: len(order)]
        weight_refs, (grad_ref, out_ref, held, sems) = refs[:count], refs[count:]
        panel = weights.panel((*order_refs, *weight_refs), held, sems, pl.program_id(0))
        out_ref[0] = contract(panel[...], grad_ref[...], 0, 0).astype(low)

    return call(
        kernel,
        "attended_backward",
        (shape.panels,),
        weights.ins() + [(grad_branch, None, None)],
        [by_panel(shape, shape.out_rows, low)],
        weights.scratch(),
        prefetch=order,
    )[0]


def input_backward(shape, there, weights, grad_qkv, residual, grad_middle, table, wide_count):
    order = weights.prefetch
    count = len(weights.arrays)
    depth = shape.width // wide_count

    def kernel(at_ref, *refs):
        refs, order_refs = refs[len(order) :], refs[: len(order)]
        weight_refs, rest = refs[:count], refs[count:]
        qkv_ref, residual_ref, middle_ref, table_ref, out_ref, sums_ref = rest[:6]
        held, sems, total, block_held = rest[6:]
        block = pl.program_id(0)
        total[...] = weighted(weights, (*order_refs, *weight_refs), held, sems, qkv_ref)
        third = norm_grads(shape, total, residual_ref, table_ref, 1, block, sums_ref, 0)
        for k in range(wide_count):
            rows = slice(k * depth, (k + 1) * depth)
            block_held[k] = middle_ref[rows] + third(rows)
        take_pieces(shape, at_ref, block_held, out_ref)

    return call(
        kernel,
        "input_backward",
        (shape.blocks,),
        weights.ins()
        + [panel_blocks(shape, grad_qkv)]
        + [token_blocks(shape, v) for v in (residual, grad_middle)]
        + [(table, None, None)],
        [pieces_out(shape), sums_out(shape, 2)],
        weights.scratch(True)
        + [
            *total_scratch(shape),
            pltpu.VMEM((wide_count, depth, shape.block), high),
        ],
        [there, *order],
    )


def on_device(
    tokens,
    ada_weight,
    ada_bias,
    class_table,
    query_weight,
    key_weight,
    value_weight,
    out_weight,
    up_weight,
    up_bias,
    down_weight,
    down_bias,
    cotangent,
    clip_frames,
    time_ids,
    class_ids,
):
    micro_count, seq_count, local_width, seq_tokens = tokens.shape
    class_count, full_width = class_table.shape
    panels, wide_count = lax.axis_size("narrow"), lax.axis_size("wide")
    wide_at = lax.axis_index("wide")
    seqs = micro_count * seq_count
    shape = Shape(seqs, seq_tokens // panels, full_width, panels)
    own_rows = ada_weight.shape[0]
    deep = wide_count // 2
    highest = lax.Precision.HIGHEST
    local_shape = (seqs, local_width, seq_tokens)
    there, came, goes = orders()

    class_hot = (class_ids.reshape(seqs)[:, None] == jnp.arange(class_count)[None, :]).astype(low)
    condition = time_embedding(time_ids.reshape(seqs), full_width) + jnp.einsum(
        "sc,cd->sd", class_hot, class_table, preferred_element_type=high
    )
    sigmoid_cond = jax.nn.sigmoid(condition)
    cond_act = (condition * sigmoid_cond).astype(low)
    silu_slope = sigmoid_cond * (1.0 + condition * (1.0 - sigmoid_cond))
    own_cond = lax.dynamic_slice_in_dim(cond_act, wide_at * own_rows, own_rows, axis=1)
    own_slope = lax.dynamic_slice_in_dim(silu_slope, wide_at * own_rows, own_rows, axis=1)

    first_piece = jnp.concatenate([query_weight, key_weight, value_weight, out_weight.T], axis=1)
    first, up = Gather(first_piece), Gather(up_weight)
    order = device_order()
    mod_part = jnp.einsum("sd,dje->jse", own_cond, ada_weight, preferred_element_type=high)
    mod_part = mod_part.reshape(6 * seqs, local_width)
    hops = [{"side_by": 1}]
    while 2 ** len(hops) <= deep:
        hops.append({"deep_by": 2 ** (len(hops) - 1)})

    first.step()
    token_swap = NarrowSwap(tokens.reshape(local_shape))
    token_same = token_swap.step(0)
    mod_part = mod_part + send(mod_part, **hops[0])
    first.ring, token_same, mod_part, token_swap.parts = sync(
        first.ring, token_same, mod_part, token_swap.parts
    )

    first.step()
    token_other = token_swap.step(1)
    mod_part = mod_part + send(mod_part, **hops[1])
    first.ring, token_other, mod_part = sync(first.ring, token_other, mod_part)

    for at in range(2, max(deep - 1, len(hops))):
        if at < len(hops):
            mod_part = mod_part + send(mod_part, **hops[at])
        if at < deep - 1:
            first.step()
        if at == 2:
            token_near, token_far = token_swap.pieces(token_same, token_other)
        if at == max(deep - 1, len(hops)) - 1:
            first.front_side()
            first.front, first.front_got = sync(first.front, first.front_got)
        first.ring, mod_part = sync(first.ring, mod_part)

    first.rear_tall()
    up.step()
    mod_own = (
        mod_part.reshape(6, seqs, local_width) + ada_bias.astype(high)[:, None, :]
    ).reshape(6 * seqs, local_width)
    small = gather_narrow(
        jnp.concatenate(
            [
                mod_own,
                down_bias.astype(high)[None, :],
                up_bias.astype(high).reshape(-1, local_width),
            ]
        )
    )
    first.rear, first.rear_got, first.front, first.front_got, token_far, small, up.ring = sync(
        first.rear, first.rear_got, first.front, first.front_got, token_far, small, up.ring
    )

    first.second()
    first.core(0, 2)
    for _ in range(2, deep):
        up.step()
    table, up_bias_full = lay_small(shape, came, small, wide_count)
    token_parts = token_near + [token_far[k : k + 1] for k in range(panels // 2)]
    frame_at = jnp.arange(shape.part) % FRAMES
    in_clip = (frame_at[None, :] < clip_frames.reshape(seqs)[:, None]).astype(jnp.int32).reshape(-1)
    residual, input_one = prepare_tokens(shape, came, token_parts, table, wide_count)
    upstream_cut = cut_tokens(shape, after(cotangent.reshape(local_shape), input_one))
    first.arrays, input_one, up.ring, upstream_cut = sync(
        first.arrays, input_one, up.ring, upstream_cut
    )

    first.core(*[k for k in range(len(first.arrays)) if k not in (0, 2)])
    qkv_weights = Weights(first.result(), 0, shape.qkv_rows)
    out_weights = Weights(first.result(), shape.out_from)
    up.front_side()
    up.rear_tall()
    qkv = project_qkv(shape, qkv_weights, input_one)
    qkv, up.front, up.front_got, up.rear, up.rear_got = sync(
        qkv, up.front, up.front_got, up.rear, up.rear_got
    )

    up.second()
    up.core(0, 2)
    down_full = lax.all_gather(after(down_weight.T, qkv), both, axis=0, tiled=False)
    attended, probs = attention_forward(shape, qkv, in_clip)
    attended, up.arrays = sync(attended, up.arrays)

    up.core(*[k for k in range(len(up.arrays)) if k not in (0, 2)])
    upstream_parts = swap_narrow(upstream_cut)
    middle, branch, input_two = project_out(shape, out_weights, attended, residual, table)
    middle, input_two, up.cores = sync(middle, input_two, up.cores)

    up_all = Weights(up.result())
    hidden, slope = project_up(shape, up_all, input_two, up_bias_full)
    hidden, slope, upstream_parts = sync(hidden, slope, upstream_parts)

    upstream, grad_mlp, down_bias_part = prepare_upstream(
        shape, there, upstream_parts, table, wide_count
    )
    down_grads = device_weight_grad(
        shape, "down_weight_grad", grad_mlp, hidden, order, wide_count
    )
    down_grad = lax.psum_scatter(
        down_grads, ("narrow", "wide"), scatter_dimension=0, tiled=False
    ).astype(high)
    down_all = GatheredWeights(down_full, order, panels)
    output_parts, gate_two_part = project_down(
        shape, there, down_all, after(hidden, down_grads), middle, upstream, table, wide_count
    )
    output_parts, gate_two_part = sync(output_parts, gate_two_part)

    output_got = swap_narrow(output_parts)
    grad_up, up_bias_part = hidden_backward(
        shape, down_all, after(grad_mlp, gate_two_part), slope
    )
    other = weight_grad(shape, "up_weight_grad", input_two, grad_up, 1)
    other, output_got = sync(other, output_got)

    up_sum = GradSum(other)
    near = weight_grad(shape, "up_weight_grad", after(input_two, other), grad_up, 0)
    near, up_sum.got = sync(near, up_sum.got)
    up_sum.near(near)
    half = deep // 2
    up_parts = up_sum.split(half)
    sums = up_parts[0].sums("y")
    up_parts[0].along("y", sums)
    grad_middle, grad_branch, middle_sums = middle_backward(
        shape, up_all, after(grad_up, near, *sums), middle, upstream, branch, table
    )
    *_, grad_branch = sync(*up_parts, grad_branch)

    tall_sums, side_sums = up_parts[1].sums("y"), up_parts[0].sums("x")
    up_parts[1].along("y", tall_sums)
    up_parts[0].along("x", side_sums)
    grad_attended = attended_backward(
        shape, out_weights, after(grad_branch, *tall_sums, *side_sums)
    )
    grad_qkv = attention_backward(shape, qkv, probs, grad_attended)
    *_, grad_qkv = sync(*up_parts, grad_qkv)

    side_sums = up_parts[1].sums("x")
    up_parts[1].along("x", side_sums)
    grad_qkv = after(grad_qkv, *side_sums)
    other = first_weight_grad(shape, input_one, grad_qkv, grad_branch, attended, 1)
    *_, other = sync(*up_parts, other)

    first_sum = GradSum(other)
    up_sums = deep_sums(up_parts)
    along_deep(up_parts, up_sums)
    near = first_weight_grad(
        shape, after(input_one, other, *up_sums), grad_qkv, grad_branch, attended, 0
    )
    near, first_sum.got = sync(near, first_sum.got)
    first_sum.near(near)
    first_parts = first_sum.split(half)
    side_sums, tall_sums = first_parts[0].sums("x"), first_parts[1].sums("y")
    first_parts[0].along("x", side_sums)
    first_parts[1].along("y", tall_sums)
    input_parts, input_sums = input_backward(
        shape,
        there,
        qkv_weights,
        after(grad_qkv, *side_sums, *tall_sums),
        residual,
        grad_middle,
        table,
        wide_count,
    )
    *_, input_parts, input_sums = sync(*first_parts, up_parts[0], input_parts, input_sums)
    input_got = swap_narrow(input_parts)

    tall_sums, side_sums = first_parts[0].sums("y"), first_parts[1].sums("x")
    first_parts[0].along("y", tall_sums)
    first_parts[1].along("x", side_sums)
    small_grad = lay_small_grads(
        shape,
        goes,
        input_sums,
        middle_sums,
        after(gate_two_part, *side_sums, *tall_sums),
        down_bias_part,
        up_bias_part,
        wide_count,
    )
    small_grad = small_grad.reshape(2, panels // 2, *small_grad.shape[1:])
    small_grad = small_grad[0] + send(small_grad[1], core_by=1)
    by = 1
    while by < deep:
        small_grad = small_grad + send(small_grad, deep_by=by)
        by *= 2
    *_, small_grad = sync(*first_parts, small_grad)
    sums = deep_sums(first_parts)
    first_got = along_deep(first_parts, sums)
    output = join_tokens(shape, after(output_got, small_grad), low)
    small_grad = small_grad + send(small_grad, side_by=1)
    small_grad = after(small_grad, output, input_got)
    small_grad = sum(
        [small_grad[0]] + [send(small_grad[k], tall_by=k) for k in range(1, panels // 2)]
    )
    own_mod = small_grad[: 6 * seqs].reshape(6, seqs, local_width)
    down_bias_grad = small_grad[6 * seqs]
    up_bias_grad = small_grad[6 * seqs + 1 :].reshape(-1)
    ada_grad = jnp.einsum("sd,jse->dje", own_cond.astype(high), own_mod, precision=highest)
    ada_bias_grad = jnp.sum(own_mod, axis=1)
    input_grad = join_tokens(shape, after(input_got, own_mod), high)
    own_mod = after(own_mod, *first_got[:1], input_grad)
    cond_local = sum_narrow(
        own_slope * jnp.einsum("jse,dje->sd", own_mod, ada_weight.astype(high), precision=highest)
    )
    cond_local = after(cond_local, *first_got)
    cond_grad = sum_wide(
        lax.dynamic_update_slice_in_dim(
            jnp.zeros((seqs, full_width), high), cond_local, wide_at * own_rows, axis=1
        )
    )
    up_grad = up_parts[0].total()
    first_grad = first_parts[0].total()
    table_grad = jnp.einsum("sc,sd->cd", class_hot.astype(high), cond_grad, precision=highest)
    return (
        output.reshape(tokens.shape),
        input_grad.reshape(tokens.shape),
        ada_grad,
        ada_bias_grad,
        table_grad,
        first_grad[:, :local_width],
        first_grad[:, local_width : 2 * local_width],
        first_grad[:, 2 * local_width : 3 * local_width],
        first_grad[:, 3 * local_width :].T,
        up_grad,
        up_bias_grad,
        down_grad.T,
        down_bias_grad,
    )


def solution(mesh):
    return jax.shard_map(
        on_device,
        mesh=mesh,
        in_specs=(
            P(None, None, "narrow", "wide"),
            P("wide", None, "narrow"),
            P(None, "narrow"),
            P(),
            P("wide", "narrow"),
            P("wide", "narrow"),
            P("wide", "narrow"),
            P("narrow", "wide"),
            P("wide", "narrow"),
            P("narrow"),
            P("narrow", "wide"),
            P("narrow"),
            P(None, None, "narrow", "wide"),
            P(),
            P(),
            P(),
        ),
        out_specs=(
            P(None, None, "narrow", "wide"),
            P(None, None, "narrow", "wide"),
            P("wide", None, "narrow"),
            P(None, "narrow"),
            P(),
            P("wide", "narrow"),
            P("wide", "narrow"),
            P("wide", "narrow"),
            P("narrow", "wide"),
            P("wide", "narrow"),
            P("narrow"),
            P("narrow", "wide"),
            P("narrow"),
        ),
        check_vma=False,
    )
```
